128 devices in a mesh: ma: 32 (over z, x, core), col: 4 (over y).
Axes of the slice: x: 4, y: 4, z: 4, core: 2. Of those that a mesh axis runs over, the one named last changes fastest.
Arguments:
- pred_four: bfloat16 [40, 2, 2, 1024, 1024], P('col', None, None, 'ma'), may hold values from -6 to 6
- target_four: bfloat16 [40, 2, 2, 1024, 1024], P('col', None, None, 'ma'), may hold values from -6 to 6
- legendre: bfloat16 [512, 1025, 1024], P(('ma', 'col')), may hold values from -0.1875 to 0.1875
- pair_order: int32 [512], replicated, may hold values from 0 to 511, each once
Outputs:
- grad_four: bfloat16 [40, 2, 2, 1024, 1024], P('col', None, None, 'ma')
The draws below stay inside these ranges and needn't reach their ends.
Inputs may be any that keep to these rules, and one draw needn't show every extreme that they name: Each of 0 to 511 appears once; pair slot p holds the orders pair_order[p] and 1023 - pair_order[p].
All inputs are finite; a program needn't handle non-finite values.
Results may differ from the reference program's by a relative error of at most 0.0015.
The reference program's roundings to bfloat16 on the way count: a program that leaves them out, or rounds other values in their place, can miss the bound.
Values may be sent and summed in bfloat16 or wider, within the bound.
No kernel may reach another device: no remote copies, remote signals or barrier semaphores. Data moves between devices by JAX's collectives and lax.ppermute only.
A program may use at most 192 MiB of HBM per device.

```python
import jax
import jax.numpy as jnp
from jax import lax

DEGREES = 1024
LATITUDES = 1024
CHANNELS = 40
SAMPLES = 2


def block_levels(rng, shape, pieces, smallest, top_value):
    gain = 1.0
    for dim, shards_of in pieces:
        draws = jax.random.uniform(jax.random.fold_in(jax.random.fold_in(rng, 6), dim), (shards_of,), jnp.float32, smallest / len(pieces), top_value / len(pieces))
        gain = gain * jnp.repeat(jnp.exp(draws), shape[dim] // shards_of).reshape((-1,) + (1,) * (len(shape) - 1 - dim))
    return gain


def normal_values(rng, shape, scale, reach, split=(), kind=jnp.bfloat16):
    entries = jax.random.normal(rng, shape, jnp.float32) * scale
    if len(split) > 0:
        entries = block_levels(rng, shape, split, -0.22, 0.18) * entries
    return jnp.clip(entries, min=-reach, max=reach).astype(kind)


def setup_inputs(seed: int = 0) -> dict:
    keys = jax.random.split(jax.random.key(seed), 5)
    pred_four = normal_values(keys[0], (CHANNELS, SAMPLES, 2, LATITUDES, DEGREES), 1.0, 6.0, ((0, 4), (3, 32)))
    target_four = normal_values(keys[1], (CHANNELS, SAMPLES, 2, LATITUDES, DEGREES), 1.0, 6.0, ((0, 4), (3, 32)))
    legendre = normal_values(keys[2], (DEGREES // 2, DEGREES + 1, LATITUDES), LATITUDES ** -0.5, 0.1875, ((0, 128),))
    pair_order = jax.random.permutation(keys[3], DEGREES // 2).astype(jnp.int32)
    return {"pred_four": pred_four, "target_four": target_four, "legendre": legendre, "pair_order": pair_order}


POWER_FLOOR = 0.5

def degree_loss(power_pred, power_true, cross_power):
    pred_floor = jnp.maximum(power_pred, POWER_FLOOR)
    true_floor = jnp.maximum(power_true, POWER_FLOOR)
    root_pred = jnp.sqrt(pred_floor)
    root_true = jnp.sqrt(true_floor)
    upper_mean = (pred_floor * pred_floor + true_floor * true_floor) / (pred_floor + true_floor)
    coherence = cross_power / (root_pred * root_true)
    spread = root_pred - root_true
    return jnp.sum(spread * spread + 2.0 * upper_mean * (1.0 - coherence))

def loss_factors(moments):
    dpower, dcross = jax.grad(degree_loss, argnums=(0, 2))(moments[:, 0], moments[:, 1], moments[:, 2])
    return jnp.stack([2.0 * dpower, dcross], axis=1)

def coeff_moments(coeffs, group_count):
    shaped = coeffs.reshape(coeffs.shape[:-1] + (2, group_count, 2))
    predicted = shaped[..., 0, :, :]
    observed = shaped[..., 1, :, :]
    return jnp.stack([lax.optimization_barrier(jnp.sum(predicted * predicted, -1)), lax.optimization_barrier(jnp.sum(observed * observed, -1)), lax.optimization_barrier(jnp.sum(predicted * observed, -1))], axis=-2)

def place_degrees(values, lower_order):
    upper_order = DEGREES - 1 - lower_order
    tail = values.shape[1:]
    padded = jnp.concatenate([jnp.zeros((DEGREES,) + tail, jnp.float32), values[:DEGREES]], axis=0)
    lower_part = lax.dynamic_slice_in_dim(padded, (DEGREES - lower_order).astype(jnp.int32), DEGREES, 0)
    degree_index = jnp.arange(DEGREES, dtype=jnp.int32)
    upper_mask = (degree_index >= upper_order).reshape((DEGREES,) + (1,) * len(tail))
    upper_part = jnp.where(upper_mask, values[1:], jnp.zeros_like(values[1:]))
    lower_weight = jnp.where(lower_order == 0, 1.0, 2.0)
    return lower_weight * lower_part + 2.0 * upper_part

def spread_factors(factors, lower_order):
    tail = factors.shape[1:]
    padded = jnp.concatenate([factors, jnp.zeros((DEGREES + 1,) + tail, jnp.float32)], axis=0)
    lower_part = lax.dynamic_slice_in_dim(padded, lower_order.astype(jnp.int32), DEGREES + 1, 0)
    upper_part = jnp.concatenate([jnp.zeros((1,) + tail, jnp.float32), factors], axis=0)
    row_index = jnp.arange(DEGREES + 1, dtype=jnp.int32)
    lower_rows = (row_index < DEGREES - lower_order).reshape((DEGREES + 1,) + (1,) * len(tail))
    lower_weight = jnp.where(lower_order == 0, 1.0, 2.0)
    return jnp.where(lower_rows, lower_weight * lower_part, 2.0 * upper_part)

def grad_from(coeffs, row_factors, group_count):
    shaped = coeffs.reshape(coeffs.shape[:-1] + (2, group_count, 2))
    predicted = shaped[..., 0, :, :]
    observed = shaped[..., 1, :, :]
    combined = row_factors[..., 0, :, None] * predicted + row_factors[..., 1, :, None] * observed
    combined = combined.astype(jnp.bfloat16)
    return combined.reshape(combined.shape[:-2] + (2 * group_count,))

def pair_coeffs(legendre_rows, fields, lower_order):
    upper_order = DEGREES - 1 - lower_order
    lower_fields = lax.dynamic_index_in_dim(fields, lower_order.astype(jnp.int32), axis=2, keepdims=False)
    upper_fields = lax.dynamic_index_in_dim(fields, upper_order.astype(jnp.int32), axis=2, keepdims=False)
    lower_coeffs = jnp.dot(legendre_rows, lower_fields.T, preferred_element_type=jnp.float32)
    upper_coeffs = jnp.dot(legendre_rows, upper_fields.T, preferred_element_type=jnp.float32)
    row_index = jnp.arange(DEGREES + 1, dtype=jnp.int32)
    return jnp.where((row_index < DEGREES - lower_order)[:, None], lower_coeffs, upper_coeffs)

def reference(pred_four, target_four, legendre, pair_order):
    group_count = CHANNELS * SAMPLES
    fields = jnp.stack([pred_four, target_four]).reshape(4 * group_count, LATITUDES, DEGREES)

    def first_pass(totals, inputs):
        legendre_rows, lower_order = inputs
        coeffs = pair_coeffs(legendre_rows, fields, lower_order)
        return (totals + place_degrees(coeff_moments(coeffs, group_count), lower_order), None)
    initial = jnp.zeros((DEGREES, 3, group_count), jnp.float32)
    moments, _ = lax.scan(first_pass, initial, (legendre, pair_order))
    factors = loss_factors(moments)

    def second_pass(inputs):
        legendre_rows, lower_order = inputs
        coeffs = pair_coeffs(legendre_rows, fields, lower_order)
        grad_rows = grad_from(coeffs, spread_factors(factors, lower_order), group_count)
        row_index = jnp.arange(DEGREES + 1, dtype=jnp.int32)
        lower_rows = (row_index < DEGREES - lower_order)[:, None]
        blank = jnp.zeros_like(grad_rows)
        lower_out = jnp.dot(jnp.where(lower_rows, grad_rows, blank).T, legendre_rows, preferred_element_type=jnp.float32)
        upper_out = jnp.dot(jnp.where(lower_rows, blank, grad_rows).T, legendre_rows, preferred_element_type=jnp.float32)
        return jnp.stack([lower_out, upper_out]).astype(jnp.bfloat16)
    outputs = lax.map(second_pass, (legendre, pair_order))
    half_count = DEGREES // 2
    inverse = jnp.zeros((half_count,), jnp.int32).at[pair_order].set(jnp.arange(half_count, dtype=jnp.int32))
    pair_of = jnp.concatenate([inverse, inverse[::-1]])
    side_of = jnp.concatenate([jnp.zeros((half_count,), jnp.int32), jnp.ones((half_count,), jnp.int32)])
    by_order = outputs[pair_of, side_of]
    return jnp.transpose(by_order, (1, 2, 0)).reshape(CHANNELS, SAMPLES, 2, LATITUDES, DEGREES)
```

```python
import functools

import jax
import jax.numpy as jnp
from jax import lax
from jax.experimental import pallas as pl
from jax.experimental.pallas import tpu as pltpu
from jax.sharding import PartitionSpec as P

DEGREES = 1024
HALF = DEGREES // 2
POWER_FLOOR = 0.5
LANES = 128
SLOTS = 8
AXES = ("ma", "col")
PARTS = (10,)
VMEM_LIMIT = 56 * 1024 * 1024


def round_up(value, multiple):
    return -(-value // multiple) * multiple


def dot_nt(left, right):
    return lax.dot_general(left, right, (((1,), (1,)), ((), ())), preferred_element_type=jnp.float32)


def dot_nn(left, right):
    return lax.dot_general(left, right, (((1,), (0,)), ((), ())), preferred_element_type=jnp.float32)


def swap_groups(blocks):
    lane = lax.broadcasted_iota(jnp.int32, blocks[0].shape, 1)
    low_half = lane < 64
    even = (lane & 32) == 0
    first = [None] * 4
    for i in (0, 1):
        upper, lower = blocks[i], blocks[i + 2]
        first[i] = jnp.where(low_half, upper, pltpu.roll(lower, 64, 1))
        first[i + 2] = jnp.where(low_half, pltpu.roll(upper, 64, 1), lower)
    result = []
    for i in (0, 2):
        upper, lower = first[i], first[i + 1]
        result.append(jnp.where(even, upper, pltpu.roll(lower, 32, 1)))
        result.append(jnp.where(even, pltpu.roll(upper, 96, 1), lower))
    return result


def pack_kernel(perm_ref, pred_ref, target_ref, out_ref):
    for f, field_ref in enumerate((pred_ref, target_ref)):
        field = field_ref[...].reshape(2 * LANES, DEGREES)
        by_slot = dot_nt(perm_ref[...], field)
        both = [
            by_slot[:, c * LANES : (c + 1) * LANES].reshape(DEGREES // SLOTS, SLOTS, LANES)
            for c in range(2)
        ]
        out_ref[:, f, 0] = jnp.concatenate(both, axis=1).astype(jnp.bfloat16)


def pack(perm, pred, target, first, count):
    devices = DEGREES // SLOTS
    field_spec = pl.BlockSpec((2, 2, 2, 32, DEGREES), lambda i: (first // 2 + i, 0, 0, 0, 0))
    return pl.pallas_call(
        pack_kernel,
        grid=(count // 2,),
        in_specs=[pl.BlockSpec((DEGREES, DEGREES), lambda i: (0, 0)), field_spec, field_spec],
        out_specs=pl.BlockSpec((devices, 2, 1, 16, LANES), lambda i: (0, 0, i, 0, 0)),
        out_shape=jax.ShapeDtypeStruct((devices, 2, count // 2, 16, LANES), jnp.bfloat16),
        compiler_params=pltpu.CompilerParams(vmem_limit_bytes=VMEM_LIMIT),
        cost_estimate=pl.CostEstimate(
            flops=2 * DEGREES * DEGREES * 2 * LANES * count,
            bytes_accessed=2 * DEGREES * DEGREES + 8 * LANES * DEGREES * count,
            transcendentals=0,
        ),
        name="pack",
    )(perm, pred, target)


def moments_of(values, rows):
    width = values.shape[-1]
    shaped = values.reshape(4, 2, rows, width)
    pieces = []
    for left, right in ((0, 0), (1, 1), (0, 1)):
        for s in range(2):
            real = shaped[2 * s, left] * shaped[2 * s, right]
            imag = shaped[2 * s + 1, left] * shaped[2 * s + 1, right]
            pieces.append(real + imag)
    return jnp.concatenate(pieces, axis=0)


def analysis_kernel(
    count, order_ref, arrived_ref, leg_ref, coef_ref, last_ref, moment_ref,
    wide_ref, field_ref, raw_ref, total_ref,
):
    p = pl.program_id(0)
    rows = 4 * count

    @pl.when(p == 0)
    def _():
        def widen(j, carry):
            for f in range(2):
                block = arrived_ref[j, :, f].reshape(rows * SLOTS, LANES)
                wide_ref[f, j] = block.astype(jnp.float32)
            return carry

        lax.fori_loop(0, 32, widen, 0)
        total_ref[...] = jnp.zeros_like(total_ref)

    for t in range(2):
        slot = 2 * p + t
        for tile in range(8):
            blocks = []
            for i in range(4):
                fields = [
                    wide_ref[f, 4 * tile + i, pl.ds(slot, rows, stride=SLOTS), :] for f in range(2)
                ]
                blocks.append(jnp.concatenate(fields, axis=0))
            for g, block in enumerate(swap_groups(blocks)):
                field_ref[t, g * 2 * rows : (g + 1) * 2 * rows, tile * LANES : (tile + 1) * LANES] = (
                    block.astype(jnp.bfloat16)
                )

    lower_order = order_ref[p]
    boundary = DEGREES - lower_order
    width = 256
    for tile in range(DEGREES // width):
        start = tile * width
        leg = leg_ref[0, start : start + width, :]
        values = dot_nt(field_ref[0], leg)
        if start >= HALF:
            upper = dot_nt(field_ref[1], leg)
            row = lax.broadcasted_iota(jnp.int32, values.shape, 1) + start
            values = jnp.where(row < boundary, values, upper)
        coef_ref[0, :, start : start + width] = values
        raw_ref[:, start : start + width] = moments_of(values, rows)
    last_leg = jnp.broadcast_to(leg_ref[0, DEGREES : DEGREES + 1, :].astype(jnp.float32), (LANES, DEGREES))
    last = dot_nt(field_ref[1], last_leg.astype(jnp.bfloat16))
    last_ref[0] = last
    last_moments = moments_of(last, rows)

    lower_weight = jnp.where(lower_order == 0, 1.0, 2.0)
    step = 2 * rows
    for k in range(3):
        raw = raw_ref[k * step : (k + 1) * step, :]
        tail = last_moments[k * step : (k + 1) * step]
        degree = lax.broadcasted_iota(jnp.int32, raw.shape, 1)
        lower = jnp.where(degree >= lower_order, pltpu.roll(raw, lower_order, 1), 0.0)
        upper = pltpu.roll(raw, DEGREES - 1, 1)
        upper = jnp.where(degree == DEGREES - 1, jnp.concatenate([tail] * 8, axis=1), upper)
        upper = jnp.where(degree >= DEGREES - 1 - lower_order, upper, 0.0)
        total_ref[k * step : (k + 1) * step, :] += lower_weight * lower + 2.0 * upper

    @pl.when(p == pl.num_programs(0) - 1)
    def _():
        moment_ref[...] = total_ref[...].T


def analysis(lower_order, arrived, legendre, count):
    pairs, leg_rows, _ = legendre.shape
    rows = 32 * count
    lanes = round_up(24 * count, LANES)
    grid_spec = pltpu.PrefetchScalarGridSpec(
        num_scalar_prefetch=1,
        grid=(pairs,),
        in_specs=[
            pl.BlockSpec((32, 4, 2, count * SLOTS, LANES), lambda p, o: (0, 0, 0, 0, 0)),
            pl.BlockSpec((1, leg_rows, DEGREES), lambda p, o: (p, 0, 0)),
        ],
        out_specs=[
            pl.BlockSpec((1, rows, DEGREES), lambda p, o: (p, 0, 0)),
            pl.BlockSpec((1, rows, LANES), lambda p, o: (p, 0, 0)),
            pl.BlockSpec((DEGREES, lanes), lambda p, o: (0, 0)),
        ],
        scratch_shapes=[
            pltpu.VMEM((2, 32, rows, LANES), jnp.float32),
            pltpu.VMEM((2, rows, DEGREES), jnp.bfloat16),
            pltpu.VMEM((24 * count, DEGREES), jnp.float32),
            pltpu.VMEM((lanes, DEGREES), jnp.float32),
        ],
    )
    return pl.pallas_call(
        functools.partial(analysis_kernel, count),
        grid_spec=grid_spec,
        out_shape=[
            jax.ShapeDtypeStruct((pairs, rows, DEGREES), jnp.float32),
            jax.ShapeDtypeStruct((pairs, rows, LANES), jnp.float32),
            jax.ShapeDtypeStruct((DEGREES, lanes), jnp.float32),
        ],
        compiler_params=pltpu.CompilerParams(vmem_limit_bytes=VMEM_LIMIT),
        cost_estimate=pl.CostEstimate(
            flops=3 * pairs * rows * DEGREES * DEGREES,
            bytes_accessed=2 * legendre.size + 4 * pairs * rows * DEGREES + 2 * arrived.size,
            transcendentals=0,
        ),
        name="analysis",
    )(lower_order, arrived.reshape(32, 4, 2, count * SLOTS, LANES), legendre)


def factor_kernel(count, parts_ref, out_ref):
    total = jnp.sum(parts_ref[...], axis=0)
    size = total.shape[1]
    span = 8 * count
    power_pred = total
    power_true = pltpu.roll(total, size - span, 1)
    cross = pltpu.roll(total, size - 2 * span, 1)
    pred = jnp.maximum(power_pred, POWER_FLOOR)
    true = jnp.maximum(power_true, POWER_FLOOR)
    root_pred = jnp.sqrt(pred)
    root_true = jnp.sqrt(true)
    both = pred + true
    upper_mean = (pred * pred + true * true) / both
    inverse = 1.0 / (root_pred * root_true)
    coherence = cross * inverse
    mean_slope = (2.0 * pred - upper_mean) / both
    slope = (
        (root_pred - root_true) / root_pred
        + 2.0 * mean_slope * (1.0 - coherence)
        + upper_mean * coherence / pred
    )
    binds = jnp.where(power_pred > POWER_FLOOR, 1.0, jnp.where(power_pred == POWER_FLOOR, 0.5, 0.0))
    dpower = 2.0 * slope * binds
    dcross = -2.0 * upper_mean * inverse
    lane = lax.broadcasted_iota(jnp.int32, total.shape, 1)
    factors = jnp.where(lane < span, dpower, pltpu.roll(dcross, span, 1))[:, : out_ref.shape[-1]]
    out_ref[...] = jnp.broadcast_to(factors[None], out_ref.shape)


def factors_of(parts, count):
    lanes = round_up(16 * count, LANES)
    return pl.pallas_call(
        functools.partial(factor_kernel, count),
        out_shape=jax.ShapeDtypeStruct(parts.shape[:2] + (lanes,), jnp.float32),
        compiler_params=pltpu.CompilerParams(vmem_limit_bytes=VMEM_LIMIT),
        cost_estimate=pl.CostEstimate(flops=parts.size, bytes_accessed=8 * parts.size, transcendentals=0),
        name="factors",
    )(parts)


def synthesis_kernel(
    count, order_ref, coef_ref, last_ref, factor_ref, leg_ref, out_ref,
    spread_ref, lower_ref, upper_ref, wide_ref,
):
    p = pl.program_id(0)
    rows = 4 * count

    @pl.when(p == 0)
    def _():
        spread_ref[...] = factor_ref[...].T

    lower_order = order_ref[p]
    boundary = DEGREES - lower_order
    lower_weight = jnp.where(lower_order == 0, 1.0, 2.0)
    back = lax.rem(DEGREES - lower_order, DEGREES)
    last_grads = []
    for s in range(2):
        row_factors, last_factors = [], []
        for k in range(2):
            at = (2 * k + s) * rows
            factor = spread_ref[at : at + rows, :]
            row = lax.broadcasted_iota(jnp.int32, factor.shape, 1)
            shifted = lower_weight * pltpu.roll(factor, back, 1)
            row_factors.append(jnp.where(row < boundary, shifted, 2.0 * pltpu.roll(factor, 1, 1)))
            last_factors.append(jnp.broadcast_to(2.0 * factor[:, DEGREES - 1 :], (rows, LANES)))
        for q in range(2):
            g = 2 * s + q
            at = 2 * g * rows
            predicted = coef_ref[0, at : at + rows, :]
            observed = coef_ref[0, at + rows : at + 2 * rows, :]
            grad = row_factors[0] * predicted + row_factors[1] * observed
            row = lax.broadcasted_iota(jnp.int32, grad.shape, 1)
            lower_ref[g * rows : (g + 1) * rows, :] = jnp.where(row < boundary, grad, 0.0)
            upper_ref[g * rows : (g + 1) * rows, :] = jnp.where(row < boundary, 0.0, grad)[:, HALF:]
            predicted = last_ref[0, at : at + rows, :]
            observed = last_ref[0, at + rows : at + 2 * rows, :]
            last_grad = last_factors[0] * predicted + last_factors[1] * observed
            last_grads.append(last_grad.astype(jnp.bfloat16).astype(jnp.float32))
    last_grad = jnp.concatenate(last_grads, axis=0)
    lower_grad = lower_ref[...].astype(jnp.bfloat16)
    upper_grad = upper_ref[...].astype(jnp.bfloat16)
    last_leg = leg_ref[0, DEGREES : DEGREES + 1, :].astype(jnp.float32)

    width = 256
    for tile in range(DEGREES // width):
        start = tile * width
        lower = dot_nn(lower_grad, leg_ref[0, :DEGREES, start : start + width])
        upper = dot_nn(upper_grad, leg_ref[0, HALF:DEGREES, start : start + width])
        for t, values in enumerate((lower, upper)):
            for sub in range(width // LANES):
                at = start + sub * LANES
                piece = values[:, sub * LANES : (sub + 1) * LANES]
                if t == 1:
                    piece = piece + last_grad * last_leg[:, at : at + LANES]
                blocks = [piece[g * rows : (g + 1) * rows] for g in range(4)]
                for i, block in enumerate(swap_groups(blocks)):
                    wide_ref[at // 32 + i, pl.ds(2 * p + t, rows, stride=SLOTS), :] = block

    @pl.when(p == pl.num_programs(0) - 1)
    def _():
        def narrow(j, carry):
            out_ref[j] = wide_ref[j].astype(jnp.bfloat16)
            return carry

        lax.fori_loop(0, 32, narrow, 0)


def synthesis(lower_order, coeffs, last, factors, legendre, count):
    pairs, leg_rows, _ = legendre.shape
    rows = 32 * count
    lanes = factors.shape[1]
    grid_spec = pltpu.PrefetchScalarGridSpec(
        num_scalar_prefetch=1,
        grid=(pairs,),
        in_specs=[
            pl.BlockSpec((1, rows, DEGREES), lambda p, o: (p, 0, 0)),
            pl.BlockSpec((1, rows, LANES), lambda p, o: (p, 0, 0)),
            pl.BlockSpec((DEGREES, lanes), lambda p, o: (0, 0)),
            pl.BlockSpec((1, leg_rows, DEGREES), lambda p, o: (p, 0, 0)),
        ],
        out_specs=pl.BlockSpec((32, rows, LANES), lambda p, o: (0, 0, 0)),
        scratch_shapes=[
            pltpu.VMEM((lanes, DEGREES), jnp.float32),
            pltpu.VMEM((rows // 2, DEGREES), jnp.float32),
            pltpu.VMEM((rows // 2, HALF), jnp.float32),
            pltpu.VMEM((32, rows, LANES), jnp.float32),
        ],
    )
    return pl.pallas_call(
        functools.partial(synthesis_kernel, count),
        grid_spec=grid_spec,
        out_shape=jax.ShapeDtypeStruct((32, rows, LANES), jnp.bfloat16),
        compiler_params=pltpu.CompilerParams(vmem_limit_bytes=VMEM_LIMIT),
        cost_estimate=pl.CostEstimate(
            flops=3 * pairs * rows // 2 * DEGREES * DEGREES,
            bytes_accessed=2 * legendre.size + 4 * pairs * rows * DEGREES + 64 * rows * LANES,
            transcendentals=0,
        ),
        name="synthesis",
    )(lower_order, coeffs, last, factors, legendre)


def unpack_kernel(perm_ref, returned_ref, *refs):
    out_ref = refs[-1]
    both = returned_ref[...].astype(jnp.float32)
    sides = [both[:, c * SLOTS : (c + 1) * SLOTS].reshape(DEGREES, LANES) for c in range(2)]
    by_slot = jnp.concatenate(sides, axis=1)
    field = dot_nn(by_slot.T.astype(jnp.bfloat16), perm_ref[...])
    out_ref[...] = field.astype(jnp.bfloat16).reshape(out_ref.shape)


def unpack(perm, returned, earlier, first, count, channels):
    devices = DEGREES // SLOTS
    block = (2, 2, 2, 32, DEGREES)
    in_specs = [
        pl.BlockSpec((DEGREES, DEGREES), lambda i: (0, 0)),
        pl.BlockSpec((devices, 16, LANES), lambda i: (0, i, 0)),
    ]
    args = [perm, returned]
    aliases = {}
    if earlier is not None:
        in_specs.append(pl.BlockSpec(memory_space=pl.ANY))
        args.append(earlier)
        aliases = {2: 0}
    return pl.pallas_call(
        unpack_kernel,
        grid=(count // 2,),
        in_specs=in_specs,
        out_specs=pl.BlockSpec(block, lambda i: (first // 2 + i, 0, 0, 0, 0)),
        out_shape=jax.ShapeDtypeStruct((channels, 2, 2, 32, DEGREES), jnp.bfloat16),
        input_output_aliases=aliases,
        compiler_params=pltpu.CompilerParams(vmem_limit_bytes=VMEM_LIMIT),
        cost_estimate=pl.CostEstimate(
            flops=2 * DEGREES * DEGREES * LANES * count,
            bytes_accessed=2 * DEGREES * DEGREES + 4 * LANES * DEGREES * count,
            transcendentals=0,
        ),
        name="unpack",
    )(*args)


def exchange(values):
    return lax.all_to_all(values, AXES, split_axis=0, concat_axis=0, tiled=True)


def per_device(pred_four, target_four, legendre, pair_order):
    channels = pred_four.shape[0]
    pairs = legendre.shape[0]
    devices = DEGREES // SLOTS
    slot_orders = jnp.stack([pair_order, DEGREES - 1 - pair_order], axis=1).reshape(DEGREES)
    order_index = jnp.arange(DEGREES, dtype=jnp.int32)
    perm = (slot_orders[:, None] == order_index[None, :]).astype(jnp.bfloat16)
    device = lax.axis_index(AXES)
    lower_order = lax.dynamic_slice_in_dim(pair_order, device * pairs, pairs)
    starts = [sum(PARTS[:i]) for i in range(len(PARTS))]

    arrived = []
    for first, count in zip(starts, PARTS):
        packed = pack(perm, pred_four, target_four, first, count)
        arrived.append(exchange(packed.reshape(devices, 2 * count * SLOTS, LANES)))
    kept, spectra = [], []
    for count, block in zip(PARTS, arrived):
        coeffs, last, moments = analysis(lower_order, block, legendre, count)
        kept.append((coeffs, last))
        spectra.append(exchange(moments.reshape(devices, SLOTS, -1)))
    factors = [
        exchange(factors_of(block, count)).reshape(DEGREES, -1)
        for count, block in zip(PARTS, spectra)
    ]
    returned = []
    for count, (coeffs, last), factor in zip(PARTS, kept, factors):
        going = synthesis(lower_order, coeffs, last, factor, legendre, count)
        returned.append(exchange(going.reshape(devices, count * SLOTS, LANES)))
    result = None
    for first, count, block in zip(starts, PARTS, returned):
        result = unpack(perm, block, result, first, count, channels)
    return result


def solution(mesh):
    placed = (
        P("col", None, None, "ma", None),
        P("col", None, None, "ma", None),
        P(AXES, None, None),
        P(),
    )
    return jax.shard_map(
        per_device,
        mesh=mesh,
        in_specs=placed,
        out_specs=P("col", None, None, "ma", None),
        check_vma=False,
    )
```

```python
import functools

import jax
import jax.numpy as jnp
from jax import lax
from jax.experimental import pallas as pl
from jax.experimental.pallas import tpu as pltpu
from jax.sharding import PartitionSpec as P

DEGREES = 1024
HALF = DEGREES // 2
POWER_FLOOR = 0.5
LANES = 128
SLOTS = 8
AXES = ("ma", "col")
PACK_LIMIT = 24 * 1024 * 1024
KERNEL_LIMIT = 32 * 1024 * 1024


def round_up(value, multiple):
    return -(-value // multiple) * multiple


def dot_nt(left, right):
    return lax.dot_general(left, right, (((1,), (1,)), ((), ())), preferred_element_type=jnp.float32)


def dot_nn(left, right):
    return lax.dot_general(left, right, (((1,), (0,)), ((), ())), preferred_element_type=jnp.float32)


def by_position(blocks, shift):
    group = lax.broadcasted_iota(jnp.int32, blocks[0].shape, 1) >> 5
    result = blocks[-shift % 4]
    for z in range(1, 4):
        result = jnp.where(group == z, blocks[(z - shift) % 4], result)
    return result


def one_hots(pairs_ref, lower_ref, upper_ref):
    row = jnp.broadcast_to(pairs_ref[...], (8, HALF)).astype(jnp.float32)
    order = row.T[:, :1].astype(jnp.int32)
    lane = lax.broadcasted_iota(jnp.int32, (HALF, HALF), 1)
    lower_ref[...] = jnp.where(lane == order, 1.0, 0.0).astype(jnp.bfloat16)
    upper_ref[...] = jnp.where(lane == HALF - 1 - order, 1.0, 0.0).astype(jnp.bfloat16)


def trade_halves(first, second):
    top = lax.broadcasted_iota(jnp.int32, first.shape, 1) < 4
    return (
        jnp.where(top, first, pltpu.roll(second, 4, 1)),
        jnp.where(top, pltpu.roll(first, 4, 1), second),
    )


def pack_kernel(turn_ref, pairs_ref, pred_ref, target_ref, out_ref, lower_ref, upper_ref):
    @pl.when(pl.program_id(0) == 0)
    def _():
        one_hots(pairs_ref, lower_ref, upper_ref)

    turn = turn_ref[0]
    for f, field_ref in enumerate((pred_ref, target_ref)):
        field = jnp.concatenate(
            [field_ref[c, (z - turn) & 3] for c in range(2) for z in range(4)], axis=0
        )
        low = dot_nt(lower_ref[...], field[:, :HALF]).reshape(HALF // 8, 8, 2 * LANES)
        high = dot_nt(upper_ref[...], field[:, HALF:]).reshape(HALF // 8, 8, 2 * LANES)
        both = jnp.stack(trade_halves(low, high), axis=1).reshape(HALF // 4, 8, 2 * LANES)
        both = jnp.concatenate([both[:, :, :LANES], both[:, :, LANES:]], axis=1)
        out_ref[:, f, 0] = both.astype(jnp.bfloat16)


def pack(turn, pairs, pred, target, first, count):
    devices = DEGREES // SLOTS
    field_spec = pl.BlockSpec((2, 4, 32, DEGREES), lambda i, t: (first // 2 + i, 0, 0, 0))
    grid_spec = pltpu.PrefetchScalarGridSpec(
        num_scalar_prefetch=1,
        grid=(count // 2,),
        in_specs=[pl.BlockSpec((1, HALF), lambda i, t: (0, 0)), field_spec, field_spec],
        out_specs=pl.BlockSpec((devices, 2, 1, 16, LANES), lambda i, t: (0, 0, i, 0, 0)),
        scratch_shapes=[pltpu.VMEM((HALF, HALF), jnp.bfloat16)] * 2,
    )
    return pl.pallas_call(
        pack_kernel,
        grid_spec=grid_spec,
        out_shape=jax.ShapeDtypeStruct((devices, 2, count // 2, 16, LANES), jnp.bfloat16),
        compiler_params=pltpu.CompilerParams(vmem_limit_bytes=PACK_LIMIT),
        cost_estimate=pl.CostEstimate(
            flops=DEGREES * DEGREES * 2 * LANES * count,
            bytes_accessed=8 * LANES * DEGREES * count,
            transcendentals=0,
        ),
        name="pack",
    )(turn, pairs, pred, target)


def moments_of(values, rows):
    width = values.shape[-1]
    shaped = values.reshape(4, 2, rows, width)
    pieces = []
    for left, right in ((0, 0), (1, 1), (0, 1)):
        for s in range(2):
            real = shaped[2 * s, left] * shaped[2 * s, right]
            imag = shaped[2 * s + 1, left] * shaped[2 * s + 1, right]
            pieces.append(real + imag)
    return jnp.concatenate(pieces, axis=0)


def analysis_kernel(
    count, order_ref, arrived_ref, leg_ref, coef_ref, last_ref, moment_ref,
    wide_ref, field_ref, raw_ref, lower_ref, upper_ref, tail_ref,
):
    rows = 4 * count
    size = 24 * count

    def widen(j, carry):
        for f in range(2):
            block = arrived_ref[j, :, f].reshape(rows * SLOTS, LANES)
            wide_ref[f, j] = block.astype(jnp.float32)
        return carry

    lax.fori_loop(0, 32, widen, 0)
    lower_ref[...] = jnp.zeros_like(lower_ref)
    upper_ref[...] = jnp.zeros_like(upper_ref)
    tail_ref[...] = jnp.zeros_like(tail_ref)

    def one_pair(p, carry):
        for t in range(2):
            slot = 4 * t + p
            for tile in range(8):
                blocks = []
                for i in range(4):
                    fields = [
                        wide_ref[f, 4 * tile + i, pl.ds(slot, rows, stride=SLOTS), :] for f in range(2)
                    ]
                    blocks.append(jnp.concatenate(fields, axis=0))
                for g in range(4):
                    block = by_position(blocks, g)
                    if g > 0:
                        block = pltpu.roll(block, LANES - 32 * g, 1)
                    field_ref[
                        t, g * 2 * rows : (g + 1) * 2 * rows, tile * LANES : (tile + 1) * LANES
                    ] = block.astype(jnp.bfloat16)

        lower_order = order_ref[p]
        boundary = DEGREES - lower_order
        width = 256
        for tile in range(DEGREES // width):
            start = tile * width
            leg = leg_ref[p, start : start + width, :]
            values = dot_nt(field_ref[0], leg)
            if start >= HALF:
                upper = dot_nt(field_ref[1], leg)
                row = lax.broadcasted_iota(jnp.int32, values.shape, 1) + start
                values = jnp.where(row < boundary, values, upper)
            coef_ref[p, :, start : start + width] = values
            moments = moments_of(values, rows)
            raw_ref[:, start : start + width] = moments
            if start >= HALF:
                row = lax.broadcasted_iota(jnp.int32, moments.shape, 1) + start
                upper_ref[:, start - HALF : start - HALF + width] += jnp.where(
                    row < boundary, 0.0, moments
                )
        last_leg = jnp.broadcast_to(
            leg_ref[p, DEGREES : DEGREES + 1, :].astype(jnp.float32), (LANES, DEGREES)
        )
        last = dot_nt(field_ref[1], last_leg.astype(jnp.bfloat16))
        last_ref[p] = last
        tail_ref[...] += moments_of(last, rows)

        lower_weight = jnp.where(lower_order == 0, 1.0, 2.0)
        tiles_up = lower_order >> 7
        lanes_up = lower_order & (LANES - 1)
        lane = lax.broadcasted_iota(jnp.int32, (size, LANES), 1)
        before = jnp.zeros((size, LANES), jnp.float32)
        for tile in range(8):
            turned = pltpu.roll(raw_ref[:, tile * LANES : (tile + 1) * LANES], lanes_up, 1)
            at = pl.multiple_of((tile + tiles_up) * LANES, LANES)
            lower_ref[:, pl.ds(at, LANES)] += lower_weight * jnp.where(lane < lanes_up, before, turned)
            before = turned
        return carry

    lax.fori_loop(0, 4, one_pair, 0)

    lane = lax.broadcasted_iota(jnp.int32, (size, LANES), 1)
    after = tail_ref[...]
    for tile in reversed(range(8)):
        total = lower_ref[:, tile * LANES : (tile + 1) * LANES]
        if tile >= 4:
            turned = pltpu.roll(upper_ref[:, (tile - 4) * LANES : (tile - 3) * LANES], LANES - 1, 1)
            total = total + 2.0 * jnp.where(lane == LANES - 1, after, turned)
            after = turned
        pad = moment_ref.shape[1] - size
        if pad > 0:
            total = jnp.concatenate([total, jnp.zeros((pad, LANES), jnp.float32)], axis=0)
        moment_ref[tile * LANES : (tile + 1) * LANES, :] = total.T


def in_vmem(*values):
    return [pltpu.with_memory_space_constraint(value, pltpu.VMEM) for value in values]


def analysis(lower_order, arrived, legendre, count):
    pairs = legendre.shape[0]
    rows = 32 * count
    lanes = round_up(24 * count, LANES)
    arrived = arrived.reshape(32, 4, 2, count * SLOTS, LANES)
    whole = pl.BlockSpec(memory_space=pltpu.VMEM)
    return pl.pallas_call(
        functools.partial(analysis_kernel, count),
        in_specs=[pl.BlockSpec(memory_space=pltpu.SMEM), whole, whole],
        out_specs=[whole, whole, whole],
        out_shape=[
            pltpu.VMEM((pairs, rows, DEGREES), jnp.float32),
            pltpu.VMEM((pairs, rows, LANES), jnp.float32),
            pltpu.VMEM((DEGREES, lanes), jnp.float32),
        ],
        scratch_shapes=[
            pltpu.VMEM((2, 32, rows, LANES), jnp.float32),
            pltpu.VMEM((2, rows, DEGREES), jnp.bfloat16),
            pltpu.VMEM((24 * count, DEGREES), jnp.float32),
            pltpu.VMEM((24 * count, DEGREES + HALF), jnp.float32),
            pltpu.VMEM((24 * count, HALF), jnp.float32),
            pltpu.VMEM((24 * count, LANES), jnp.float32),
        ],
        compiler_params=pltpu.CompilerParams(vmem_limit_bytes=KERNEL_LIMIT),
        cost_estimate=pl.CostEstimate(
            flops=3 * pairs * rows * DEGREES * DEGREES,
            bytes_accessed=2 * legendre.size + 4 * pairs * rows * DEGREES + 2 * arrived.size,
            transcendentals=0,
        ),
        name="analysis",
    )(lower_order, *in_vmem(arrived, legendre))


def factor_kernel(count, parts_ref, out_ref):
    total = jnp.sum(parts_ref[...], axis=0)
    size = total.shape[1]
    span = 8 * count
    power_pred = total
    power_true = pltpu.roll(total, size - span, 1)
    cross = pltpu.roll(total, size - 2 * span, 1)
    pred = jnp.maximum(power_pred, POWER_FLOOR)
    true = jnp.maximum(power_true, POWER_FLOOR)
    root_pred = jnp.sqrt(pred)
    root_true = jnp.sqrt(true)
    both = pred + true
    upper_mean = (pred * pred + true * true) / both
    inverse = 1.0 / (root_pred * root_true)
    coherence = cross * inverse
    mean_slope = (2.0 * pred - upper_mean) / both
    slope = (
        (root_pred - root_true) / root_pred
        + 2.0 * mean_slope * (1.0 - coherence)
        + upper_mean * coherence / pred
    )
    binds = jnp.where(power_pred > POWER_FLOOR, 1.0, jnp.where(power_pred == POWER_FLOOR, 0.5, 0.0))
    dpower = 2.0 * slope * binds
    dcross = -2.0 * upper_mean * inverse
    lane = lax.broadcasted_iota(jnp.int32, total.shape, 1)
    factors = jnp.where(lane < span, dpower, pltpu.roll(dcross, span, 1))[:, : out_ref.shape[-1]]
    out_ref[...] = jnp.broadcast_to(factors[None], out_ref.shape)


def factors_of(parts, count):
    lanes = round_up(16 * count, LANES)
    whole = pl.BlockSpec(memory_space=pltpu.VMEM)
    return pl.pallas_call(
        functools.partial(factor_kernel, count),
        in_specs=[whole],
        out_specs=whole,
        out_shape=pltpu.VMEM(parts.shape[:2] + (lanes,), jnp.float32),
        compiler_params=pltpu.CompilerParams(vmem_limit_bytes=KERNEL_LIMIT),
        cost_estimate=pl.CostEstimate(flops=parts.size, bytes_accessed=8 * parts.size, transcendentals=0),
        name="factors",
    )(*in_vmem(parts))


def synthesis_kernel(
    count, order_ref, coef_ref, last_ref, factor_ref, leg_ref, out_ref,
    spread_ref, upspread_ref, lower_ref, upper_ref, wide_ref,
):
    rows = 4 * count
    size = 16 * count
    lane = lax.broadcasted_iota(jnp.int32, (size, LANES), 1)

    before = None
    for tile in range(8):
        turned = factor_ref[tile * LANES : (tile + 1) * LANES, :].T[:size]
        spread_ref[:, tile * LANES : (tile + 1) * LANES] = turned
        shifted = pltpu.roll(turned, 1, 1)
        if tile >= 4:
            upspread_ref[:, (tile - 4) * LANES : (tile - 3) * LANES] = 2.0 * jnp.where(
                lane == 0, before, shifted
            )
        before = shifted

    def one_pair(p, carry):
        lower_order = order_ref[p]
        boundary = DEGREES - lower_order
        lower_weight = jnp.where(lower_order == 0, 1.0, 2.0)
        tiles_up = lower_order >> 7
        lanes_up = lower_order & (LANES - 1)
        back = (LANES - lanes_up) & (LANES - 1)

        def turned_tile(tile):
            at = pl.multiple_of((tile + tiles_up) * LANES, LANES)
            return pltpu.roll(spread_ref[:, pl.ds(at, LANES)], back, 1)

        def graded(factors, observe):
            grads = []
            for g in range(4):
                s = g // 2
                predicted = observe(2 * g * rows)
                observed = observe((2 * g + 1) * rows)
                grads.append(
                    factors[s * rows : (s + 1) * rows] * predicted
                    + factors[(2 + s) * rows : (3 + s) * rows] * observed
                )
            return jnp.concatenate(grads, axis=0)

        now = turned_tile(0)
        for tile in range(8):
            start = tile * LANES
            then = turned_tile(tile + 1)
            factors = lower_weight * jnp.where(lane < LANES - lanes_up, now, then)
            now = then
            row = lane + start
            if tile >= 4:
                factors = jnp.where(
                    row < boundary, factors, upspread_ref[:, start - HALF : start - HALF + LANES]
                )
            grad = graded(factors, lambda at: coef_ref[p, at : at + rows, start : start + LANES])
            if tile >= 4:
                upper_ref[:, start - HALF : start - HALF + LANES] = jnp.where(
                    row < boundary, 0.0, grad
                ).astype(jnp.bfloat16)
                grad = jnp.where(row < boundary, grad, 0.0)
            lower_ref[:, start : start + LANES] = grad.astype(jnp.bfloat16)
        last_factors = jnp.broadcast_to(2.0 * spread_ref[:, DEGREES - 1 : DEGREES], (size, LANES))
        last_grad = graded(last_factors, lambda at: last_ref[p, at : at + rows, :])
        last_grad = last_grad.astype(jnp.bfloat16).astype(jnp.float32)
        last_leg = leg_ref[p, DEGREES : DEGREES + 1, :].astype(jnp.float32)

        width = 256
        for tile in range(DEGREES // width):
            start = tile * width
            lower = dot_nn(lower_ref[...], leg_ref[p, :DEGREES, start : start + width])
            upper = dot_nn(upper_ref[...], leg_ref[p, HALF:DEGREES, start : start + width])
            for t, values in enumerate((lower, upper)):
                for sub in range(width // LANES):
                    at = start + sub * LANES
                    piece = values[:, sub * LANES : (sub + 1) * LANES]
                    if t == 1:
                        piece = piece + last_grad * last_leg[:, at : at + LANES]
                    blocks = [piece[g * rows : (g + 1) * rows] for g in range(4)]
                    blocks = [
                        block if g == 0 else pltpu.roll(block, 32 * g, 1) for g, block in enumerate(blocks)
                    ]
                    for i in range(4):
                        wide_ref[at // 32 + i, pl.ds(4 * t + p, rows, stride=SLOTS), :] = by_position(
                            blocks, i
                        )
        return carry

    lax.fori_loop(0, 4, one_pair, 0)

    def narrow(j, carry):
        out_ref[j] = wide_ref[j].astype(jnp.bfloat16)
        return carry

    lax.fori_loop(0, 32, narrow, 0)


def synthesis(lower_order, coeffs, last, factors, legendre, count):
    pairs = legendre.shape[0]
    rows = 32 * count
    whole = pl.BlockSpec(memory_space=pltpu.VMEM)
    return pl.pallas_call(
        functools.partial(synthesis_kernel, count),
        in_specs=[pl.BlockSpec(memory_space=pltpu.SMEM), whole, whole, whole, whole],
        out_specs=whole,
        out_shape=pltpu.VMEM((32, rows, LANES), jnp.bfloat16),
        scratch_shapes=[
            pltpu.VMEM((rows // 2, DEGREES + HALF), jnp.float32),
            pltpu.VMEM((rows // 2, HALF), jnp.float32),
            pltpu.VMEM((rows // 2, DEGREES), jnp.bfloat16),
            pltpu.VMEM((rows // 2, HALF), jnp.bfloat16),
            pltpu.VMEM((32, rows, LANES), jnp.float32),
        ],
        compiler_params=pltpu.CompilerParams(vmem_limit_bytes=KERNEL_LIMIT),
        cost_estimate=pl.CostEstimate(
            flops=3 * pairs * rows // 2 * DEGREES * DEGREES,
            bytes_accessed=2 * legendre.size + 4 * pairs * rows * DEGREES + 64 * rows * LANES,
            transcendentals=0,
        ),
        name="synthesis",
    )(lower_order, *in_vmem(coeffs, last, factors, legendre))


def unpack_kernel(turn_ref, pairs_ref, returned_ref, out_ref, lower_ref, upper_ref):
    @pl.when(pl.program_id(0) == 0)
    def _():
        one_hots(pairs_ref, lower_ref, upper_ref)

    turn = turn_ref[0]
    both = returned_ref[...].astype(jnp.float32).reshape(HALF // 8, 2, 2 * SLOTS, LANES)
    sides = [
        trade_halves(both[:, 0, c * SLOTS : (c + 1) * SLOTS], both[:, 1, c * SLOTS : (c + 1) * SLOTS])
        for c in range(2)
    ]
    for o, one_hot_ref in enumerate((lower_ref, upper_ref)):
        by_slot = jnp.concatenate([side[o].reshape(HALF, LANES) for side in sides], axis=1)
        field = dot_nn(by_slot.T.astype(jnp.bfloat16), one_hot_ref[...]).astype(jnp.bfloat16)
        for c in range(2):
            for z in range(4):
                at = c * LANES + z * 32
                out_ref[c, (z - turn) & 3, :, o * HALF : (o + 1) * HALF] = field[at : at + 32]


def unpack(turn, pairs, returned, count):
    devices = DEGREES // SLOTS
    grid_spec = pltpu.PrefetchScalarGridSpec(
        num_scalar_prefetch=1,
        grid=(count // 2,),
        in_specs=[
            pl.BlockSpec((1, HALF), lambda i, t: (0, 0)),
            pl.BlockSpec((devices, 16, LANES), lambda i, t: (0, i, 0)),
        ],
        out_specs=pl.BlockSpec((2, 4, 32, DEGREES), lambda i, t: (i, 0, 0, 0)),
        scratch_shapes=[pltpu.VMEM((HALF, HALF), jnp.bfloat16)] * 2,
    )
    return pl.pallas_call(
        unpack_kernel,
        grid_spec=grid_spec,
        out_shape=jax.ShapeDtypeStruct((count, 4, 32, DEGREES), jnp.bfloat16),
        compiler_params=pltpu.CompilerParams(vmem_limit_bytes=PACK_LIMIT),
        cost_estimate=pl.CostEstimate(
            flops=DEGREES * DEGREES * LANES * count,
            bytes_accessed=4 * LANES * DEGREES * count,
            transcendentals=0,
        ),
        name="unpack",
    )(turn, pairs, returned)


def exchange(values):
    return lax.all_to_all(values, AXES, split_axis=0, concat_axis=0, tiled=True)


def per_device(pred_four, target_four, legendre, pair_order):
    channels = pred_four.shape[0]
    pairs = legendre.shape[0]
    devices = DEGREES // SLOTS
    device = lax.axis_index(AXES)
    turn = (lax.axis_index("ma") & 3).reshape(1)
    lower_order = lax.dynamic_slice_in_dim(pair_order, device * pairs, pairs)
    pair_row = pair_order.reshape(1, HALF)

    by_group = (channels, 4, 32, DEGREES)
    packed = pack(
        turn, pair_row, pred_four.reshape(by_group), target_four.reshape(by_group), 0, channels
    )
    arrived = exchange(packed.reshape(devices, 2 * channels * SLOTS, LANES))
    coeffs, last, moments = analysis(lower_order, arrived, legendre, channels)
    spectra = exchange(moments.reshape(devices, SLOTS, -1))
    factors = exchange(factors_of(spectra, channels)).reshape(DEGREES, -1)
    going = synthesis(lower_order, coeffs, last, factors, legendre, channels)
    returned = exchange(going.reshape(devices, channels * SLOTS, LANES))
    return unpack(turn, pair_row, returned, channels).reshape(pred_four.shape)


def solution(mesh):
    placed = (
        P("col", None, None, "ma", None),
        P("col", None, None, "ma", None),
        P(AXES, None, None),
        P(),
    )
    return jax.shard_map(
        per_device,
        mesh=mesh,
        in_specs=placed,
        out_specs=P("col", None, None, "ma", None),
        check_vma=False,
    )
```

```python
import functools

import jax
import jax.numpy as jnp
from jax import lax
from jax.experimental import pallas as pl
from jax.experimental.pallas import tpu as pltpu
from jax.sharding import PartitionSpec as P

DEGREES = 1024
HALF = DEGREES // 2
POWER_FLOOR = 0.5
LANES = 128
SLOTS = 8
AXES = ("ma", "col")
PACK_LIMIT = 24 * 1024 * 1024
KERNEL_LIMIT = 40 * 1024 * 1024


def round_up(value, multiple):
    return -(-value // multiple) * multiple


def dot_nt(left, right):
    return lax.dot_general(left, right, (((1,), (1,)), ((), ())), preferred_element_type=jnp.float32)


def dot_nn(left, right):
    return lax.dot_general(left, right, (((1,), (0,)), ((), ())), preferred_element_type=jnp.float32)


def by_position(blocks, shift):
    group = lax.broadcasted_iota(jnp.int32, blocks[0].shape, 1) >> 5
    result = blocks[-shift % 4]
    for z in range(1, 4):
        result = jnp.where(group == z, blocks[(z - shift) % 4], result)
    return result


def one_hots(pairs_ref, lower_ref, upper_ref):
    row = jnp.broadcast_to(pairs_ref[...], (8, HALF)).astype(jnp.float32)
    order = row.T[:, :1].astype(jnp.int32)
    lane = lax.broadcasted_iota(jnp.int32, (HALF, HALF), 1)
    lower_ref[...] = jnp.where(lane == order, 1.0, 0.0).astype(jnp.bfloat16)
    upper_ref[...] = jnp.where(lane == HALF - 1 - order, 1.0, 0.0).astype(jnp.bfloat16)


def trade_halves(first, second):
    top = lax.broadcasted_iota(jnp.int32, first.shape, 1) < 4
    return (
        jnp.where(top, first, pltpu.roll(second, 4, 1)),
        jnp.where(top, pltpu.roll(first, 4, 1), second),
    )


def pack_kernel(
    count, turn_ref, pairs_hbm, pred_hbm, target_hbm, out_hbm,
    pairs_ref, field_ref, out_ref, lower_ref, upper_ref, pair_sem, in_sems, out_sems,
):
    def fetch(i, f):
        source = (pred_hbm, target_hbm)[f].at[pl.ds(2 * i, 2)]
        return pltpu.make_async_copy(source, field_ref.at[f, pl.ds(2 * i, 2)], in_sems.at[f, i])

    def send(i):
        return pltpu.make_async_copy(out_ref.at[i], out_hbm.at[:, :, i], out_sems.at[i])

    pair_copy = pltpu.make_async_copy(pairs_hbm, pairs_ref, pair_sem)
    pair_copy.start()
    for i in range(2):
        for f in range(2):
            fetch(i, f).start()
    pair_copy.wait()
    one_hots(pairs_ref, lower_ref, upper_ref)

    turn = turn_ref[0]

    def step(i, carry):
        @pl.when(i + 2 < count // 2)
        def _():
            for f in range(2):
                fetch(i + 2, f).start()

        for f in range(2):
            fetch(i, f).wait()
            field = jnp.concatenate(
                [field_ref[f, 2 * i + c, (z - turn) & 3] for c in range(2) for z in range(4)], axis=0
            )
            low = dot_nt(lower_ref[...], field[:, :HALF]).reshape(HALF // 8, 8, 2 * LANES)
            high = dot_nt(upper_ref[...], field[:, HALF:]).reshape(HALF // 8, 8, 2 * LANES)
            both = jnp.stack(trade_halves(low, high), axis=1).reshape(HALF // 4, 8, 2 * LANES)
            both = jnp.concatenate([both[:, :, :LANES], both[:, :, LANES:]], axis=1)
            out_ref[i, :, f] = both.astype(jnp.bfloat16)
        send(i).start()
        return carry

    lax.fori_loop(0, count // 2, step, 0)
    for i in range(count // 2):
        send(i).wait()


def pack(turn, pairs, pred, target, count):
    devices = DEGREES // SLOTS
    steps = count // 2
    far = pl.BlockSpec(memory_space=pltpu.HBM)
    return pl.pallas_call(
        functools.partial(pack_kernel, count),
        in_specs=[pl.BlockSpec(memory_space=pltpu.SMEM), far, far, far],
        out_specs=far,
        out_shape=pltpu.HBM((devices, 2, steps, 16, LANES), jnp.bfloat16),
        scratch_shapes=[
            pltpu.VMEM((1, HALF), jnp.int32),
            pltpu.VMEM((2, count, 4, 32, DEGREES), jnp.bfloat16),
            pltpu.VMEM((steps, devices, 2, 16, LANES), jnp.bfloat16),
            pltpu.VMEM((HALF, HALF), jnp.bfloat16),
            pltpu.VMEM((HALF, HALF), jnp.bfloat16),
            pltpu.SemaphoreType.DMA,
            pltpu.SemaphoreType.DMA((2, steps)),
            pltpu.SemaphoreType.DMA((steps,)),
        ],
        compiler_params=pltpu.CompilerParams(vmem_limit_bytes=PACK_LIMIT),
        cost_estimate=pl.CostEstimate(
            flops=DEGREES * DEGREES * 2 * LANES * count,
            bytes_accessed=8 * LANES * DEGREES * count,
            transcendentals=0,
        ),
        name="pack",
    )(turn, in_hbm(pairs), in_hbm(pred), in_hbm(target))


def moments_of(values, rows):
    width = values.shape[-1]
    shaped = values.reshape(4, 2, rows, width)
    pieces = []
    for left, right in ((0, 0), (1, 1), (0, 1)):
        for s in range(2):
            real = shaped[2 * s, left] * shaped[2 * s, right]
            imag = shaped[2 * s + 1, left] * shaped[2 * s + 1, right]
            pieces.append(real + imag)
    return jnp.concatenate(pieces, axis=0)


def analysis_kernel(
    count, order_ref, arrived_ref, source_ref, coef_ref, last_ref, moment_ref,
    narrow_ref, leg_ref, wide_ref, field_ref, raw_ref, lower_ref, upper_ref, tail_ref, sems, leg_sems,
):
    rows = 4 * count
    size = 24 * count
    span = count * SLOTS

    def chunk(k):
        at = pl.ds(4 * k, 4)
        return pltpu.make_async_copy(arrived_ref.at[at], narrow_ref.at[at], sems.at[k])

    def leg_copy(p):
        return pltpu.make_async_copy(source_ref.at[p], leg_ref.at[p], leg_sems.at[p])

    for k in range(8):
        chunk(k).start()
    lower_ref[...] = jnp.zeros_like(lower_ref)
    upper_ref[...] = jnp.zeros_like(upper_ref)
    tail_ref[...] = jnp.zeros_like(tail_ref)

    def build(k, carry):
        chunk(k).wait()

        @pl.when((k == 1) | (k == 4))
        def _():
            leg_copy(k // 4).start()

        for g in range(4):
            for col in range(4):
                for f in range(2):
                    blocks = [narrow_ref[4 * k + i, col, f] for i in range(4)]
                    block = by_position(blocks, g).astype(jnp.float32)
                    if g > 0:
                        block = pltpu.roll(block, LANES - 32 * g, 1)
                    wide_ref[g, f, col * span : (col + 1) * span, :] = block
            for slot in range(SLOTS):
                fields = [wide_ref[g, f, pl.ds(slot, rows, stride=SLOTS), :] for f in range(2)]
                at = pl.multiple_of(k * LANES, LANES)
                field_ref[slot, g * 2 * rows : (g + 1) * 2 * rows, pl.ds(at, LANES)] = (
                    jnp.concatenate(fields, axis=0).astype(jnp.bfloat16)
                )
        return carry

    lax.fori_loop(0, 8, build, 0)

    def one_pair(p, carry):
        @pl.when(p < 2)
        def _():
            leg_copy(p + 2).start()

        leg_copy(p).wait()
        lower_order = order_ref[p]
        boundary = DEGREES - lower_order
        width = 256
        late = (lower_order <= width).astype(jnp.int32)
        at = pl.multiple_of(HALF + width * late, width)
        extra = dot_nt(field_ref[4 * (1 - late) + p], leg_ref[p, pl.ds(at, width), :])
        for tile in range(DEGREES // width):
            start = tile * width
            values = dot_nt(field_ref[4 * (tile // 3) + p], leg_ref[p, start : start + width, :])
            if start >= HALF:
                row = lax.broadcasted_iota(jnp.int32, values.shape, 1) + start
                first, second = (values, extra) if tile == 2 else (extra, values)
                values = jnp.where(row < boundary, first, second)
            coef_ref[p, :, start : start + width] = values
            moments = moments_of(values, rows)
            raw_ref[:, start : start + width] = moments
            if start >= HALF:
                row = lax.broadcasted_iota(jnp.int32, moments.shape, 1) + start
                upper_ref[:, start - HALF : start - HALF + width] += jnp.where(
                    row < boundary, 0.0, moments
                )
        last_leg = jnp.broadcast_to(
            leg_ref[p, DEGREES : DEGREES + 1, :].astype(jnp.float32), (LANES, DEGREES)
        )
        last = dot_nt(field_ref[4 + p], last_leg.astype(jnp.bfloat16))
        last_ref[p] = last
        tail_ref[...] += moments_of(last, rows)

        lower_weight = jnp.where(lower_order == 0, 1.0, 2.0)
        tiles_up = lower_order >> 7
        lanes_up = lower_order & (LANES - 1)
        lane = lax.broadcasted_iota(jnp.int32, (size, LANES), 1)
        before = jnp.zeros((size, LANES), jnp.float32)
        for tile in range(8):
            turned = pltpu.roll(raw_ref[:, tile * LANES : (tile + 1) * LANES], lanes_up, 1)
            at = pl.multiple_of((tile + tiles_up) * LANES, LANES)
            lower_ref[:, pl.ds(at, LANES)] += lower_weight * jnp.where(lane < lanes_up, before, turned)
            before = turned
        return carry

    lax.fori_loop(0, 4, one_pair, 0)

    lane = lax.broadcasted_iota(jnp.int32, (size, LANES), 1)
    after = tail_ref[...]
    for tile in reversed(range(8)):
        total = lower_ref[:, tile * LANES : (tile + 1) * LANES]
        if tile >= 4:
            turned = pltpu.roll(upper_ref[:, (tile - 4) * LANES : (tile - 3) * LANES], LANES - 1, 1)
            total = total + 2.0 * jnp.where(lane == LANES - 1, after, turned)
            after = turned
        pad = moment_ref.shape[1] - size
        if pad > 0:
            total = jnp.concatenate([total, jnp.zeros((pad, LANES), jnp.float32)], axis=0)
        moment_ref[tile * LANES : (tile + 1) * LANES, :] = total.T


def in_vmem(value):
    return pltpu.with_memory_space_constraint(value, pltpu.VMEM)


def in_hbm(value):
    return pltpu.with_memory_space_constraint(value, pltpu.HBM)


def analysis(lower_order, arrived, legendre, count):
    pairs = legendre.shape[0]
    rows = 32 * count
    lanes = round_up(24 * count, LANES)
    arrived = arrived.reshape(32, 4, 2, count * SLOTS, LANES)
    whole = pl.BlockSpec(memory_space=pltpu.VMEM)
    return pl.pallas_call(
        functools.partial(analysis_kernel, count),
        in_specs=[pl.BlockSpec(memory_space=pltpu.SMEM)] + [pl.BlockSpec(memory_space=pltpu.HBM)] * 2,
        out_specs=[whole, whole, whole],
        out_shape=[
            pltpu.VMEM((pairs, rows, DEGREES), jnp.float32),
            pltpu.VMEM((pairs, rows, LANES), jnp.float32),
            pltpu.VMEM((DEGREES, lanes), jnp.float32),
        ],
        scratch_shapes=[
            pltpu.VMEM((32, 4, 2, count * SLOTS, LANES), jnp.bfloat16),
            pltpu.VMEM(legendre.shape, jnp.bfloat16),
            pltpu.VMEM((4, 2, rows, LANES), jnp.float32),
            pltpu.VMEM((SLOTS, rows, DEGREES), jnp.bfloat16),
            pltpu.VMEM((24 * count, DEGREES), jnp.float32),
            pltpu.VMEM((24 * count, DEGREES + HALF), jnp.float32),
            pltpu.VMEM((24 * count, HALF), jnp.float32),
            pltpu.VMEM((24 * count, LANES), jnp.float32),
            pltpu.SemaphoreType.DMA((8,)),
            pltpu.SemaphoreType.DMA((4,)),
        ],
        compiler_params=pltpu.CompilerParams(vmem_limit_bytes=KERNEL_LIMIT),
        cost_estimate=pl.CostEstimate(
            flops=3 * pairs * rows * DEGREES * DEGREES,
            bytes_accessed=2 * legendre.size + 4 * pairs * rows * DEGREES + 2 * arrived.size,
            transcendentals=0,
        ),
        name="analysis",
    )(lower_order, in_hbm(arrived), in_hbm(legendre))


def factor_kernel(count, parts_ref, out_ref):
    total = jnp.sum(parts_ref[...], axis=0)
    size = total.shape[1]
    span = 8 * count
    power_pred = total
    power_true = pltpu.roll(total, size - span, 1)
    cross = pltpu.roll(total, size - 2 * span, 1)
    pred = jnp.maximum(power_pred, POWER_FLOOR)
    true = jnp.maximum(power_true, POWER_FLOOR)
    root_pred = jnp.sqrt(pred)
    root_true = jnp.sqrt(true)
    both = pred + true
    upper_mean = (pred * pred + true * true) / both
    inverse = 1.0 / (root_pred * root_true)
    coherence = cross * inverse
    mean_slope = (2.0 * pred - upper_mean) / both
    slope = (
        (root_pred - root_true) / root_pred
        + 2.0 * mean_slope * (1.0 - coherence)
        + upper_mean * coherence / pred
    )
    binds = jnp.where(power_pred > POWER_FLOOR, 1.0, jnp.where(power_pred == POWER_FLOOR, 0.5, 0.0))
    dpower = 2.0 * slope * binds
    dcross = -2.0 * upper_mean * inverse
    lane = lax.broadcasted_iota(jnp.int32, total.shape, 1)
    factors = jnp.where(lane < span, dpower, pltpu.roll(dcross, span, 1))[:, : out_ref.shape[-1]]
    out_ref[...] = jnp.broadcast_to(factors[None], out_ref.shape)


def factors_of(parts, count):
    lanes = round_up(16 * count, LANES)
    whole = pl.BlockSpec(memory_space=pltpu.VMEM)
    return pl.pallas_call(
        functools.partial(factor_kernel, count),
        in_specs=[whole],
        out_specs=whole,
        out_shape=pltpu.VMEM(parts.shape[:2] + (lanes,), jnp.float32),
        compiler_params=pltpu.CompilerParams(vmem_limit_bytes=KERNEL_LIMIT),
        cost_estimate=pl.CostEstimate(flops=parts.size, bytes_accessed=8 * parts.size, transcendentals=0),
        name="factors",
    )(in_vmem(parts))


def synthesis_kernel(
    count, order_ref, coef_ref, last_ref, factor_ref, leg_ref, out_ref,
    spread_ref, upspread_ref, lower_ref, upper_ref, wide_ref,
):
    rows = 4 * count
    size = 16 * count
    lane = lax.broadcasted_iota(jnp.int32, (size, LANES), 1)

    before = None
    for tile in range(8):
        turned = factor_ref[tile * LANES : (tile + 1) * LANES, :].T[:size]
        spread_ref[:, tile * LANES : (tile + 1) * LANES] = turned
        shifted = pltpu.roll(turned, 1, 1)
        if tile >= 4:
            upspread_ref[:, (tile - 4) * LANES : (tile - 3) * LANES] = 2.0 * jnp.where(
                lane == 0, before, shifted
            )
        before = shifted

    def one_pair(p, carry):
        lower_order = order_ref[p]
        boundary = DEGREES - lower_order
        lower_weight = jnp.where(lower_order == 0, 1.0, 2.0)
        tiles_up = lower_order >> 7
        lanes_up = lower_order & (LANES - 1)
        back = (LANES - lanes_up) & (LANES - 1)

        def turned_tile(tile):
            at = pl.multiple_of((tile + tiles_up) * LANES, LANES)
            return pltpu.roll(spread_ref[:, pl.ds(at, LANES)], back, 1)

        def graded(factors, observe):
            grads = []
            for g in range(4):
                s = g // 2
                predicted = observe(2 * g * rows)
                observed = observe((2 * g + 1) * rows)
                grads.append(
                    factors[s * rows : (s + 1) * rows] * predicted
                    + factors[(2 + s) * rows : (3 + s) * rows] * observed
                )
            return jnp.concatenate(grads, axis=0)

        now = turned_tile(0)
        for tile in range(8):
            start = tile * LANES
            then = turned_tile(tile + 1)
            factors = lower_weight * jnp.where(lane < LANES - lanes_up, now, then)
            now = then
            row = lane + start
            if tile >= 4:
                factors = jnp.where(
                    row < boundary, factors, upspread_ref[:, start - HALF : start - HALF + LANES]
                )
            grad = graded(factors, lambda at: coef_ref[p, at : at + rows, start : start + LANES])
            if tile >= 4:
                upper_ref[:, start - HALF : start - HALF + LANES] = jnp.where(
                    row < boundary, 0.0, grad
                ).astype(jnp.bfloat16)
                grad = jnp.where(row < boundary, grad, 0.0)
            lower_ref[:, start : start + LANES] = grad.astype(jnp.bfloat16)
        last_factors = jnp.broadcast_to(2.0 * spread_ref[:, DEGREES - 1 : DEGREES], (size, LANES))
        last_grad = graded(last_factors, lambda at: last_ref[p, at : at + rows, :])
        last_grad = last_grad.astype(jnp.bfloat16).astype(jnp.float32)
        last_leg = leg_ref[p, DEGREES : DEGREES + 1, :].astype(jnp.float32)

        width = 256
        for tile in range(DEGREES // width):
            start = tile * width
            lower = dot_nn(lower_ref[...], leg_ref[p, :DEGREES, start : start + width])
            upper = dot_nn(upper_ref[...], leg_ref[p, HALF:DEGREES, start : start + width])
            for t, values in enumerate((lower, upper)):
                for sub in range(width // LANES):
                    at = start + sub * LANES
                    piece = values[:, sub * LANES : (sub + 1) * LANES]
                    if t == 1:
                        piece = piece + last_grad * last_leg[:, at : at + LANES]
                    blocks = [piece[g * rows : (g + 1) * rows] for g in range(4)]
                    blocks = [
                        block if g == 0 else pltpu.roll(block, 32 * g, 1) for g, block in enumerate(blocks)
                    ]
                    for i in range(4):
                        wide_ref[at // 32 + i, pl.ds(4 * t + p, rows, stride=SLOTS), :] = by_position(
                            blocks, i
                        )
        return carry

    lax.fori_loop(0, 4, one_pair, 0)

    def narrow(j, carry):
        out_ref[j] = wide_ref[j].astype(jnp.bfloat16)
        return carry

    lax.fori_loop(0, 32, narrow, 0)


def synthesis(lower_order, coeffs, last, factors, legendre, count):
    pairs = legendre.shape[0]
    rows = 32 * count
    whole = pl.BlockSpec(memory_space=pltpu.VMEM)
    return pl.pallas_call(
        functools.partial(synthesis_kernel, count),
        in_specs=[pl.BlockSpec(memory_space=pltpu.SMEM), whole, whole, whole, whole],
        out_specs=whole,
        out_shape=pltpu.VMEM((32, rows, LANES), jnp.bfloat16),
        scratch_shapes=[
            pltpu.VMEM((rows // 2, DEGREES + HALF), jnp.float32),
            pltpu.VMEM((rows // 2, HALF), jnp.float32),
            pltpu.VMEM((rows // 2, DEGREES), jnp.bfloat16),
            pltpu.VMEM((rows // 2, HALF), jnp.bfloat16),
            pltpu.VMEM((32, rows, LANES), jnp.float32),
        ],
        compiler_params=pltpu.CompilerParams(vmem_limit_bytes=KERNEL_LIMIT),
        cost_estimate=pl.CostEstimate(
            flops=3 * pairs * rows // 2 * DEGREES * DEGREES,
            bytes_accessed=2 * legendre.size + 4 * pairs * rows * DEGREES + 64 * rows * LANES,
            transcendentals=0,
        ),
        name="synthesis",
    )(lower_order, *(in_vmem(value) for value in (coeffs, last, factors, legendre)))


def unpack_kernel(turn_ref, pairs_ref, returned_ref, out_ref, lower_ref, upper_ref):
    @pl.when(pl.program_id(0) == 0)
    def _():
        one_hots(pairs_ref, lower_ref, upper_ref)

    turn = turn_ref[0]
    both = returned_ref[...].astype(jnp.float32).reshape(HALF // 8, 2, 2 * SLOTS, LANES)
    sides = [
        trade_halves(both[:, 0, c * SLOTS : (c + 1) * SLOTS], both[:, 1, c * SLOTS : (c + 1) * SLOTS])
        for c in range(2)
    ]
    for o, one_hot_ref in enumerate((lower_ref, upper_ref)):
        by_slot = jnp.concatenate([side[o].reshape(HALF, LANES) for side in sides], axis=1)
        field = dot_nn(by_slot.T.astype(jnp.bfloat16), one_hot_ref[...]).astype(jnp.bfloat16)
        for c in range(2):
            for z in range(4):
                at = c * LANES + z * 32
                out_ref[c, (z - turn) & 3, :, o * HALF : (o + 1) * HALF] = field[at : at + 32]


def unpack(turn, pairs, returned, count):
    devices = DEGREES // SLOTS
    grid_spec = pltpu.PrefetchScalarGridSpec(
        num_scalar_prefetch=1,
        grid=(count // 2,),
        in_specs=[
            pl.BlockSpec((1, HALF), lambda i, t: (0, 0)),
            pl.BlockSpec((devices, 16, LANES), lambda i, t: (0, i, 0)),
        ],
        out_specs=pl.BlockSpec((2, 4, 32, DEGREES), lambda i, t: (i, 0, 0, 0)),
        scratch_shapes=[pltpu.VMEM((HALF, HALF), jnp.bfloat16)] * 2,
    )
    return pl.pallas_call(
        unpack_kernel,
        grid_spec=grid_spec,
        out_shape=jax.ShapeDtypeStruct((count, 4, 32, DEGREES), jnp.bfloat16),
        compiler_params=pltpu.CompilerParams(vmem_limit_bytes=PACK_LIMIT),
        cost_estimate=pl.CostEstimate(
            flops=DEGREES * DEGREES * LANES * count,
            bytes_accessed=4 * LANES * DEGREES * count,
            transcendentals=0,
        ),
        name="unpack",
    )(turn, pairs, returned)


def exchange(values):
    return lax.all_to_all(values, AXES, split_axis=0, concat_axis=0, tiled=True)


def per_device(pred_four, target_four, legendre, pair_order):
    channels = pred_four.shape[0]
    pairs = legendre.shape[0]
    devices = DEGREES // SLOTS
    device = lax.axis_index(AXES)
    turn = (lax.axis_index("ma") & 3).reshape(1)
    lower_order = lax.dynamic_slice_in_dim(pair_order, device * pairs, pairs)
    pair_row = pair_order.reshape(1, HALF)

    by_group = (channels, 4, 32, DEGREES)
    packed = pack(
        turn, pair_row, pred_four.reshape(by_group), target_four.reshape(by_group), channels
    )
    arrived = exchange(packed.reshape(devices, 2 * channels * SLOTS, LANES))
    coeffs, last, moments = analysis(lower_order, arrived, legendre, channels)
    spectra = exchange(moments.reshape(devices, SLOTS, -1))
    factors = exchange(factors_of(spectra, channels)).reshape(DEGREES, -1)
    going = synthesis(lower_order, coeffs, last, factors, legendre, channels)
    returned = exchange(going.reshape(devices, channels * SLOTS, LANES))
    return unpack(turn, pair_row, returned, channels).reshape(pred_four.shape)


def solution(mesh):
    placed = (
        P("col", None, None, "ma", None),
        P("col", None, None, "ma", None),
        P(AXES, None, None),
        P(),
    )
    return jax.shard_map(
        per_device,
        mesh=mesh,
        in_specs=placed,
        out_specs=P("col", None, None, "ma", None),
        check_vma=False,
    )
```

```python
import functools

import jax
import jax.numpy as jnp
from jax import lax
from jax.experimental import pallas as pl
from jax.experimental.pallas import tpu as pltpu
from jax.sharding import Mesh
from jax.sharding import PartitionSpec as P

DEGREES = 1024
HALF = DEGREES // 2
POWER_FLOOR = 0.5
LANES = 128
SLOTS = 8
PAIRS = 4
DEVICES = ("zx", "core", "col")
SAME_CORE = ("zx", "col")
KERNEL_LIMIT = 36 * 1024 * 1024
SMALL_LIMIT = 16 * 1024 * 1024
TINY_LIMIT = 4 * 1024 * 1024


def dot_nt(left, right):
    return lax.dot_general(left, right, (((1,), (1,)), ((), ())), preferred_element_type=jnp.float32)


def dot_nn(left, right):
    return lax.dot_general(left, right, (((1,), (0,)), ((), ())), preferred_element_type=jnp.float32)


def by_position(blocks, shift):
    group = lax.broadcasted_iota(jnp.int32, blocks[0].shape, 1) >> 5
    result = blocks[-shift % 4]
    for z in range(1, 4):
        result = jnp.where(group == z, blocks[(z - shift) % 4], result)
    return result


def trade_halves(first, second):
    top = lax.broadcasted_iota(jnp.int32, first.shape, 1) < 4
    return (
        jnp.where(top, first, pltpu.roll(second, 4, 1)),
        jnp.where(top, pltpu.roll(first, 4, 1), second),
    )


def one_hots(pairs_ref, lower_ref, upper_ref):
    order = jnp.broadcast_to(pairs_ref[...].astype(jnp.float32), (LANES, HALF)).T
    by_core = order.reshape(16, 2, 2, 8, LANES)
    first, second = by_core[:, 0].reshape(32, 8, LANES), by_core[:, 1].reshape(32, 8, LANES)
    order = jnp.stack(trade_halves(first, second), axis=1).reshape(HALF, LANES)
    order = jnp.concatenate([order] * (HALF // LANES), axis=1).astype(jnp.int32)
    lane = lax.broadcasted_iota(jnp.int32, (HALF, HALF), 1)
    lower_ref[...] = jnp.where(lane == order, 1.0, 0.0).astype(jnp.bfloat16)
    upper_ref[...] = jnp.where(lane == HALF - 1 - order, 1.0, 0.0).astype(jnp.bfloat16)


def pack_kernel(
    channels, turn_ref, pairs_hbm, pred_hbm, target_hbm, out_hbm,
    pairs_ref, field_ref, out_ref, lower_ref, upper_ref, pair_sem, in_sems, out_sems,
):
    steps = channels // 2
    ahead = 2

    def fetch(i, f):
        source = (pred_hbm, target_hbm)[f].at[pl.ds(2 * i, 2)]
        return pltpu.make_async_copy(source, field_ref.at[f, pl.ds(2 * i, 2)], in_sems.at[f, i])

    def send(i):
        return pltpu.make_async_copy(
            out_ref.at[i], out_hbm.at[:, :, :, pl.ds(2 * i, 2)], out_sems.at[i]
        )

    pair_copy = pltpu.make_async_copy(pairs_hbm, pairs_ref, pair_sem)
    pair_copy.start()
    for i in range(ahead):
        for f in range(2):
            fetch(i, f).start()
    pair_copy.wait()
    one_hots(pairs_ref, lower_ref, upper_ref)

    turn = turn_ref[0]

    def step(i, carry):
        @pl.when(i + ahead < steps)
        def _():
            for f in range(2):
                fetch(i + ahead, f).start()

        for f in range(2):
            fetch(i, f).wait()
        for c in range(2):
            pieces = []
            for sample in range(2):
                for z in range(4):
                    group = (z - turn) & 3
                    pieces.append(field_ref[group >> 1, 2 * i + c, 2 * sample + (group & 1)])
            field = jnp.concatenate(pieces, axis=0)
            low = dot_nt(lower_ref[...], field[:, :HALF]).reshape(HALF // 8, 8, 2 * LANES)
            high = dot_nt(upper_ref[...], field[:, HALF:]).reshape(HALF // 8, 8, 2 * LANES)
            both = jnp.concatenate([low, high], axis=1).astype(jnp.bfloat16)
            for sample in range(2):
                block = both[:, :, sample * LANES : (sample + 1) * LANES]
                out_ref[i, :, sample, :, c] = block.reshape(16, 4, 16, LANES)
        send(i).start()
        return carry

    lax.fori_loop(0, steps, step, 0)
    for i in range(steps):
        send(i).wait()


def pack(turn, pairs, pred, target):
    channels = pred.shape[0]
    steps = channels // 2
    far = pl.BlockSpec(memory_space=pltpu.HBM)
    return pl.pallas_call(
        functools.partial(pack_kernel, channels),
        in_specs=[pl.BlockSpec(memory_space=pltpu.SMEM), far, far, far],
        out_specs=far,
        out_shape=pltpu.HBM((16, 2, 4, channels, 16, LANES), jnp.bfloat16),
        scratch_shapes=[
            pltpu.VMEM((1, HALF), jnp.int32),
            pltpu.VMEM((2, channels, 4, 32, DEGREES), jnp.bfloat16),
            pltpu.VMEM((steps, 16, 2, 4, 2, 16, LANES), jnp.bfloat16),
            pltpu.VMEM((HALF, HALF), jnp.bfloat16),
            pltpu.VMEM((HALF, HALF), jnp.bfloat16),
            pltpu.SemaphoreType.DMA,
            pltpu.SemaphoreType.DMA((2, steps)),
            pltpu.SemaphoreType.DMA((steps,)),
        ],
        compiler_params=pltpu.CompilerParams(vmem_limit_bytes=KERNEL_LIMIT),
        cost_estimate=pl.CostEstimate(
            flops=DEGREES * DEGREES * 2 * LANES * channels,
            bytes_accessed=8 * LANES * DEGREES * channels,
            transcendentals=0,
        ),
        name="pack",
    )(turn, in_hbm(pairs), in_hbm(pred), in_hbm(target))


def moments_of(values, rows):
    shaped = values.reshape(2, 2, rows, values.shape[-1])
    pieces = []
    for left, right in ((0, 0), (1, 1), (0, 1)):
        real = shaped[left, 0] * shaped[right, 0]
        imag = shaped[left, 1] * shaped[right, 1]
        pieces.append(real + imag)
    return jnp.concatenate(pieces, axis=0)


def leg_stream(own_hbm, other_hbm, leg_ref, sems):
    def start(p):
        for hbm, here in ((own_hbm, p < PAIRS), (other_hbm, p >= PAIRS)):

            @pl.when(here)
            def _(hbm=hbm):
                at = p & 3
                pltpu.make_async_copy(hbm.at[at], leg_ref.at[at], sems.at[at]).start()

    def wait(p):
        at = p & 3
        pltpu.make_async_copy(own_hbm.at[at], leg_ref.at[at], sems.at[at]).wait()

    return start, wait


def analysis_kernel(
    rows, scalar_ref, arrived_ref, own_hbm, other_hbm, coef_ref, last_ref, moment_ref,
    narrow_ref, leg_ref, wide_ref, field_ref, lower_ref, upper_ref, tail_ref, sems, leg_sems,
):
    size = 3 * rows
    span = arrived_ref.shape[2]
    slots = 2 * SLOTS

    def chunk(k):
        at = pl.ds(4 * k, 4)
        return pltpu.make_async_copy(arrived_ref.at[at], narrow_ref.at[at], sems.at[k])

    start_leg, wait_leg = leg_stream(own_hbm, other_hbm, leg_ref, leg_sems)
    for k in range(8):
        chunk(k).start()
    lower_ref[...] = jnp.zeros_like(lower_ref)
    upper_ref[...] = jnp.zeros_like(upper_ref)
    tail_ref[...] = jnp.zeros_like(tail_ref)

    def build(k, carry):
        chunk(k).wait()

        @pl.when((k == 1) | (k == 3) | (k == 5))
        def _():
            start_leg(k >> 1)

        at = pl.multiple_of(k * LANES, LANES)
        for f in range(2):
            for q in range(2):
                g = 2 * f + q
                for col in range(4):
                    blocks = [narrow_ref[4 * k + i, col] for i in range(4)]
                    block = by_position(blocks, g).astype(jnp.float32)
                    if g > 0:
                        block = pltpu.roll(block, LANES - 32 * g, 1)
                    wide_ref[g, col * span : (col + 1) * span, :] = block
            for slot in range(slots):
                parts = [wide_ref[2 * f + q, pl.ds(slot, rows, stride=slots), :] for q in range(2)]
                low = 4 * rows * (slot // SLOTS) + 2 * f * rows
                field_ref[slot % SLOTS, low : low + 2 * rows, pl.ds(at, LANES)] = jnp.concatenate(
                    parts, axis=0
                ).astype(jnp.bfloat16)
        return carry

    lax.fori_loop(0, 8, build, 0)
    core = scalar_ref[2 * PAIRS]

    def one_pair(p, carry):
        @pl.when(p + 3 < 2 * PAIRS)
        def _():
            start_leg(p + 3)

        wait_leg(p)
        ring = p & 3
        slot = p ^ (core * PAIRS)
        lower_order = scalar_ref[p]
        boundary = DEGREES - lower_order
        width = 256
        lower_weight = jnp.where(lower_order == 0, 1.0, 2.0)
        tiles_up = lower_order >> 7
        lanes_up = lower_order & (LANES - 1)
        lane = lax.broadcasted_iota(jnp.int32, (size, LANES), 1)
        before = jnp.zeros((size, LANES), jnp.float32)
        for tile in range(DEGREES // width):
            start = tile * width
            count = 4 * rows if start < HALF else 8 * rows
            values = dot_nt(field_ref[slot, :count], leg_ref[ring, start : start + width, :])
            if start >= HALF:
                lower, upper = values[: 4 * rows], values[4 * rows :]
                row = lax.broadcasted_iota(jnp.int32, lower.shape, 1) + start
                values = jnp.where(row < boundary, lower, upper)
            coef_ref[p, :, start : start + width] = values
            for sub in range(width // LANES):
                moments = moments_of(values[:, sub * LANES : (sub + 1) * LANES], rows)
                now = start + sub * LANES
                if start >= HALF:
                    upper_ref[:, now - HALF : now - HALF + LANES] += jnp.where(
                        lane + now < boundary, 0.0, moments
                    )
                turned = pltpu.roll(moments, lanes_up, 1)
                at = pl.multiple_of(now + tiles_up * LANES, LANES)
                lower_ref[:, pl.ds(at, LANES)] += lower_weight * jnp.where(
                    lane < lanes_up, before, turned
                )
                before = turned
        last_leg = jnp.broadcast_to(
            leg_ref[ring, DEGREES : DEGREES + 1, :].astype(jnp.float32), (LANES, DEGREES)
        )
        last = dot_nt(field_ref[slot, 4 * rows :], last_leg.astype(jnp.bfloat16))
        last_ref[p] = last
        tail_ref[...] += moments_of(last, rows)
        return carry

    lax.fori_loop(0, 2 * PAIRS, one_pair, 0)

    lane = lax.broadcasted_iota(jnp.int32, (size, LANES), 1)
    after = tail_ref[...]
    for tile in reversed(range(8)):
        total = lower_ref[:, tile * LANES : (tile + 1) * LANES]
        if tile >= 4:
            turned = pltpu.roll(upper_ref[:, (tile - 4) * LANES : (tile - 3) * LANES], LANES - 1, 1)
            total = total + 2.0 * jnp.where(lane == LANES - 1, after, turned)
            after = turned
        total = jnp.concatenate([total, jnp.zeros((LANES - size, LANES), jnp.float32)], axis=0)
        moment_ref[tile * LANES : (tile + 1) * LANES, :] = total.T


def in_vmem(value):
    return pltpu.with_memory_space_constraint(value, pltpu.VMEM)


def in_hbm(value):
    return pltpu.with_memory_space_constraint(value, pltpu.HBM)


def analysis(scalars, arrived, own, other, rows):
    leg_rows = own.shape[1]
    span = rows * 4
    arrived = arrived.reshape(32, 4, span, LANES)
    whole = pl.BlockSpec(memory_space=pltpu.VMEM)
    far = pl.BlockSpec(memory_space=pltpu.HBM)
    return pl.pallas_call(
        functools.partial(analysis_kernel, rows),
        in_specs=[pl.BlockSpec(memory_space=pltpu.SMEM), far, far, far],
        out_specs=[whole, whole, whole],
        out_shape=[
            pltpu.VMEM((2 * PAIRS, 4 * rows, DEGREES), jnp.float32),
            pltpu.VMEM((2 * PAIRS, 4 * rows, LANES), jnp.float32),
            pltpu.VMEM((DEGREES, LANES), jnp.float32),
        ],
        scratch_shapes=[
            pltpu.VMEM((32, 4, span, LANES), jnp.bfloat16),
            pltpu.VMEM((4, leg_rows, DEGREES), jnp.bfloat16),
            pltpu.VMEM((4, 4 * span, LANES), jnp.float32),
            pltpu.VMEM((SLOTS, 8 * rows, DEGREES), jnp.bfloat16),
            pltpu.VMEM((3 * rows, DEGREES + HALF), jnp.float32),
            pltpu.VMEM((3 * rows, HALF), jnp.float32),
            pltpu.VMEM((3 * rows, LANES), jnp.float32),
            pltpu.SemaphoreType.DMA((8,)),
            pltpu.SemaphoreType.DMA((4,)),
        ],
        compiler_params=pltpu.CompilerParams(vmem_limit_bytes=KERNEL_LIMIT),
        cost_estimate=pl.CostEstimate(
            flops=20 * rows * PAIRS * DEGREES * DEGREES,
            bytes_accessed=4 * own.size + 16 * rows * PAIRS * DEGREES + 2 * arrived.size,
            transcendentals=0,
        ),
        name="analysis",
    )(scalars, in_hbm(arrived), in_hbm(own), in_hbm(other))


def factor_kernel(span, parts_ref, out_ref):
    total = jnp.sum(parts_ref[...], axis=0)
    size = total.shape[1]
    power_pred = total
    power_true = pltpu.roll(total, size - span, 1)
    cross = pltpu.roll(total, size - 2 * span, 1)
    pred = jnp.maximum(power_pred, POWER_FLOOR)
    true = jnp.maximum(power_true, POWER_FLOOR)
    root_pred = jnp.sqrt(pred)
    root_true = jnp.sqrt(true)
    both = pred + true
    upper_mean = (pred * pred + true * true) / both
    inverse = 1.0 / (root_pred * root_true)
    coherence = cross * inverse
    mean_slope = (2.0 * pred - upper_mean) / both
    slope = (
        (root_pred - root_true) / root_pred
        + 2.0 * mean_slope * (1.0 - coherence)
        + upper_mean * coherence / pred
    )
    binds = jnp.where(power_pred > POWER_FLOOR, 1.0, jnp.where(power_pred == POWER_FLOOR, 0.5, 0.0))
    dpower = 2.0 * slope * binds
    dcross = -2.0 * upper_mean * inverse
    lane = lax.broadcasted_iota(jnp.int32, total.shape, 1)
    factors = jnp.where(lane < span, dpower, pltpu.roll(dcross, span, 1))
    out_ref[...] = jnp.broadcast_to(factors[None], out_ref.shape)


def factors_of(parts, rows):
    whole = pl.BlockSpec(memory_space=pltpu.VMEM)
    return pl.pallas_call(
        functools.partial(factor_kernel, rows),
        in_specs=[whole],
        out_specs=whole,
        out_shape=pltpu.VMEM(parts.shape, jnp.float32),
        compiler_params=pltpu.CompilerParams(vmem_limit_bytes=TINY_LIMIT),
        cost_estimate=pl.CostEstimate(flops=parts.size, bytes_accessed=8 * parts.size, transcendentals=0),
        name="factors",
    )(in_vmem(parts))


def synthesis_kernel(
    rows, scalar_ref, coef_ref, last_ref, factor_ref, own_ref, other_ref, out_ref,
    spread_ref, upspread_ref, early_ref, late_ref, wide_ref,
):
    size = 2 * rows
    lane = lax.broadcasted_iota(jnp.int32, (size, LANES), 1)
    before = None
    for tile in range(8):
        turned = factor_ref[tile * LANES : (tile + 1) * LANES, :].T[:size]
        spread_ref[:, tile * LANES : (tile + 1) * LANES] = turned
        shifted = pltpu.roll(turned, 1, 1)
        if tile >= 4:
            upspread_ref[:, (tile - 4) * LANES : (tile - 3) * LANES] = 2.0 * jnp.where(
                lane == 0, before, shifted
            )
        before = shifted
    core = scalar_ref[2 * PAIRS]

    def one_pair(leg_ref, first, ring, carry):
        p = first + ring
        slot = p ^ (core * PAIRS)
        lower_order = scalar_ref[p]
        boundary = DEGREES - lower_order
        lower_weight = jnp.where(lower_order == 0, 1.0, 2.0)
        tiles_up = lower_order >> 7
        lanes_up = lower_order & (LANES - 1)
        back = (LANES - lanes_up) & (LANES - 1)

        def turned_tile(tile):
            at = pl.multiple_of((tile + tiles_up) * LANES, LANES)
            return pltpu.roll(spread_ref[:, pl.ds(at, LANES)], back, 1)

        def graded(factors, observe):
            grads = []
            for q in range(2):
                predicted = observe(q * rows)
                observed = observe((2 + q) * rows)
                grads.append(factors[:rows] * predicted + factors[rows:] * observed)
            return jnp.concatenate(grads, axis=0)

        now = turned_tile(0)
        for tile in range(8):
            start = tile * LANES
            then = turned_tile(tile + 1)
            factors = lower_weight * jnp.where(lane < LANES - lanes_up, now, then)
            now = then
            row = lane + start
            if tile >= 4:
                factors = jnp.where(
                    row < boundary, factors, upspread_ref[:, start - HALF : start - HALF + LANES]
                )
            grad = graded(factors, lambda at: coef_ref[p, at : at + rows, start : start + LANES])
            if tile >= 4:
                at = start - HALF
                late_ref[:size, at : at + LANES] = jnp.where(row < boundary, grad, 0.0).astype(
                    jnp.bfloat16
                )
                late_ref[size:, at : at + LANES] = jnp.where(row < boundary, 0.0, grad).astype(
                    jnp.bfloat16
                )
            else:
                early_ref[:, start : start + LANES] = grad.astype(jnp.bfloat16)
        last_factors = jnp.broadcast_to(2.0 * spread_ref[:, DEGREES - 1 : DEGREES], (size, LANES))
        last_grad = graded(last_factors, lambda at: last_ref[p, at : at + rows, :])
        last_grad = last_grad.astype(jnp.bfloat16).astype(jnp.float32)
        last_leg = leg_ref[ring, DEGREES : DEGREES + 1, :].astype(jnp.float32)

        width = 256
        for tile in range(DEGREES // width):
            start = tile * width
            early = dot_nn(early_ref[...], leg_ref[ring, :HALF, start : start + width])
            late = dot_nn(late_ref[...], leg_ref[ring, HALF:DEGREES, start : start + width])
            lower, upper = early + late[:size], late[size:]
            for sub in range(width // LANES):
                at = start + sub * LANES
                inside = slice(sub * LANES, (sub + 1) * LANES)
                top = lower[:, inside]
                bottom = upper[:, inside] + last_grad * last_leg[:, at : at + LANES]
                blocks = [top[:rows], top[rows:], bottom[:rows], bottom[rows:]]
                blocks = [
                    block if g == 0 else pltpu.roll(block, 32 * g, 1) for g, block in enumerate(blocks)
                ]
                for i in range(4):
                    wide_ref[at // 32 + i, pl.ds(slot, rows, stride=SLOTS), :] = by_position(blocks, i)
        return carry

    lax.fori_loop(0, PAIRS, functools.partial(one_pair, own_ref, 0), 0)
    lax.fori_loop(0, PAIRS, functools.partial(one_pair, other_ref, PAIRS), 0)

    def narrow(j, carry):
        out_ref[j] = wide_ref[j].astype(jnp.bfloat16)
        return carry

    lax.fori_loop(0, 32, narrow, 0)


def synthesis(scalars, coeffs, last, factors, own, other, rows):
    whole = pl.BlockSpec(memory_space=pltpu.VMEM)
    return pl.pallas_call(
        functools.partial(synthesis_kernel, rows),
        in_specs=[pl.BlockSpec(memory_space=pltpu.SMEM)] + [whole] * 5,
        out_specs=whole,
        out_shape=pltpu.VMEM((32, rows * SLOTS, LANES), jnp.bfloat16),
        scratch_shapes=[
            pltpu.VMEM((2 * rows, DEGREES + HALF), jnp.float32),
            pltpu.VMEM((2 * rows, HALF), jnp.float32),
            pltpu.VMEM((2 * rows, HALF), jnp.bfloat16),
            pltpu.VMEM((4 * rows, HALF), jnp.bfloat16),
            pltpu.VMEM((32, rows * SLOTS, LANES), jnp.float32),
        ],
        compiler_params=pltpu.CompilerParams(vmem_limit_bytes=SMALL_LIMIT),
        cost_estimate=pl.CostEstimate(
            flops=12 * rows * PAIRS * DEGREES * DEGREES,
            bytes_accessed=4 * own.size + 16 * rows * PAIRS * DEGREES + 64 * rows * SLOTS * LANES,
            transcendentals=0,
        ),
        name="synthesis",
    )(scalars, *(in_vmem(value) for value in (coeffs, last, factors, own, other)))


def unpack_kernel(turn_ref, pairs_ref, returned_ref, out_ref, lower_ref, upper_ref):
    @pl.when(pl.program_id(0) == 0)
    def _():
        one_hots(pairs_ref, lower_ref, upper_ref)

    turn = turn_ref[0]
    both = returned_ref[...].astype(jnp.float32)
    sides = []
    for c in range(2):
        first, second = (
            both[:, sample, :, c * SLOTS : (c + 1) * SLOTS].reshape(HALF, LANES) for sample in range(2)
        )
        group = lax.broadcasted_iota(jnp.int32, first.shape, 1) >> 5
        keep = ((group - turn) & 3) < 2
        sides.append(
            (
                jnp.where(keep, first, pltpu.roll(second, 64, 1)),
                jnp.where(keep, pltpu.roll(first, 64, 1), second),
            )
        )
    for o, one_hot_ref in enumerate((lower_ref, upper_ref)):
        by_slot = jnp.concatenate([side[o] for side in sides], axis=1)
        field = dot_nn(by_slot.T.astype(jnp.bfloat16), one_hot_ref[...]).astype(jnp.bfloat16)
        for c in range(2):
            for z in range(4):
                at = c * LANES + z * 32
                out_ref[c, (z - turn) & 3, :, o * HALF : (o + 1) * HALF] = field[at : at + 32]


def unpack(turn, pairs, returned, channels):
    grid_spec = pltpu.PrefetchScalarGridSpec(
        num_scalar_prefetch=1,
        grid=(channels // 2,),
        in_specs=[
            pl.BlockSpec((1, HALF), lambda i, t: (0, 0)),
            pl.BlockSpec((16, 2, 4, 16, LANES), lambda i, t: (0, 0, 0, i, 0)),
        ],
        out_specs=pl.BlockSpec((2, 4, 32, DEGREES), lambda i, t: (i, 0, 0, 0)),
        scratch_shapes=[pltpu.VMEM((HALF, HALF), jnp.bfloat16)] * 2,
    )
    return pl.pallas_call(
        unpack_kernel,
        grid_spec=grid_spec,
        out_shape=jax.ShapeDtypeStruct((channels, 4, 32, DEGREES), jnp.bfloat16),
        compiler_params=pltpu.CompilerParams(vmem_limit_bytes=SMALL_LIMIT),
        cost_estimate=pl.CostEstimate(
            flops=DEGREES * DEGREES * LANES * channels,
            bytes_accessed=4 * LANES * DEGREES * channels,
            transcendentals=0,
        ),
        name="unpack",
    )(turn, pairs, returned)


def exchange(values, axes):
    return lax.all_to_all(values, axes, split_axis=0, concat_axis=0, tiled=True)


def per_device(pred_four, target_four, legendre, pair_order):
    channels = pred_four.shape[0]
    devices = DEGREES // SLOTS
    rows = 4 * channels
    core = lax.axis_index("core")
    device = lax.axis_index(DEVICES)
    turn = ((2 * lax.axis_index("zx") + core) & 3).reshape(1)
    pair_row = pair_order.reshape(1, HALF)
    other_legendre = lax.ppermute(legendre, "core", [(0, 1), (1, 0)])
    own_order = lax.dynamic_slice_in_dim(pair_order, device * PAIRS, PAIRS)
    other_order = lax.dynamic_slice_in_dim(pair_order, (device ^ 4) * PAIRS, PAIRS)
    scalars = jnp.concatenate([own_order, other_order, core.astype(jnp.int32).reshape(1)])

    by_group = (channels, 4, 32, DEGREES)
    packed = pack(turn, pair_row, pred_four.reshape(by_group), target_four.reshape(by_group))
    arrived = exchange(packed.reshape(devices, rows * 4, LANES), DEVICES)
    coeffs, last, moments = analysis(scalars, arrived, legendre, other_legendre, rows)
    spectra = exchange(moments.reshape(devices // 2, 2 * SLOTS, LANES), SAME_CORE)
    factors = exchange(factors_of(spectra, rows), SAME_CORE).reshape(DEGREES, LANES)
    going = synthesis(scalars, coeffs, last, factors, legendre, other_legendre, rows)
    returned = exchange(going.reshape(devices, rows * 2, LANES), DEVICES)
    returned = returned.reshape(16, 2, 4, rows * 2, LANES)
    return unpack(turn, pair_row, returned, channels).reshape(pred_four.shape)


def solution(mesh):
    by_core = Mesh(mesh.devices.reshape(16, 2, 4), DEVICES)
    field = P("col", None, None, ("zx", "core"), None)
    return jax.shard_map(
        per_device,
        mesh=by_core,
        in_specs=(field, field, P(DEVICES, None, None), P()),
        out_specs=field,
        check_vma=False,
    )
```

```python
import functools

import jax
import jax.numpy as jnp
from jax import lax
from jax.experimental import pallas as pl
from jax.experimental.pallas import tpu as pltpu
from jax.sharding import Mesh
from jax.sharding import PartitionSpec as P

DEGREES = 1024
HALF = DEGREES // 2
POWER_FLOOR = 0.5
LANES = 128
SLOTS = 8
PAIRS = 4
DEVICES = ("zx", "core", "col")
SAME_CORE = ("zx", "col")
KERNEL_LIMIT = 36 * 1024 * 1024
SMALL_LIMIT = 16 * 1024 * 1024
TINY_LIMIT = 4 * 1024 * 1024


def dot_nt(left, right):
    return lax.dot_general(left, right, (((1,), (1,)), ((), ())), preferred_element_type=jnp.float32)


def dot_nn(left, right):
    return lax.dot_general(left, right, (((1,), (0,)), ((), ())), preferred_element_type=jnp.float32)


def dot_tn(left, right):
    return lax.dot_general(left, right, (((0,), (0,)), ((), ())), preferred_element_type=jnp.float32)


def by_position(blocks, shift):
    group = lax.broadcasted_iota(jnp.int32, blocks[0].shape, 1) >> 5
    result = blocks[-shift % 4]
    for z in range(1, 4):
        result = jnp.where(group == z, blocks[(z - shift) % 4], result)
    return result


def trade_halves(first, second):
    top = lax.broadcasted_iota(jnp.int32, first.shape, 1) < 4
    return (
        jnp.where(top, first, pltpu.roll(second, 4, 1)),
        jnp.where(top, pltpu.roll(first, 4, 1), second),
    )


def one_hots(pairs_ref, lower_ref, upper_ref):
    order = jnp.broadcast_to(pairs_ref[...].astype(jnp.float32), (LANES, HALF)).T
    by_core = order.reshape(16, 2, 2, 8, LANES)
    first, second = by_core[:, 0].reshape(32, 8, LANES), by_core[:, 1].reshape(32, 8, LANES)
    order = jnp.stack(trade_halves(first, second), axis=1).reshape(HALF, LANES)
    order = jnp.concatenate([order] * (HALF // LANES), axis=1).astype(jnp.int32)
    lane = lax.broadcasted_iota(jnp.int32, (HALF, HALF), 1)
    lower_ref[...] = jnp.where(lane == order, 1.0, 0.0).astype(jnp.bfloat16)
    upper_ref[...] = jnp.where(lane == HALF - 1 - order, 1.0, 0.0).astype(jnp.bfloat16)


def pack_kernel(
    channels, turn_ref, pairs_hbm, pred_hbm, target_hbm, out_hbm,
    pairs_ref, field_ref, out_ref, lower_ref, upper_ref, pair_sem, in_sems, out_sems,
):
    steps = channels // 2
    ahead = 2

    def fetch(i, f):
        source = (pred_hbm, target_hbm)[f].at[pl.ds(2 * i, 2)]
        return pltpu.make_async_copy(source, field_ref.at[f, pl.ds(2 * i, 2)], in_sems.at[f, i])

    def send(i):
        return pltpu.make_async_copy(
            out_ref.at[i], out_hbm.at[:, :, :, pl.ds(2 * i, 2)], out_sems.at[i]
        )

    pair_copy = pltpu.make_async_copy(pairs_hbm, pairs_ref, pair_sem)
    pair_copy.start()
    for i in range(ahead):
        for f in range(2):
            fetch(i, f).start()
    pair_copy.wait()
    one_hots(pairs_ref, lower_ref, upper_ref)

    turn = turn_ref[0]

    def step(i, carry):
        @pl.when(i + ahead < steps)
        def _():
            for f in range(2):
                fetch(i + ahead, f).start()

        for f in range(2):
            fetch(i, f).wait()
        for c in range(2):
            pieces = []
            for sample in range(2):
                for z in range(4):
                    group = (z - turn) & 3
                    pieces.append(field_ref[group >> 1, 2 * i + c, 2 * sample + (group & 1)])
            field = jnp.concatenate(pieces, axis=0)
            low = dot_nt(lower_ref[...], field[:, :HALF]).reshape(HALF // 8, 8, 2 * LANES)
            high = dot_nt(upper_ref[...], field[:, HALF:]).reshape(HALF // 8, 8, 2 * LANES)
            both = jnp.concatenate([low, high], axis=1).astype(jnp.bfloat16)
            for sample in range(2):
                block = both[:, :, sample * LANES : (sample + 1) * LANES]
                out_ref[i, :, sample, :, c] = block.reshape(16, 4, 16, LANES)
        send(i).start()
        return carry

    lax.fori_loop(0, steps, step, 0)
    for i in range(steps):
        send(i).wait()


def pack(turn, pairs, pred, target):
    channels = pred.shape[0]
    steps = channels // 2
    far = pl.BlockSpec(memory_space=pltpu.HBM)
    return pl.pallas_call(
        functools.partial(pack_kernel, channels),
        in_specs=[pl.BlockSpec(memory_space=pltpu.SMEM), far, far, far],
        out_specs=far,
        out_shape=pltpu.HBM((16, 2, 4, channels, 16, LANES), jnp.bfloat16),
        scratch_shapes=[
            pltpu.VMEM((1, HALF), jnp.int32),
            pltpu.VMEM((2, channels, 4, 32, DEGREES), jnp.bfloat16),
            pltpu.VMEM((steps, 16, 2, 4, 2, 16, LANES), jnp.bfloat16),
            pltpu.VMEM((HALF, HALF), jnp.bfloat16),
            pltpu.VMEM((HALF, HALF), jnp.bfloat16),
            pltpu.SemaphoreType.DMA,
            pltpu.SemaphoreType.DMA((2, steps)),
            pltpu.SemaphoreType.DMA((steps,)),
        ],
        compiler_params=pltpu.CompilerParams(vmem_limit_bytes=KERNEL_LIMIT),
        cost_estimate=pl.CostEstimate(
            flops=DEGREES * DEGREES * 2 * LANES * channels,
            bytes_accessed=8 * LANES * DEGREES * channels,
            transcendentals=0,
        ),
        name="pack",
    )(turn, in_hbm(pairs), in_hbm(pred), in_hbm(target))


def moments_of(values, rows):
    shaped = values.reshape(2, 2, rows, values.shape[-1])
    pieces = []
    for left, right in ((0, 0), (1, 1), (0, 1)):
        real = shaped[left, 0] * shaped[right, 0]
        imag = shaped[left, 1] * shaped[right, 1]
        pieces.append(real + imag)
    return jnp.concatenate(pieces, axis=0)


def leg_stream(own_hbm, other_hbm, leg_ref, sems):
    def start(p):
        for hbm, here in ((own_hbm, p < PAIRS), (other_hbm, p >= PAIRS)):

            @pl.when(here)
            def _(hbm=hbm):
                at = p & 3
                pltpu.make_async_copy(hbm.at[at], leg_ref.at[at], sems.at[at]).start()

    def wait(p):
        at = p & 3
        pltpu.make_async_copy(own_hbm.at[at], leg_ref.at[at], sems.at[at]).wait()

    return start, wait


def analysis_kernel(
    rows, scalar_ref, arrived_ref, edge_ref, own_hbm, other_hbm, coef_ref, last_ref, moment_ref,
    narrow_ref, leg_ref, sort_ref, turned_edge_ref, field_ref, lower_ref, upper_ref, tail_ref, sems, leg_sems,
):
    size = 3 * rows
    span = arrived_ref.shape[2]
    slots = 2 * SLOTS

    def chunk(k):
        at = pl.ds(4 * k, 4)
        return pltpu.make_async_copy(arrived_ref.at[at], narrow_ref.at[at], sems.at[k])

    start_leg, wait_leg = leg_stream(own_hbm, other_hbm, leg_ref, leg_sems)
    for k in range(8):
        chunk(k).start()
    lower_ref[...] = jnp.zeros_like(lower_ref)
    upper_ref[...] = jnp.zeros_like(upper_ref)
    tail_ref[...] = jnp.zeros_like(tail_ref)
    edges = jnp.concatenate([edge_ref[...], jnp.zeros((LANES - SLOTS, DEGREES), jnp.float32)], axis=0)
    turned_edge_ref[...] = edges.T.astype(jnp.bfloat16)
    row = lax.broadcasted_iota(jnp.int32, (LANES, LANES), 0)
    column = lax.broadcasted_iota(jnp.int32, (LANES, LANES), 1)
    takes = column == (row & (SLOTS - 1)) * slots + (row >> 3)
    sort_ref[...] = jnp.where(takes, 1.0, 0.0).astype(jnp.bfloat16)

    def build(k, carry):
        chunk(k).wait()

        @pl.when((k == 1) | (k == 3) | (k == 5))
        def _():
            start_leg(k >> 1)

        at = pl.multiple_of(k * LANES, LANES)
        for f in range(2):
            tiles = []
            for col in range(4):
                both = []
                for q in range(2):
                    g = 2 * f + q
                    block = by_position([narrow_ref[4 * k + i, col] for i in range(4)], g)
                    if g > 0:
                        block = pltpu.roll(block, LANES - 32 * g, 1)
                    both.append(block)
                both = jnp.concatenate(both, axis=1)
                tiles += [both[c * slots : (c + 1) * slots] for c in range(span // slots)]
            sorted_rows = []
            for u in range(rows // SLOTS):
                group = jnp.concatenate(tiles[u * SLOTS : (u + 1) * SLOTS], axis=0)
                sorted_rows.append(dot_nn(sort_ref[...], group))
            for slot in range(slots):
                parts = [
                    block[slot * SLOTS : (slot + 1) * SLOTS, q * LANES : (q + 1) * LANES]
                    for q in range(2)
                    for block in sorted_rows
                ]
                low = 4 * rows * (slot // SLOTS) + 2 * f * rows
                field_ref[slot % SLOTS, low : low + 2 * rows, pl.ds(at, LANES)] = jnp.concatenate(
                    parts, axis=0
                ).astype(jnp.bfloat16)
        return carry

    lax.fori_loop(0, 8, build, 0)
    core = scalar_ref[2 * PAIRS]

    def one_pair(p, carry):
        @pl.when(p + 3 < 2 * PAIRS)
        def _():
            start_leg(p + 3)

        wait_leg(p)
        ring = p & 3
        slot = p ^ (core * PAIRS)
        lower_order = scalar_ref[p]
        boundary = DEGREES - lower_order
        width = 256
        lower_weight = jnp.where(lower_order == 0, 1.0, 2.0)
        tiles_up = lower_order >> 7
        lanes_up = lower_order & (LANES - 1)
        lane = lax.broadcasted_iota(jnp.int32, (size, LANES), 1)
        late = (lower_order <= width).astype(jnp.int32)
        at = pl.multiple_of(HALF + width * late, width)
        low = pl.multiple_of(4 * rows * (1 - late), 4 * rows)
        extra = dot_nn(field_ref[slot, pl.ds(low, 4 * rows)], leg_ref[ring, :, pl.ds(at, width)])
        before = jnp.zeros((size, LANES), jnp.float32)
        for tile in range(DEGREES // width):
            start = tile * width
            low = 4 * rows * (tile // 3)
            values = dot_nn(field_ref[slot, low : low + 4 * rows], leg_ref[ring, :, start : start + width])
            if start >= HALF:
                row = lax.broadcasted_iota(jnp.int32, values.shape, 1) + start
                first, second = (values, extra) if tile == 2 else (extra, values)
                values = jnp.where(row < boundary, first, second)
            coef_ref[p, :, start : start + width] = values
            for sub in range(width // LANES):
                moments = moments_of(values[:, sub * LANES : (sub + 1) * LANES], rows)
                now = start + sub * LANES
                if start >= HALF:
                    upper_ref[:, now - HALF : now - HALF + LANES] += jnp.where(
                        lane + now < boundary, 0.0, moments
                    )
                turned = pltpu.roll(moments, lanes_up, 1)
                at = pl.multiple_of(now + tiles_up * LANES, LANES)
                lower_ref[:, pl.ds(at, LANES)] += lower_weight * jnp.where(
                    lane < lanes_up, before, turned
                )
                before = turned
        last = dot_nn(field_ref[slot, 4 * rows :], turned_edge_ref[...])
        last_ref[p] = last
        tail_ref[...] += jnp.where(lane == p, moments_of(last, rows), 0.0)
        return carry

    lax.fori_loop(0, 2 * PAIRS, one_pair, 0)

    lane = lax.broadcasted_iota(jnp.int32, (size, LANES), 1)
    after = jnp.broadcast_to(jnp.sum(tail_ref[...], axis=1, keepdims=True), (size, LANES))
    for tile in reversed(range(8)):
        total = lower_ref[:, tile * LANES : (tile + 1) * LANES]
        if tile >= 4:
            turned = pltpu.roll(upper_ref[:, (tile - 4) * LANES : (tile - 3) * LANES], LANES - 1, 1)
            total = total + 2.0 * jnp.where(lane == LANES - 1, after, turned)
            after = turned
        total = jnp.concatenate([total, jnp.zeros((LANES - size, LANES), jnp.float32)], axis=0)
        moment_ref[tile * LANES : (tile + 1) * LANES, :] = total.T


def in_vmem(value):
    return pltpu.with_memory_space_constraint(value, pltpu.VMEM)


def in_hbm(value):
    return pltpu.with_memory_space_constraint(value, pltpu.HBM)


def turn_kernel(leg_ref, out_ref):
    out_ref[0] = leg_ref[0].T


def turned(legendre):
    pairs, _, size = legendre.shape
    width = 256
    return pl.pallas_call(
        turn_kernel,
        grid=(pairs, DEGREES // width),
        in_specs=[pl.BlockSpec((1, width, size), lambda p, i: (p, i, 0))],
        out_specs=pl.BlockSpec((1, size, width), lambda p, i: (p, 0, i)),
        out_shape=pltpu.HBM((pairs, size, DEGREES), legendre.dtype),
        compiler_params=pltpu.CompilerParams(vmem_limit_bytes=SMALL_LIMIT),
        cost_estimate=pl.CostEstimate(flops=0, bytes_accessed=4 * legendre.size, transcendentals=0),
        name="turned",
    )(in_hbm(legendre))


def analysis(scalars, arrived, edges, own, other, rows):
    span = rows * 4
    arrived = arrived.reshape(32, 4, span, LANES)
    whole = pl.BlockSpec(memory_space=pltpu.VMEM)
    far = pl.BlockSpec(memory_space=pltpu.HBM)
    return pl.pallas_call(
        functools.partial(analysis_kernel, rows),
        in_specs=[pl.BlockSpec(memory_space=pltpu.SMEM), far, whole, far, far],
        out_specs=[whole, whole, whole],
        out_shape=[
            pltpu.VMEM((2 * PAIRS, 4 * rows, DEGREES), jnp.float32),
            pltpu.VMEM((2 * PAIRS, 4 * rows, LANES), jnp.float32),
            pltpu.VMEM((DEGREES, LANES), jnp.float32),
        ],
        scratch_shapes=[
            pltpu.VMEM((32, 4, span, LANES), jnp.bfloat16),
            pltpu.VMEM((4, DEGREES, DEGREES), jnp.bfloat16),
            pltpu.VMEM((LANES, LANES), jnp.bfloat16),
            pltpu.VMEM((DEGREES, LANES), jnp.bfloat16),
            pltpu.VMEM((SLOTS, 8 * rows, DEGREES), jnp.bfloat16),
            pltpu.VMEM((3 * rows, DEGREES + HALF), jnp.float32),
            pltpu.VMEM((3 * rows, HALF), jnp.float32),
            pltpu.VMEM((3 * rows, LANES), jnp.float32),
            pltpu.SemaphoreType.DMA((8,)),
            pltpu.SemaphoreType.DMA((4,)),
        ],
        compiler_params=pltpu.CompilerParams(vmem_limit_bytes=KERNEL_LIMIT),
        cost_estimate=pl.CostEstimate(
            flops=20 * rows * PAIRS * DEGREES * DEGREES,
            bytes_accessed=4 * own.size + 16 * rows * PAIRS * DEGREES + 2 * arrived.size,
            transcendentals=0,
        ),
        name="analysis",
    )(scalars, in_hbm(arrived), edges, in_hbm(own), in_hbm(other))


def factor_kernel(span, parts_ref, out_ref):
    total = jnp.sum(parts_ref[...], axis=0)
    size = total.shape[1]
    power_pred = total
    power_true = pltpu.roll(total, size - span, 1)
    cross = pltpu.roll(total, size - 2 * span, 1)
    pred = jnp.maximum(power_pred, POWER_FLOOR)
    true = jnp.maximum(power_true, POWER_FLOOR)
    root_pred = jnp.sqrt(pred)
    root_true = jnp.sqrt(true)
    both = pred + true
    upper_mean = (pred * pred + true * true) / both
    inverse = 1.0 / (root_pred * root_true)
    coherence = cross * inverse
    mean_slope = (2.0 * pred - upper_mean) / both
    slope = (
        (root_pred - root_true) / root_pred
        + 2.0 * mean_slope * (1.0 - coherence)
        + upper_mean * coherence / pred
    )
    binds = jnp.where(power_pred > POWER_FLOOR, 1.0, jnp.where(power_pred == POWER_FLOOR, 0.5, 0.0))
    dpower = 2.0 * slope * binds
    dcross = -2.0 * upper_mean * inverse
    lane = lax.broadcasted_iota(jnp.int32, total.shape, 1)
    factors = jnp.where(lane < span, dpower, pltpu.roll(dcross, span, 1))
    out_ref[...] = jnp.broadcast_to(factors[None], out_ref.shape)


def factors_of(parts, rows):
    whole = pl.BlockSpec(memory_space=pltpu.VMEM)
    return pl.pallas_call(
        functools.partial(factor_kernel, rows),
        in_specs=[whole],
        out_specs=whole,
        out_shape=pltpu.VMEM(parts.shape, jnp.float32),
        compiler_params=pltpu.CompilerParams(vmem_limit_bytes=TINY_LIMIT),
        cost_estimate=pl.CostEstimate(flops=parts.size, bytes_accessed=8 * parts.size, transcendentals=0),
        name="factors",
    )(in_vmem(parts))


def synthesis_kernel(
    rows, scalar_ref, coef_ref, last_ref, factor_ref, own_ref, other_ref, out_ref,
    spread_ref, upspread_ref, early_ref, late_ref, wide_ref,
):
    size = 2 * rows
    lane = lax.broadcasted_iota(jnp.int32, (size, LANES), 1)
    before = None
    for tile in range(8):
        turned = factor_ref[tile * LANES : (tile + 1) * LANES, :].T[:size]
        spread_ref[:, tile * LANES : (tile + 1) * LANES] = turned
        shifted = pltpu.roll(turned, 1, 1)
        if tile >= 4:
            upspread_ref[:, (tile - 4) * LANES : (tile - 3) * LANES] = 2.0 * jnp.where(
                lane == 0, before, shifted
            )
        before = shifted
    core = scalar_ref[2 * PAIRS]

    def one_pair(leg_ref, first, ring, carry):
        p = first + ring
        slot = p ^ (core * PAIRS)
        lower_order = scalar_ref[p]
        boundary = DEGREES - lower_order
        lower_weight = jnp.where(lower_order == 0, 1.0, 2.0)
        tiles_up = lower_order >> 7
        lanes_up = lower_order & (LANES - 1)
        back = (LANES - lanes_up) & (LANES - 1)

        def turned_tile(tile):
            at = pl.multiple_of((tile + tiles_up) * LANES, LANES)
            return pltpu.roll(spread_ref[:, pl.ds(at, LANES)], back, 1)

        def graded(factors, observe):
            grads = []
            for q in range(2):
                predicted = observe(q * rows)
                observed = observe((2 + q) * rows)
                grads.append(factors[:rows] * predicted + factors[rows:] * observed)
            return jnp.concatenate(grads, axis=0)

        now = turned_tile(0)
        for tile in range(8):
            start = tile * LANES
            then = turned_tile(tile + 1)
            factors = lower_weight * jnp.where(lane < LANES - lanes_up, now, then)
            now = then
            row = lane + start
            if tile >= 4:
                factors = jnp.where(
                    row < boundary, factors, upspread_ref[:, start - HALF : start - HALF + LANES]
                )
            grad = graded(factors, lambda at: coef_ref[p, at : at + rows, start : start + LANES])
            if tile >= 4:
                at = start - HALF
                late_ref[:size, at : at + LANES] = jnp.where(row < boundary, grad, 0.0).astype(
                    jnp.bfloat16
                )
                late_ref[size:, at : at + LANES] = jnp.where(row < boundary, 0.0, grad).astype(
                    jnp.bfloat16
                )
            else:
                early_ref[:, start : start + LANES] = grad.astype(jnp.bfloat16)
        last_factors = jnp.broadcast_to(2.0 * spread_ref[:, DEGREES - 1 : DEGREES], (size, LANES))
        edge_lane = lax.broadcasted_iota(jnp.int32, (4 * rows, LANES), 1)
        last = jnp.sum(jnp.where(edge_lane == p, last_ref[p], 0.0), axis=1, keepdims=True)
        last = jnp.broadcast_to(last, (4 * rows, LANES))
        last_grad = graded(last_factors, lambda at: last[at : at + rows])
        last_grad = last_grad.astype(jnp.bfloat16).astype(jnp.float32)
        last_leg = leg_ref[ring, DEGREES : DEGREES + 1, :].astype(jnp.float32)

        width = 256
        for tile in range(DEGREES // width):
            start = tile * width
            early = dot_nn(early_ref[...], leg_ref[ring, :HALF, start : start + width])
            late = dot_nn(late_ref[...], leg_ref[ring, HALF:DEGREES, start : start + width])
            lower, upper = early + late[:size], late[size:]
            for sub in range(width // LANES):
                at = start + sub * LANES
                inside = slice(sub * LANES, (sub + 1) * LANES)
                top = lower[:, inside]
                bottom = upper[:, inside] + last_grad * last_leg[:, at : at + LANES]
                blocks = [top[:rows], top[rows:], bottom[:rows], bottom[rows:]]
                blocks = [
                    block if g == 0 else pltpu.roll(block, 32 * g, 1) for g, block in enumerate(blocks)
                ]
                for i in range(4):
                    wide_ref[at // 32 + i, pl.ds(slot, rows, stride=SLOTS), :] = by_position(blocks, i)
        return carry

    lax.fori_loop(0, PAIRS, functools.partial(one_pair, own_ref, 0), 0, unroll=2)
    lax.fori_loop(0, PAIRS, functools.partial(one_pair, other_ref, PAIRS), 0, unroll=2)

    def narrow(j, carry):
        out_ref[j] = wide_ref[j].astype(jnp.bfloat16)
        return carry

    lax.fori_loop(0, 32, narrow, 0, unroll=8)


def synthesis(scalars, coeffs, last, factors, own, other, rows):
    whole = pl.BlockSpec(memory_space=pltpu.VMEM)
    return pl.pallas_call(
        functools.partial(synthesis_kernel, rows),
        in_specs=[pl.BlockSpec(memory_space=pltpu.SMEM)] + [whole] * 5,
        out_specs=whole,
        out_shape=pltpu.VMEM((32, rows * SLOTS, LANES), jnp.bfloat16),
        scratch_shapes=[
            pltpu.VMEM((2 * rows, DEGREES + HALF), jnp.float32),
            pltpu.VMEM((2 * rows, HALF), jnp.float32),
            pltpu.VMEM((2 * rows, HALF), jnp.bfloat16),
            pltpu.VMEM((4 * rows, HALF), jnp.bfloat16),
            pltpu.VMEM((32, rows * SLOTS, LANES), jnp.float32),
        ],
        compiler_params=pltpu.CompilerParams(vmem_limit_bytes=SMALL_LIMIT),
        cost_estimate=pl.CostEstimate(
            flops=12 * rows * PAIRS * DEGREES * DEGREES,
            bytes_accessed=4 * own.size + 16 * rows * PAIRS * DEGREES + 64 * rows * SLOTS * LANES,
            transcendentals=0,
        ),
        name="synthesis",
    )(scalars, *(in_vmem(value) for value in (coeffs, last, factors, own, other)))


def unpack_kernel(turn_ref, pairs_ref, returned_ref, out_ref, lower_ref, upper_ref):
    @pl.when(pl.program_id(0) == 0)
    def _():
        one_hots(pairs_ref, lower_ref, upper_ref)

    turn = turn_ref[0]
    both = returned_ref[...].astype(jnp.float32)
    sides = []
    for c in range(2):
        first, second = (
            both[:, sample, :, c * SLOTS : (c + 1) * SLOTS].reshape(HALF, LANES) for sample in range(2)
        )
        group = lax.broadcasted_iota(jnp.int32, first.shape, 1) >> 5
        keep = ((group - turn) & 3) < 2
        sides.append(
            (
                jnp.where(keep, first, pltpu.roll(second, 64, 1)),
                jnp.where(keep, pltpu.roll(first, 64, 1), second),
            )
        )
    for o, one_hot_ref in enumerate((lower_ref, upper_ref)):
        by_slot = jnp.concatenate([side[o] for side in sides], axis=1)
        field = dot_tn(by_slot.astype(jnp.bfloat16), one_hot_ref[...]).astype(jnp.bfloat16)
        for c in range(2):
            for z in range(4):
                at = c * LANES + z * 32
                out_ref[c, (z - turn) & 3, :, o * HALF : (o + 1) * HALF] = field[at : at + 32]


def unpack(turn, pairs, returned, channels):
    grid_spec = pltpu.PrefetchScalarGridSpec(
        num_scalar_prefetch=1,
        grid=(channels // 2,),
        in_specs=[
            pl.BlockSpec((1, HALF), lambda i, t: (0, 0)),
            pl.BlockSpec((16, 2, 4, 16, LANES), lambda i, t: (0, 0, 0, i, 0)),
        ],
        out_specs=pl.BlockSpec((2, 4, 32, DEGREES), lambda i, t: (i, 0, 0, 0)),
        scratch_shapes=[pltpu.VMEM((HALF, HALF), jnp.bfloat16)] * 2,
    )
    return pl.pallas_call(
        unpack_kernel,
        grid_spec=grid_spec,
        out_shape=jax.ShapeDtypeStruct((channels, 4, 32, DEGREES), jnp.bfloat16),
        compiler_params=pltpu.CompilerParams(vmem_limit_bytes=SMALL_LIMIT),
        cost_estimate=pl.CostEstimate(
            flops=DEGREES * DEGREES * LANES * channels,
            bytes_accessed=4 * LANES * DEGREES * channels,
            transcendentals=0,
        ),
        name="unpack",
    )(turn, pairs, returned)


def exchange(values, axes):
    return lax.all_to_all(values, axes, split_axis=0, concat_axis=0, tiled=True)


def per_device(pred_four, target_four, legendre, pair_order):
    channels = pred_four.shape[0]
    devices = DEGREES // SLOTS
    rows = 4 * channels
    core = lax.axis_index("core")
    device = lax.axis_index(DEVICES)
    turn = ((2 * lax.axis_index("zx") + core) & 3).reshape(1)
    pair_row = pair_order.reshape(1, HALF)
    other_legendre = lax.ppermute(legendre, "core", [(0, 1), (1, 0)])
    own_order = lax.dynamic_slice_in_dim(pair_order, device * PAIRS, PAIRS)
    other_order = lax.dynamic_slice_in_dim(pair_order, (device ^ 4) * PAIRS, PAIRS)
    scalars = jnp.concatenate([own_order, other_order, core.astype(jnp.int32).reshape(1)])

    by_group = (channels, 4, 32, DEGREES)
    packed = pack(turn, pair_row, pred_four.reshape(by_group), target_four.reshape(by_group))
    arrived = exchange(packed.reshape(devices, rows * 4, LANES), DEVICES)
    edges = jnp.concatenate([legendre[:, DEGREES], other_legendre[:, DEGREES]]).astype(jnp.float32)
    coeffs, last, moments = analysis(
        scalars, arrived, edges, turned(legendre), turned(other_legendre), rows
    )
    spectra = exchange(moments.reshape(devices // 2, 2 * SLOTS, LANES), SAME_CORE)
    factors = exchange(factors_of(spectra, rows), SAME_CORE).reshape(DEGREES, LANES)
    going = synthesis(scalars, coeffs, last, factors, legendre, other_legendre, rows)
    returned = exchange(going.reshape(devices, rows * 2, LANES), DEVICES)
    returned = returned.reshape(16, 2, 4, rows * 2, LANES)
    return unpack(turn, pair_row, returned, channels).reshape(pred_four.shape)


def solution(mesh):
    by_core = Mesh(mesh.devices.reshape(16, 2, 4), DEVICES)
    field = P("col", None, None, ("zx", "core"), None)
    return jax.shard_map(
        per_device,
        mesh=by_core,
        in_specs=(field, field, P(DEVICES, None, None), P()),
        out_specs=field,
        check_vma=False,
    )
```

```python
import functools

import jax
import jax.numpy as jnp
from jax import lax
from jax.experimental import pallas as pl
from jax.experimental.pallas import tpu as pltpu
from jax.sharding import Mesh
from jax.sharding import PartitionSpec as P

DEGREES = 1024
HALF = DEGREES // 2
POWER_FLOOR = 0.5
LANES = 128
SLOTS = 8
PAIRS = 4
DEVICES = ("zx", "core", "col")
SAME_CORE = ("zx", "col")
KERNEL_LIMIT = 36 * 1024 * 1024
SMALL_LIMIT = 16 * 1024 * 1024
TINY_LIMIT = 4 * 1024 * 1024


def dot_nt(left, right):
    return lax.dot_general(left, right, (((1,), (1,)), ((), ())), preferred_element_type=jnp.float32)


def dot_nn(left, right):
    return lax.dot_general(left, right, (((1,), (0,)), ((), ())), preferred_element_type=jnp.float32)


def dot_tn(left, right):
    return lax.dot_general(left, right, (((0,), (0,)), ((), ())), preferred_element_type=jnp.float32)


def by_position(blocks, shift):
    group = lax.broadcasted_iota(jnp.int32, blocks[0].shape, 1) >> 5
    result = blocks[-shift % 4]
    for z in range(1, 4):
        result = jnp.where(group == z, blocks[(z - shift) % 4], result)
    return result


def trade_halves(first, second):
    top = lax.broadcasted_iota(jnp.int32, first.shape, 1) < 4
    return (
        jnp.where(top, first, pltpu.roll(second, 4, 1)),
        jnp.where(top, pltpu.roll(first, 4, 1), second),
    )


def one_hots(pairs_ref, lower_ref, upper_ref):
    order = jnp.broadcast_to(pairs_ref[...].astype(jnp.float32), (LANES, HALF)).T
    by_core = order.reshape(16, 2, 2, 8, LANES)
    first, second = by_core[:, 0].reshape(32, 8, LANES), by_core[:, 1].reshape(32, 8, LANES)
    order = jnp.stack(trade_halves(first, second), axis=1).reshape(HALF, LANES)
    order = jnp.concatenate([order] * (HALF // LANES), axis=1).astype(jnp.int32)
    lane = lax.broadcasted_iota(jnp.int32, (HALF, HALF), 1)
    lower_ref[...] = jnp.where(lane == order, 1.0, 0.0).astype(jnp.bfloat16)
    upper_ref[...] = jnp.where(lane == HALF - 1 - order, 1.0, 0.0).astype(jnp.bfloat16)


def pack_kernel(
    channels, turn_ref, pairs_hbm, pred_hbm, target_hbm, out_hbm,
    pairs_ref, field_ref, out_ref, lower_ref, upper_ref, pair_sem, in_sems, out_sems,
):
    steps = channels // 2
    ahead = 2

    def fetch(i, f):
        source = (pred_hbm, target_hbm)[f].at[pl.ds(2 * i, 2)]
        return pltpu.make_async_copy(source, field_ref.at[f, pl.ds(2 * i, 2)], in_sems.at[f, i])

    def send(i):
        return pltpu.make_async_copy(
            out_ref.at[i], out_hbm.at[:, :, :, pl.ds(2 * i, 2)], out_sems.at[i]
        )

    pair_copy = pltpu.make_async_copy(pairs_hbm, pairs_ref, pair_sem)
    pair_copy.start()
    for i in range(ahead):
        for f in range(2):
            fetch(i, f).start()
    pair_copy.wait()
    one_hots(pairs_ref, lower_ref, upper_ref)

    turn = turn_ref[0]

    def step(i, carry):
        @pl.when(i + ahead < steps)
        def _():
            for f in range(2):
                fetch(i + ahead, f).start()

        for f in range(2):
            fetch(i, f).wait()
        for c in range(2):
            pieces = []
            for sample in range(2):
                for z in range(4):
                    group = (z - turn) & 3
                    pieces.append(field_ref[group >> 1, 2 * i + c, 2 * sample + (group & 1)])
            field = jnp.concatenate(pieces, axis=0)
            low = dot_nt(lower_ref[...], field[:, :HALF]).reshape(HALF // 8, 8, 2 * LANES)
            high = dot_nt(upper_ref[...], field[:, HALF:]).reshape(HALF // 8, 8, 2 * LANES)
            both = jnp.concatenate([low, high], axis=1).astype(jnp.bfloat16)
            for sample in range(2):
                block = both[:, :, sample * LANES : (sample + 1) * LANES]
                out_ref[i, :, sample, :, c] = block.reshape(16, 4, 16, LANES)
        send(i).start()
        return carry

    lax.fori_loop(0, steps, step, 0, unroll=True)
    for i in range(steps):
        send(i).wait()


def pack(turn, pairs, pred, target):
    channels = pred.shape[0]
    steps = channels // 2
    far = pl.BlockSpec(memory_space=pltpu.HBM)
    return pl.pallas_call(
        functools.partial(pack_kernel, channels),
        in_specs=[pl.BlockSpec(memory_space=pltpu.SMEM), far, far, far],
        out_specs=far,
        out_shape=pltpu.HBM((16, 2, 4, channels, 16, LANES), jnp.bfloat16),
        scratch_shapes=[
            pltpu.VMEM((1, HALF), jnp.int32),
            pltpu.VMEM((2, channels, 4, 32, DEGREES), jnp.bfloat16),
            pltpu.VMEM((steps, 16, 2, 4, 2, 16, LANES), jnp.bfloat16),
            pltpu.VMEM((HALF, HALF), jnp.bfloat16),
            pltpu.VMEM((HALF, HALF), jnp.bfloat16),
            pltpu.SemaphoreType.DMA,
            pltpu.SemaphoreType.DMA((2, steps)),
            pltpu.SemaphoreType.DMA((steps,)),
        ],
        compiler_params=pltpu.CompilerParams(vmem_limit_bytes=KERNEL_LIMIT),
        cost_estimate=pl.CostEstimate(
            flops=DEGREES * DEGREES * 2 * LANES * channels,
            bytes_accessed=8 * LANES * DEGREES * channels,
            transcendentals=0,
        ),
        name="pack",
    )(turn, in_hbm(pairs), in_hbm(pred), in_hbm(target))


def moments_of(values, rows):
    shaped = values.reshape(2, 2, rows, values.shape[-1])
    pieces = []
    for left, right in ((0, 0), (1, 1), (0, 1)):
        real = shaped[left, 0] * shaped[right, 0]
        imag = shaped[left, 1] * shaped[right, 1]
        pieces.append(real + imag)
    return jnp.concatenate(pieces, axis=0)


def leg_stream(own_hbm, other_hbm, leg_ref, sems):
    def start(p):
        for hbm, here in ((own_hbm, p < PAIRS), (other_hbm, p >= PAIRS)):

            @pl.when(here)
            def _(hbm=hbm):
                at = p & 3
                pltpu.make_async_copy(hbm.at[at], leg_ref.at[at], sems.at[at]).start()

    def wait(p):
        at = p & 3
        pltpu.make_async_copy(own_hbm.at[at], leg_ref.at[at], sems.at[at]).wait()

    return start, wait


def analysis_kernel(
    rows, scalar_ref, arrived_ref, edge_ref, own_hbm, other_hbm, coef_ref, last_ref, moment_ref,
    narrow_ref, leg_ref, sort_ref, turned_edge_ref, field_ref, lower_ref, upper_ref, tail_ref, sems, leg_sems,
):
    size = 3 * rows
    span = arrived_ref.shape[2]
    slots = 2 * SLOTS

    def chunk(k):
        at = pl.ds(4 * k, 4)
        return pltpu.make_async_copy(arrived_ref.at[at], narrow_ref.at[at], sems.at[k])

    start_leg, wait_leg = leg_stream(own_hbm, other_hbm, leg_ref, leg_sems)
    for k in range(8):
        chunk(k).start()
    lower_ref[...] = jnp.zeros_like(lower_ref)
    upper_ref[...] = jnp.zeros_like(upper_ref)
    tail_ref[...] = jnp.zeros_like(tail_ref)
    edges = jnp.concatenate([edge_ref[...], jnp.zeros((LANES - SLOTS, DEGREES), jnp.float32)], axis=0)
    turned_edge_ref[...] = edges.T.astype(jnp.bfloat16)
    row = lax.broadcasted_iota(jnp.int32, (LANES, LANES), 0)
    column = lax.broadcasted_iota(jnp.int32, (LANES, LANES), 1)
    takes = column == (row & (SLOTS - 1)) * slots + (row >> 3)
    sort_ref[...] = jnp.where(takes, 1.0, 0.0).astype(jnp.bfloat16)

    def build(k, carry):
        chunk(k).wait()

        @pl.when((k == 1) | (k == 3) | (k == 5))
        def _():
            start_leg(k >> 1)

        at = pl.multiple_of(k * LANES, LANES)
        for f in range(2):
            tiles = []
            for col in range(4):
                both = []
                for q in range(2):
                    g = 2 * f + q
                    block = by_position([narrow_ref[4 * k + i, col] for i in range(4)], g)
                    if g > 0:
                        block = pltpu.roll(block, LANES - 32 * g, 1)
                    both.append(block)
                both = jnp.concatenate(both, axis=1)
                tiles += [both[c * slots : (c + 1) * slots] for c in range(span // slots)]
            sorted_rows = []
            for u in range(rows // SLOTS):
                group = jnp.concatenate(tiles[u * SLOTS : (u + 1) * SLOTS], axis=0)
                sorted_rows.append(dot_nn(sort_ref[...], group))
            for slot in range(slots):
                parts = [
                    block[slot * SLOTS : (slot + 1) * SLOTS, q * LANES : (q + 1) * LANES]
                    for q in range(2)
                    for block in sorted_rows
                ]
                low = 4 * rows * (slot // SLOTS) + 2 * f * rows
                field_ref[slot % SLOTS, low : low + 2 * rows, pl.ds(at, LANES)] = jnp.concatenate(
                    parts, axis=0
                ).astype(jnp.bfloat16)
        return carry

    lax.fori_loop(0, 8, build, 0)
    core = scalar_ref[2 * PAIRS]

    def one_pair(p, carry):
        @pl.when(p + 3 < 2 * PAIRS)
        def _():
            start_leg(p + 3)

        wait_leg(p)
        ring = p & 3
        slot = p ^ (core * PAIRS)
        lower_order = scalar_ref[p]
        boundary = DEGREES - lower_order
        width = 256
        lower_weight = jnp.where(lower_order == 0, 1.0, 2.0)
        tiles_up = lower_order >> 7
        lanes_up = lower_order & (LANES - 1)
        lane = lax.broadcasted_iota(jnp.int32, (size, LANES), 1)
        late = (lower_order <= width).astype(jnp.int32)
        at = pl.multiple_of(HALF + width * late, width)
        low = pl.multiple_of(4 * rows * (1 - late), 4 * rows)
        extra = dot_nn(field_ref[slot, pl.ds(low, 4 * rows)], leg_ref[ring, :, pl.ds(at, width)])
        before = jnp.zeros((size, LANES), jnp.float32)
        for tile in range(DEGREES // width):
            start = tile * width
            low = 4 * rows * (tile // 3)
            values = dot_nn(field_ref[slot, low : low + 4 * rows], leg_ref[ring, :, start : start + width])
            if start >= HALF:
                row = lax.broadcasted_iota(jnp.int32, values.shape, 1) + start
                first, second = (values, extra) if tile == 2 else (extra, values)
                values = jnp.where(row < boundary, first, second)
            coef_ref[p, :, start : start + width] = values
            for sub in range(width // LANES):
                moments = moments_of(values[:, sub * LANES : (sub + 1) * LANES], rows)
                now = start + sub * LANES
                if start >= HALF:
                    upper_ref[:, now - HALF : now - HALF + LANES] += jnp.where(
                        lane + now < boundary, 0.0, moments
                    )
                turned = pltpu.roll(moments, lanes_up, 1)
                at = pl.multiple_of(now + tiles_up * LANES, LANES)
                lower_ref[:, pl.ds(at, LANES)] += lower_weight * jnp.where(
                    lane < lanes_up, before, turned
                )
                before = turned
        last = dot_nn(field_ref[slot, 4 * rows :], turned_edge_ref[...])
        last_ref[p] = last
        tail_ref[...] += jnp.where(lane == p, moments_of(last, rows), 0.0)
        return carry

    lax.fori_loop(0, 2 * PAIRS, one_pair, 0)

    lane = lax.broadcasted_iota(jnp.int32, (size, LANES), 1)
    after = jnp.broadcast_to(jnp.sum(tail_ref[...], axis=1, keepdims=True), (size, LANES))
    for tile in reversed(range(8)):
        total = lower_ref[:, tile * LANES : (tile + 1) * LANES]
        if tile >= 4:
            turned = pltpu.roll(upper_ref[:, (tile - 4) * LANES : (tile - 3) * LANES], LANES - 1, 1)
            total = total + 2.0 * jnp.where(lane == LANES - 1, after, turned)
            after = turned
        total = jnp.concatenate([total, jnp.zeros((LANES - size, LANES), jnp.float32)], axis=0)
        moment_ref[tile * LANES : (tile + 1) * LANES, :] = total.T


def in_vmem(value):
    return pltpu.with_memory_space_constraint(value, pltpu.VMEM)


def in_hbm(value):
    return pltpu.with_memory_space_constraint(value, pltpu.HBM)


def turn_kernel(leg_ref, out_ref):
    out_ref[0] = leg_ref[0].T


def turned(legendre):
    pairs, _, size = legendre.shape
    width = 256
    return pl.pallas_call(
        turn_kernel,
        grid=(pairs, DEGREES // width),
        in_specs=[pl.BlockSpec((1, width, size), lambda p, i: (p, i, 0))],
        out_specs=pl.BlockSpec((1, size, width), lambda p, i: (p, 0, i)),
        out_shape=pltpu.HBM((pairs, size, DEGREES), legendre.dtype),
        compiler_params=pltpu.CompilerParams(vmem_limit_bytes=SMALL_LIMIT),
        cost_estimate=pl.CostEstimate(flops=0, bytes_accessed=4 * legendre.size, transcendentals=0),
        name="turned",
    )(in_hbm(legendre))


def analysis(scalars, arrived, edges, own, other, rows):
    span = rows * 4
    arrived = arrived.reshape(32, 4, span, LANES)
    whole = pl.BlockSpec(memory_space=pltpu.VMEM)
    far = pl.BlockSpec(memory_space=pltpu.HBM)
    return pl.pallas_call(
        functools.partial(analysis_kernel, rows),
        in_specs=[pl.BlockSpec(memory_space=pltpu.SMEM), far, whole, far, far],
        out_specs=[whole, whole, whole],
        out_shape=[
            pltpu.VMEM((2 * PAIRS, 4 * rows, DEGREES), jnp.float32),
            pltpu.VMEM((2 * PAIRS, 4 * rows, LANES), jnp.float32),
            pltpu.VMEM((DEGREES, LANES), jnp.float32),
        ],
        scratch_shapes=[
            pltpu.VMEM((32, 4, span, LANES), jnp.bfloat16),
            pltpu.VMEM((4, DEGREES, DEGREES), jnp.bfloat16),
            pltpu.VMEM((LANES, LANES), jnp.bfloat16),
            pltpu.VMEM((DEGREES, LANES), jnp.bfloat16),
            pltpu.VMEM((SLOTS, 8 * rows, DEGREES), jnp.bfloat16),
            pltpu.VMEM((3 * rows, DEGREES + HALF), jnp.float32),
            pltpu.VMEM((3 * rows, HALF), jnp.float32),
            pltpu.VMEM((3 * rows, LANES), jnp.float32),
            pltpu.SemaphoreType.DMA((8,)),
            pltpu.SemaphoreType.DMA((4,)),
        ],
        compiler_params=pltpu.CompilerParams(vmem_limit_bytes=KERNEL_LIMIT),
        cost_estimate=pl.CostEstimate(
            flops=20 * rows * PAIRS * DEGREES * DEGREES,
            bytes_accessed=4 * own.size + 16 * rows * PAIRS * DEGREES + 2 * arrived.size,
            transcendentals=0,
        ),
        name="analysis",
    )(scalars, in_hbm(arrived), edges, in_hbm(own), in_hbm(other))


def factor_kernel(span, parts_ref, out_ref):
    total = jnp.sum(parts_ref[...], axis=0)
    size = total.shape[1]
    power_pred = total
    power_true = pltpu.roll(total, size - span, 1)
    cross = pltpu.roll(total, size - 2 * span, 1)
    pred = jnp.maximum(power_pred, POWER_FLOOR)
    true = jnp.maximum(power_true, POWER_FLOOR)
    root_pred = jnp.sqrt(pred)
    root_true = jnp.sqrt(true)
    both = pred + true
    upper_mean = (pred * pred + true * true) / both
    inverse = 1.0 / (root_pred * root_true)
    coherence = cross * inverse
    mean_slope = (2.0 * pred - upper_mean) / both
    slope = (
        (root_pred - root_true) / root_pred
        + 2.0 * mean_slope * (1.0 - coherence)
        + upper_mean * coherence / pred
    )
    binds = jnp.where(power_pred > POWER_FLOOR, 1.0, jnp.where(power_pred == POWER_FLOOR, 0.5, 0.0))
    dpower = 2.0 * slope * binds
    dcross = -2.0 * upper_mean * inverse
    lane = lax.broadcasted_iota(jnp.int32, total.shape, 1)
    factors = jnp.where(lane < span, dpower, pltpu.roll(dcross, span, 1))
    out_ref[...] = jnp.broadcast_to(factors[None], out_ref.shape)


def factors_of(parts, rows):
    whole = pl.BlockSpec(memory_space=pltpu.VMEM)
    return pl.pallas_call(
        functools.partial(factor_kernel, rows),
        in_specs=[whole],
        out_specs=whole,
        out_shape=pltpu.VMEM(parts.shape, jnp.float32),
        compiler_params=pltpu.CompilerParams(vmem_limit_bytes=TINY_LIMIT),
        cost_estimate=pl.CostEstimate(flops=parts.size, bytes_accessed=8 * parts.size, transcendentals=0),
        name="factors",
    )(in_vmem(parts))


def synthesis_kernel(
    rows, scalar_ref, coef_ref, last_ref, factor_ref, own_ref, other_ref, out_ref,
    spread_ref, upspread_ref, early_ref, late_ref, wide_ref,
):
    size = 2 * rows
    lane = lax.broadcasted_iota(jnp.int32, (size, LANES), 1)
    before = None
    for tile in range(8):
        turned = factor_ref[tile * LANES : (tile + 1) * LANES, :].T[:size]
        spread_ref[:, tile * LANES : (tile + 1) * LANES] = turned
        shifted = pltpu.roll(turned, 1, 1)
        if tile >= 4:
            upspread_ref[:, (tile - 4) * LANES : (tile - 3) * LANES] = 2.0 * jnp.where(
                lane == 0, before, shifted
            )
        before = shifted
    core = scalar_ref[2 * PAIRS]

    def one_pair(leg_ref, first, ring, carry):
        p = first + ring
        slot = p ^ (core * PAIRS)
        lower_order = scalar_ref[p]
        boundary = DEGREES - lower_order
        lower_weight = jnp.where(lower_order == 0, 1.0, 2.0)
        tiles_up = lower_order >> 7
        lanes_up = lower_order & (LANES - 1)
        back = (LANES - lanes_up) & (LANES - 1)

        def turned_tile(tile):
            at = pl.multiple_of((tile + tiles_up) * LANES, LANES)
            return pltpu.roll(spread_ref[:, pl.ds(at, LANES)], back, 1)

        def graded(factors, observe):
            grads = []
            for q in range(2):
                predicted = observe(q * rows)
                observed = observe((2 + q) * rows)
                grads.append(factors[:rows] * predicted + factors[rows:] * observed)
            return jnp.concatenate(grads, axis=0)

        now = turned_tile(0)
        for tile in range(8):
            start = tile * LANES
            then = turned_tile(tile + 1)
            factors = lower_weight * jnp.where(lane < LANES - lanes_up, now, then)
            now = then
            row = lane + start
            if tile >= 4:
                factors = jnp.where(
                    row < boundary, factors, upspread_ref[:, start - HALF : start - HALF + LANES]
                )
            grad = graded(factors, lambda at: coef_ref[p, at : at + rows, start : start + LANES])
            if tile >= 4:
                at = start - HALF
                late_ref[:size, at : at + LANES] = jnp.where(row < boundary, grad, 0.0).astype(
                    jnp.bfloat16
                )
                late_ref[size:, at : at + LANES] = jnp.where(row < boundary, 0.0, grad).astype(
                    jnp.bfloat16
                )
            else:
                early_ref[:, start : start + LANES] = grad.astype(jnp.bfloat16)
        last_factors = jnp.broadcast_to(2.0 * spread_ref[:, DEGREES - 1 : DEGREES], (size, LANES))
        edge_lane = lax.broadcasted_iota(jnp.int32, (4 * rows, LANES), 1)
        last = jnp.sum(jnp.where(edge_lane == p, last_ref[p], 0.0), axis=1, keepdims=True)
        last = jnp.broadcast_to(last, (4 * rows, LANES))
        last_grad = graded(last_factors, lambda at: last[at : at + rows])
        last_grad = last_grad.astype(jnp.bfloat16).astype(jnp.float32)
        last_leg = leg_ref[ring, DEGREES : DEGREES + 1, :].astype(jnp.float32)

        width = 256
        for tile in range(DEGREES // width):
            start = tile * width
            early = dot_nn(early_ref[...], leg_ref[ring, :HALF, start : start + width])
            late = dot_nn(late_ref[...], leg_ref[ring, HALF:DEGREES, start : start + width])
            lower, upper = early + late[:size], late[size:]
            for sub in range(width // LANES):
                at = start + sub * LANES
                inside = slice(sub * LANES, (sub + 1) * LANES)
                top = lower[:, inside]
                bottom = upper[:, inside] + last_grad * last_leg[:, at : at + LANES]
                blocks = [top[:rows], top[rows:], bottom[:rows], bottom[rows:]]
                blocks = [
                    block if g == 0 else pltpu.roll(block, 32 * g, 1) for g, block in enumerate(blocks)
                ]
                for i in range(4):
                    wide_ref[at // 32 + i, pl.ds(slot, rows, stride=SLOTS), :] = by_position(blocks, i)
        return carry

    lax.fori_loop(0, PAIRS, functools.partial(one_pair, own_ref, 0), 0, unroll=4)
    lax.fori_loop(0, PAIRS, functools.partial(one_pair, other_ref, PAIRS), 0, unroll=4)

    def narrow(j, carry):
        out_ref[j] = wide_ref[j].astype(jnp.bfloat16)
        return carry

    lax.fori_loop(0, 32, narrow, 0, unroll=8)


def synthesis(scalars, coeffs, last, factors, own, other, rows):
    whole = pl.BlockSpec(memory_space=pltpu.VMEM)
    return pl.pallas_call(
        functools.partial(synthesis_kernel, rows),
        in_specs=[pl.BlockSpec(memory_space=pltpu.SMEM)] + [whole] * 5,
        out_specs=whole,
        out_shape=pltpu.VMEM((32, rows * SLOTS, LANES), jnp.bfloat16),
        scratch_shapes=[
            pltpu.VMEM((2 * rows, DEGREES + HALF), jnp.float32),
            pltpu.VMEM((2 * rows, HALF), jnp.float32),
            pltpu.VMEM((2 * rows, HALF), jnp.bfloat16),
            pltpu.VMEM((4 * rows, HALF), jnp.bfloat16),
            pltpu.VMEM((32, rows * SLOTS, LANES), jnp.float32),
        ],
        compiler_params=pltpu.CompilerParams(vmem_limit_bytes=SMALL_LIMIT),
        cost_estimate=pl.CostEstimate(
            flops=12 * rows * PAIRS * DEGREES * DEGREES,
            bytes_accessed=4 * own.size + 16 * rows * PAIRS * DEGREES + 64 * rows * SLOTS * LANES,
            transcendentals=0,
        ),
        name="synthesis",
    )(scalars, *(in_vmem(value) for value in (coeffs, last, factors, own, other)))


def unpack_kernel(
    channels, turn_ref, pairs_ref, returned_ref, out_hbm, out_ref, lower_ref, upper_ref, sems
):
    one_hots(pairs_ref, lower_ref, upper_ref)
    turn = turn_ref[0]

    def send(i):
        at = pl.ds(2 * i, 2)
        return pltpu.make_async_copy(out_ref.at[at], out_hbm.at[at], sems.at[i])

    steps = channels // 2
    for i in range(steps):
        sides = []
        for c in range(2 * i, 2 * i + 2):
            first, second = (
                returned_ref[:, sample, :, (c // 2) * 16 : (c // 2) * 16 + 16]
                .astype(jnp.float32)[:, :, (c % 2) * SLOTS : (c % 2 + 1) * SLOTS]
                .reshape(HALF, LANES)
                for sample in range(2)
            )
            group = lax.broadcasted_iota(jnp.int32, first.shape, 1) >> 5
            keep = ((group - turn) & 3) < 2
            sides.append(
                (
                    jnp.where(keep, first, pltpu.roll(second, 64, 1)),
                    jnp.where(keep, pltpu.roll(first, 64, 1), second),
                )
            )
        for o, one_hot_ref in enumerate((lower_ref, upper_ref)):
            by_slot = jnp.concatenate([side[o] for side in sides], axis=1)
            field = dot_tn(by_slot.astype(jnp.bfloat16), one_hot_ref[...]).astype(jnp.bfloat16)
            for c in range(2):
                for z in range(4):
                    at = c * LANES + z * 32
                    out_ref[2 * i + c, (z - turn) & 3, :, o * HALF : (o + 1) * HALF] = field[at : at + 32]
        send(i).start()
    for i in range(steps):
        send(i).wait()


def unpack(turn, pairs, returned, channels):
    whole = pl.BlockSpec(memory_space=pltpu.VMEM)
    return pl.pallas_call(
        functools.partial(unpack_kernel, channels),
        in_specs=[pl.BlockSpec(memory_space=pltpu.SMEM), whole, whole],
        out_specs=pl.BlockSpec(memory_space=pltpu.HBM),
        out_shape=pltpu.HBM((channels, 4, 32, DEGREES), jnp.bfloat16),
        scratch_shapes=[
            pltpu.VMEM((channels, 4, 32, DEGREES), jnp.bfloat16),
            pltpu.VMEM((HALF, HALF), jnp.bfloat16),
            pltpu.VMEM((HALF, HALF), jnp.bfloat16),
            pltpu.SemaphoreType.DMA((channels // 2,)),
        ],
        compiler_params=pltpu.CompilerParams(vmem_limit_bytes=KERNEL_LIMIT),
        cost_estimate=pl.CostEstimate(
            flops=DEGREES * DEGREES * LANES * channels,
            bytes_accessed=4 * LANES * DEGREES * channels,
            transcendentals=0,
        ),
        name="unpack",
    )(turn, pairs, in_vmem(returned))


def exchange(values, axes):
    return lax.all_to_all(values, axes, split_axis=0, concat_axis=0, tiled=True)


def per_device(pred_four, target_four, legendre, pair_order):
    channels = pred_four.shape[0]
    devices = DEGREES // SLOTS
    rows = 4 * channels
    core = lax.axis_index("core")
    device = lax.axis_index(DEVICES)
    turn = ((2 * lax.axis_index("zx") + core) & 3).reshape(1)
    pair_row = pair_order.reshape(1, HALF)
    other_legendre = lax.ppermute(legendre, "core", [(0, 1), (1, 0)])
    own_order = lax.dynamic_slice_in_dim(pair_order, device * PAIRS, PAIRS)
    other_order = lax.dynamic_slice_in_dim(pair_order, (device ^ 4) * PAIRS, PAIRS)
    scalars = jnp.concatenate([own_order, other_order, core.astype(jnp.int32).reshape(1)])

    by_group = (channels, 4, 32, DEGREES)
    packed = pack(turn, pair_row, pred_four.reshape(by_group), target_four.reshape(by_group))
    arrived = exchange(packed.reshape(devices, rows * 4, LANES), DEVICES)
    edges = jnp.concatenate([legendre[:, DEGREES], other_legendre[:, DEGREES]]).astype(jnp.float32)
    coeffs, last, moments = analysis(
        scalars, arrived, edges, turned(legendre), turned(other_legendre), rows
    )
    spectra = exchange(moments.reshape(devices // 2, 2 * SLOTS, LANES), SAME_CORE)
    factors = exchange(factors_of(spectra, rows), SAME_CORE).reshape(DEGREES, LANES)
    going = synthesis(scalars, coeffs, last, factors, legendre, other_legendre, rows)
    returned = exchange(going.reshape(devices, rows * 2, LANES), DEVICES)
    returned = returned.reshape(16, 2, 4, rows * 2, LANES)
    return unpack(turn, pair_row, returned, channels).reshape(pred_four.shape)


def solution(mesh):
    by_core = Mesh(mesh.devices.reshape(16, 2, 4), DEVICES)
    field = P("col", None, None, ("zx", "core"), None)
    return jax.shard_map(
        per_device,
        mesh=by_core,
        in_specs=(field, field, P(DEVICES, None, None), P()),
        out_specs=field,
        check_vma=False,
    )
```

```python
import functools

import jax
import jax.numpy as jnp
from jax import lax
from jax.experimental import pallas as pl
from jax.experimental.pallas import tpu as pltpu
from jax.sharding import Mesh
from jax.sharding import PartitionSpec as P

DEGREES = 1024
HALF = DEGREES // 2
POWER_FLOOR = 0.5
LANES = 128
SLOTS = 8
PAIRS = 4
DEVICES = ("zx", "core", "col")
SAME_CORE = ("zx", "col")
KERNEL_LIMIT = 36 * 1024 * 1024
MIDDLE_LIMIT = 26 * 1024 * 1024
SMALL_LIMIT = 16 * 1024 * 1024
TINY_LIMIT = 4 * 1024 * 1024


def dot_nt(left, right):
    return lax.dot_general(left, right, (((1,), (1,)), ((), ())), preferred_element_type=jnp.float32)


def dot_nn(left, right):
    return lax.dot_general(left, right, (((1,), (0,)), ((), ())), preferred_element_type=jnp.float32)


def dot_tn(left, right):
    return lax.dot_general(left, right, (((0,), (0,)), ((), ())), preferred_element_type=jnp.float32)


def by_position(blocks, shift):
    group = lax.broadcasted_iota(jnp.int32, blocks[0].shape, 1) >> 5
    result = blocks[-shift % 4]
    for z in range(1, 4):
        result = jnp.where(group == z, blocks[(z - shift) % 4], result)
    return result


def trade_halves(first, second):
    top = lax.broadcasted_iota(jnp.int32, first.shape, 1) < 4
    return (
        jnp.where(top, first, pltpu.roll(second, 4, 1)),
        jnp.where(top, pltpu.roll(first, 4, 1), second),
    )


def one_hots(pairs_ref, lower_ref, upper_ref):
    order = jnp.broadcast_to(pairs_ref[...].astype(jnp.float32), (LANES, HALF)).T
    by_core = order.reshape(16, 2, 2, 8, LANES)
    first, second = by_core[:, 0].reshape(32, 8, LANES), by_core[:, 1].reshape(32, 8, LANES)
    order = jnp.stack(trade_halves(first, second), axis=1).reshape(HALF, LANES)
    order = jnp.concatenate([order] * (HALF // LANES), axis=1).astype(jnp.int32)
    lane = lax.broadcasted_iota(jnp.int32, (HALF, HALF), 1)
    lower_ref[...] = jnp.where(lane == order, 1.0, 0.0).astype(jnp.bfloat16)
    upper_ref[...] = jnp.where(lane == HALF - 1 - order, 1.0, 0.0).astype(jnp.bfloat16)


def pack_kernel(
    channels, turn_ref, pairs_hbm, pred_hbm, target_hbm, out_hbm,
    pairs_ref, field_ref, out_ref, lower_ref, upper_ref, pair_sem, in_sems, out_sems,
):
    steps = channels // 2
    ahead = 2

    def fetch(i, f):
        source = (pred_hbm, target_hbm)[f].at[pl.ds(2 * i, 2)]
        return pltpu.make_async_copy(source, field_ref.at[f, pl.ds(2 * i, 2)], in_sems.at[f, i])

    def send(i):
        return pltpu.make_async_copy(
            out_ref.at[i], out_hbm.at[:, :, :, pl.ds(2 * i, 2)], out_sems.at[i]
        )

    pair_copy = pltpu.make_async_copy(pairs_hbm, pairs_ref, pair_sem)
    pair_copy.start()
    for i in range(ahead):
        for f in range(2):
            fetch(i, f).start()
    pair_copy.wait()
    one_hots(pairs_ref, lower_ref, upper_ref)

    turn = turn_ref[0]

    def step(i, carry):
        @pl.when(i + ahead < steps)
        def _():
            for f in range(2):
                fetch(i + ahead, f).start()

        for f in range(2):
            fetch(i, f).wait()
        for c in range(2):
            pieces = []
            for sample in range(2):
                for z in range(4):
                    group = (z - turn) & 3
                    pieces.append(field_ref[group >> 1, 2 * i + c, 2 * sample + (group & 1)])
            field = jnp.concatenate(pieces, axis=0)
            low = dot_nt(lower_ref[...], field[:, :HALF]).reshape(HALF // 8, 8, 2 * LANES)
            high = dot_nt(upper_ref[...], field[:, HALF:]).reshape(HALF // 8, 8, 2 * LANES)
            both = jnp.concatenate([low, high], axis=1).astype(jnp.bfloat16)
            for sample in range(2):
                block = both[:, :, sample * LANES : (sample + 1) * LANES]
                out_ref[i, :, sample, :, c] = block.reshape(16, 4, 16, LANES)
        send(i).start()
        return carry

    lax.fori_loop(0, steps, step, 0, unroll=True)
    for i in range(steps):
        send(i).wait()


def pack(turn, pairs, pred, target):
    channels = pred.shape[0]
    steps = channels // 2
    far = pl.BlockSpec(memory_space=pltpu.HBM)
    return pl.pallas_call(
        functools.partial(pack_kernel, channels),
        in_specs=[pl.BlockSpec(memory_space=pltpu.SMEM), far, far, far],
        out_specs=far,
        out_shape=pltpu.HBM((16, 2, 4, channels, 16, LANES), jnp.bfloat16),
        scratch_shapes=[
            pltpu.VMEM((1, HALF), jnp.int32),
            pltpu.VMEM((2, channels, 4, 32, DEGREES), jnp.bfloat16),
            pltpu.VMEM((steps, 16, 2, 4, 2, 16, LANES), jnp.bfloat16),
            pltpu.VMEM((HALF, HALF), jnp.bfloat16),
            pltpu.VMEM((HALF, HALF), jnp.bfloat16),
            pltpu.SemaphoreType.DMA,
            pltpu.SemaphoreType.DMA((2, steps)),
            pltpu.SemaphoreType.DMA((steps,)),
        ],
        compiler_params=pltpu.CompilerParams(vmem_limit_bytes=KERNEL_LIMIT),
        cost_estimate=pl.CostEstimate(
            flops=DEGREES * DEGREES * 2 * LANES * channels,
            bytes_accessed=8 * LANES * DEGREES * channels,
            transcendentals=0,
        ),
        name="pack",
    )(turn, in_hbm(pairs), in_hbm(pred), in_hbm(target))


def moments_of(values, rows):
    shaped = values.reshape(2, 2, rows, values.shape[-1])
    pieces = []
    for left, right in ((0, 0), (1, 1), (0, 1)):
        real = shaped[left, 0] * shaped[right, 0]
        imag = shaped[left, 1] * shaped[right, 1]
        pieces.append(real + imag)
    return jnp.concatenate(pieces, axis=0)


def leg_stream(own_hbm, other_hbm, leg_ref, sems):
    def start(p):
        for hbm, here in ((own_hbm, p < PAIRS), (other_hbm, p >= PAIRS)):

            @pl.when(here)
            def _(hbm=hbm):
                at = p & 3
                pltpu.make_async_copy(hbm.at[at], leg_ref.at[at], sems.at[at]).start()

    def wait(p):
        at = p & 3
        pltpu.make_async_copy(own_hbm.at[at], leg_ref.at[at], sems.at[at]).wait()

    return start, wait


def analysis_kernel(
    rows, scalar_ref, arrived_ref, edge_ref, own_hbm, other_hbm, coef_ref, last_ref, moment_ref,
    narrow_ref, leg_ref, sort_ref, turned_edge_ref, field_ref, lower_ref, upper_ref, tail_ref, sems, leg_sems,
):
    size = 3 * rows
    span = arrived_ref.shape[2]
    slots = 2 * SLOTS

    def chunk(k):
        at = pl.ds(4 * k, 4)
        return pltpu.make_async_copy(arrived_ref.at[at], narrow_ref.at[at], sems.at[k])

    start_leg, wait_leg = leg_stream(own_hbm, other_hbm, leg_ref, leg_sems)
    for k in range(8):
        chunk(k).start()
    lower_ref[...] = jnp.zeros_like(lower_ref)
    upper_ref[...] = jnp.zeros_like(upper_ref)
    tail_ref[...] = jnp.zeros_like(tail_ref)
    edges = jnp.concatenate([edge_ref[...], jnp.zeros((LANES - SLOTS, DEGREES), jnp.float32)], axis=0)
    turned_edge_ref[...] = edges.T.astype(jnp.bfloat16)
    row = lax.broadcasted_iota(jnp.int32, (LANES, LANES), 0)
    column = lax.broadcasted_iota(jnp.int32, (LANES, LANES), 1)
    takes = column == (row & (SLOTS - 1)) * slots + (row >> 3)
    sort_ref[...] = jnp.where(takes, 1.0, 0.0).astype(jnp.bfloat16)

    def build(k, carry):
        chunk(k).wait()

        @pl.when((k == 1) | (k == 3) | (k == 5))
        def _():
            start_leg(k >> 1)

        at = pl.multiple_of(k * LANES, LANES)
        for f in range(2):
            tiles = []
            for col in range(4):
                both = []
                for q in range(2):
                    g = 2 * f + q
                    block = by_position([narrow_ref[4 * k + i, col] for i in range(4)], g)
                    if g > 0:
                        block = pltpu.roll(block, LANES - 32 * g, 1)
                    both.append(block)
                both = jnp.concatenate(both, axis=1)
                tiles += [both[c * slots : (c + 1) * slots] for c in range(span // slots)]
            sorted_rows = []
            for u in range(rows // SLOTS):
                group = jnp.concatenate(tiles[u * SLOTS : (u + 1) * SLOTS], axis=0)
                sorted_rows.append(dot_nn(sort_ref[...], group))
            for slot in range(slots):
                parts = [
                    block[slot * SLOTS : (slot + 1) * SLOTS, q * LANES : (q + 1) * LANES]
                    for q in range(2)
                    for block in sorted_rows
                ]
                low = 4 * rows * (slot // SLOTS) + 2 * f * rows
                field_ref[slot % SLOTS, low : low + 2 * rows, pl.ds(at, LANES)] = jnp.concatenate(
                    parts, axis=0
                ).astype(jnp.bfloat16)
        return carry

    lax.fori_loop(0, 8, build, 0)
    core = scalar_ref[2 * PAIRS]

    def one_pair(p, carry):
        @pl.when(p + 3 < 2 * PAIRS)
        def _():
            start_leg(p + 3)

        wait_leg(p)
        ring = p & 3
        slot = p ^ (core * PAIRS)
        lower_order = scalar_ref[p]
        boundary = DEGREES - lower_order
        width = 256
        lower_weight = jnp.where(lower_order == 0, 1.0, 2.0)
        tiles_up = lower_order >> 7
        lanes_up = lower_order & (LANES - 1)
        lane = lax.broadcasted_iota(jnp.int32, (size, LANES), 1)
        late = (lower_order <= width).astype(jnp.int32)
        at = pl.multiple_of(HALF + width * late, width)
        low = pl.multiple_of(4 * rows * (1 - late), 4 * rows)
        extra = dot_nn(field_ref[slot, pl.ds(low, 4 * rows)], leg_ref[ring, :, pl.ds(at, width)])
        before = jnp.zeros((size, LANES), jnp.float32)
        for tile in range(DEGREES // width):
            start = tile * width
            low = 4 * rows * (tile // 3)
            values = dot_nn(field_ref[slot, low : low + 4 * rows], leg_ref[ring, :, start : start + width])
            if start >= HALF:
                row = lax.broadcasted_iota(jnp.int32, values.shape, 1) + start
                first, second = (values, extra) if tile == 2 else (extra, values)
                values = jnp.where(row < boundary, first, second)
            coef_ref[p, :, start : start + width] = values
            for sub in range(width // LANES):
                moments = moments_of(values[:, sub * LANES : (sub + 1) * LANES], rows)
                now = start + sub * LANES
                if start >= HALF:
                    upper_ref[:, now - HALF : now - HALF + LANES] += jnp.where(
                        lane + now < boundary, 0.0, moments
                    )
                turned = pltpu.roll(moments, lanes_up, 1)
                at = pl.multiple_of(now + tiles_up * LANES, LANES)
                lower_ref[:, pl.ds(at, LANES)] += lower_weight * jnp.where(
                    lane < lanes_up, before, turned
                )
                before = turned
        last = dot_nn(field_ref[slot, 4 * rows :], turned_edge_ref[...])
        last_ref[p] = last
        tail_ref[...] += jnp.where(lane == p, moments_of(last, rows), 0.0)
        return carry

    lax.fori_loop(0, 2 * PAIRS, one_pair, 0)

    lane = lax.broadcasted_iota(jnp.int32, (size, LANES), 1)
    after = jnp.broadcast_to(jnp.sum(tail_ref[...], axis=1, keepdims=True), (size, LANES))
    for tile in reversed(range(8)):
        total = lower_ref[:, tile * LANES : (tile + 1) * LANES]
        if tile >= 4:
            turned = pltpu.roll(upper_ref[:, (tile - 4) * LANES : (tile - 3) * LANES], LANES - 1, 1)
            total = total + 2.0 * jnp.where(lane == LANES - 1, after, turned)
            after = turned
        total = jnp.concatenate([total, jnp.zeros((LANES - size, LANES), jnp.float32)], axis=0)
        by_degree = total.T
        for h in range(2):
            moment_ref[pl.ds(2 * tile + h, 64, stride=16), :] = by_degree[64 * h : 64 * (h + 1)]


def in_vmem(value):
    return pltpu.with_memory_space_constraint(value, pltpu.VMEM)


def in_hbm(value):
    return pltpu.with_memory_space_constraint(value, pltpu.HBM)


def turn_kernel(leg_ref, out_ref):
    out_ref[0] = leg_ref[0].T


def turned(legendre):
    pairs, _, size = legendre.shape
    width = 256
    return pl.pallas_call(
        turn_kernel,
        grid=(pairs, DEGREES // width),
        in_specs=[pl.BlockSpec((1, width, size), lambda p, i: (p, i, 0))],
        out_specs=pl.BlockSpec((1, size, width), lambda p, i: (p, 0, i)),
        out_shape=pltpu.HBM((pairs, size, DEGREES), legendre.dtype),
        compiler_params=pltpu.CompilerParams(vmem_limit_bytes=SMALL_LIMIT),
        cost_estimate=pl.CostEstimate(flops=0, bytes_accessed=4 * legendre.size, transcendentals=0),
        name="turned",
    )(in_hbm(legendre))


def analysis(scalars, arrived, edges, own, other, rows):
    span = rows * 4
    arrived = arrived.reshape(32, 4, span, LANES)
    whole = pl.BlockSpec(memory_space=pltpu.VMEM)
    far = pl.BlockSpec(memory_space=pltpu.HBM)
    return pl.pallas_call(
        functools.partial(analysis_kernel, rows),
        in_specs=[pl.BlockSpec(memory_space=pltpu.SMEM), far, whole, far, far],
        out_specs=[whole, whole, whole],
        out_shape=[
            pltpu.VMEM((2 * PAIRS, 4 * rows, DEGREES), jnp.float32),
            pltpu.VMEM((2 * PAIRS, 4 * rows, LANES), jnp.float32),
            pltpu.VMEM((DEGREES, LANES), jnp.float32),
        ],
        scratch_shapes=[
            pltpu.VMEM((32, 4, span, LANES), jnp.bfloat16),
            pltpu.VMEM((4, DEGREES, DEGREES), jnp.bfloat16),
            pltpu.VMEM((LANES, LANES), jnp.bfloat16),
            pltpu.VMEM((DEGREES, LANES), jnp.bfloat16),
            pltpu.VMEM((SLOTS, 8 * rows, DEGREES), jnp.bfloat16),
            pltpu.VMEM((3 * rows, DEGREES + HALF), jnp.float32),
            pltpu.VMEM((3 * rows, HALF), jnp.float32),
            pltpu.VMEM((3 * rows, LANES), jnp.float32),
            pltpu.SemaphoreType.DMA((8,)),
            pltpu.SemaphoreType.DMA((4,)),
        ],
        compiler_params=pltpu.CompilerParams(vmem_limit_bytes=KERNEL_LIMIT),
        cost_estimate=pl.CostEstimate(
            flops=20 * rows * PAIRS * DEGREES * DEGREES,
            bytes_accessed=4 * own.size + 16 * rows * PAIRS * DEGREES + 2 * arrived.size,
            transcendentals=0,
        ),
        name="analysis",
    )(scalars, in_hbm(arrived), edges, in_hbm(own), in_hbm(other))


def factor_kernel(span, parts_ref, out_ref):
    total = jnp.sum(parts_ref[...], axis=0)
    size = total.shape[1]
    power_pred = total
    power_true = pltpu.roll(total, size - span, 1)
    cross = pltpu.roll(total, size - 2 * span, 1)
    pred = jnp.maximum(power_pred, POWER_FLOOR)
    true = jnp.maximum(power_true, POWER_FLOOR)
    root_pred = jnp.sqrt(pred)
    root_true = jnp.sqrt(true)
    both = pred + true
    upper_mean = (pred * pred + true * true) / both
    inverse = 1.0 / (root_pred * root_true)
    coherence = cross * inverse
    mean_slope = (2.0 * pred - upper_mean) / both
    slope = (
        (root_pred - root_true) / root_pred
        + 2.0 * mean_slope * (1.0 - coherence)
        + upper_mean * coherence / pred
    )
    binds = jnp.where(power_pred > POWER_FLOOR, 1.0, jnp.where(power_pred == POWER_FLOOR, 0.5, 0.0))
    dpower = 2.0 * slope * binds
    dcross = -2.0 * upper_mean * inverse
    lane = lax.broadcasted_iota(jnp.int32, total.shape, 1)
    factors = jnp.where(lane < span, dpower, pltpu.roll(dcross, span, 1))
    by_half = [
        jnp.concatenate([factors[2 * k + h : 2 * k + h + 1, : 2 * span] for k in range(8)], axis=1)
        for h in range(2)
    ]
    out_ref[...] = jnp.broadcast_to(jnp.concatenate(by_half, axis=0)[None], out_ref.shape)


def factors_of(parts, rows):
    whole = pl.BlockSpec(memory_space=pltpu.VMEM)
    return pl.pallas_call(
        functools.partial(factor_kernel, rows),
        in_specs=[whole],
        out_specs=whole,
        out_shape=pltpu.VMEM((parts.shape[0], 2, 16 * rows), jnp.float32),
        compiler_params=pltpu.CompilerParams(vmem_limit_bytes=TINY_LIMIT),
        cost_estimate=pl.CostEstimate(flops=parts.size, bytes_accessed=8 * parts.size, transcendentals=0),
        name="factors",
    )(in_vmem(parts))


def synthesis_kernel(
    rows, scalar_ref, coef_ref, last_ref, factor_ref, own_hbm, other_ref, out_ref,
    own_ref, spread_ref, upspread_ref, early_ref, late_ref, wide_ref, sems,
):
    size = 2 * rows
    lane = lax.broadcasted_iota(jnp.int32, (size, LANES), 1)
    def own_copy(p):
        return pltpu.make_async_copy(own_hbm.at[p], own_ref.at[p], sems.at[p])

    for p in range(PAIRS):
        own_copy(p).start()

    before = None
    by_degree = jnp.concatenate([factor_ref[:, h, :] for h in range(2)], axis=0).T
    for tile in range(8):
        turned = by_degree[tile * size : (tile + 1) * size]
        spread_ref[:, tile * LANES : (tile + 1) * LANES] = turned
        shifted = pltpu.roll(turned, 1, 1)
        if tile >= 4:
            upspread_ref[:, (tile - 4) * LANES : (tile - 3) * LANES] = 2.0 * jnp.where(
                lane == 0, before, shifted
            )
        before = shifted
    core = scalar_ref[2 * PAIRS]

    def one_pair(leg_ref, first, ring, carry):
        p = first + ring
        slot = p ^ (core * PAIRS)
        lower_order = scalar_ref[p]
        boundary = DEGREES - lower_order
        lower_weight = jnp.where(lower_order == 0, 1.0, 2.0)
        tiles_up = lower_order >> 7
        lanes_up = lower_order & (LANES - 1)
        back = (LANES - lanes_up) & (LANES - 1)

        def turned_tile(tile):
            at = pl.multiple_of((tile + tiles_up) * LANES, LANES)
            return pltpu.roll(spread_ref[:, pl.ds(at, LANES)], back, 1)

        def graded(factors, observe):
            grads = []
            for q in range(2):
                predicted = observe(q * rows)
                observed = observe((2 + q) * rows)
                grads.append(factors[:rows] * predicted + factors[rows:] * observed)
            return jnp.concatenate(grads, axis=0)

        now = turned_tile(0)
        for tile in range(8):
            start = tile * LANES
            then = turned_tile(tile + 1)
            factors = lower_weight * jnp.where(lane < LANES - lanes_up, now, then)
            now = then
            row = lane + start
            if tile >= 4:
                factors = jnp.where(
                    row < boundary, factors, upspread_ref[:, start - HALF : start - HALF + LANES]
                )
            grad = graded(factors, lambda at: coef_ref[p, at : at + rows, start : start + LANES])
            if tile >= 4:
                at = start - HALF
                late_ref[:size, at : at + LANES] = jnp.where(row < boundary, grad, 0.0).astype(
                    jnp.bfloat16
                )
                late_ref[size:, at : at + LANES] = jnp.where(row < boundary, 0.0, grad).astype(
                    jnp.bfloat16
                )
            else:
                early_ref[:, start : start + LANES] = grad.astype(jnp.bfloat16)
        last_factors = jnp.broadcast_to(2.0 * spread_ref[:, DEGREES - 1 : DEGREES], (size, LANES))
        edge_lane = lax.broadcasted_iota(jnp.int32, (4 * rows, LANES), 1)
        last = jnp.sum(jnp.where(edge_lane == p, last_ref[p], 0.0), axis=1, keepdims=True)
        last = jnp.broadcast_to(last, (4 * rows, LANES))
        last_grad = graded(last_factors, lambda at: last[at : at + rows])
        last_grad = last_grad.astype(jnp.bfloat16).astype(jnp.float32)
        last_leg = leg_ref[ring, DEGREES : DEGREES + 1, :].astype(jnp.float32)

        width = 256
        for tile in range(DEGREES // width):
            start = tile * width
            early = dot_nn(early_ref[...], leg_ref[ring, :HALF, start : start + width])
            late = dot_nn(late_ref[...], leg_ref[ring, HALF:DEGREES, start : start + width])
            lower, upper = early + late[:size], late[size:]
            for sub in range(width // LANES):
                at = start + sub * LANES
                inside = slice(sub * LANES, (sub + 1) * LANES)
                top = lower[:, inside]
                bottom = upper[:, inside] + last_grad * last_leg[:, at : at + LANES]
                blocks = [top[:rows], top[rows:], bottom[:rows], bottom[rows:]]
                blocks = [
                    block if g == 0 else pltpu.roll(block, 32 * g, 1) for g, block in enumerate(blocks)
                ]
                for i in range(4):
                    wide_ref[at // 32 + i, pl.ds(slot, rows, stride=SLOTS), :] = by_position(blocks, i)
        return carry

    def own_pair(p, carry):
        own_copy(p).wait()
        return one_pair(own_ref, 0, p, carry)

    lax.fori_loop(0, PAIRS, functools.partial(one_pair, other_ref, PAIRS), 0, unroll=4)
    lax.fori_loop(0, PAIRS, own_pair, 0, unroll=4)

    def narrow(j, carry):
        out_ref[j] = wide_ref[j].astype(jnp.bfloat16)
        return carry

    lax.fori_loop(0, 32, narrow, 0, unroll=8)


def synthesis(scalars, coeffs, last, factors, own, other, rows):
    whole = pl.BlockSpec(memory_space=pltpu.VMEM)
    return pl.pallas_call(
        functools.partial(synthesis_kernel, rows),
        in_specs=[pl.BlockSpec(memory_space=pltpu.SMEM)]
        + [whole] * 3
        + [pl.BlockSpec(memory_space=pltpu.HBM), whole],
        out_specs=whole,
        out_shape=pltpu.VMEM((32, rows * SLOTS, LANES), jnp.bfloat16),
        scratch_shapes=[
            pltpu.VMEM(own.shape, jnp.bfloat16),
            pltpu.VMEM((2 * rows, DEGREES + HALF), jnp.float32),
            pltpu.VMEM((2 * rows, HALF), jnp.float32),
            pltpu.VMEM((2 * rows, HALF), jnp.bfloat16),
            pltpu.VMEM((4 * rows, HALF), jnp.bfloat16),
            pltpu.VMEM((32, rows * SLOTS, LANES), jnp.float32),
            pltpu.SemaphoreType.DMA((PAIRS,)),
        ],
        compiler_params=pltpu.CompilerParams(vmem_limit_bytes=MIDDLE_LIMIT),
        cost_estimate=pl.CostEstimate(
            flops=12 * rows * PAIRS * DEGREES * DEGREES,
            bytes_accessed=4 * own.size + 16 * rows * PAIRS * DEGREES + 64 * rows * SLOTS * LANES,
            transcendentals=0,
        ),
        name="synthesis",
    )(scalars, *(in_vmem(value) for value in (coeffs, last, factors)), in_hbm(own), in_vmem(other))


def unpack_kernel(
    channels, turn_ref, pairs_ref, returned_ref, out_hbm, out_ref, lower_ref, upper_ref, sems
):
    one_hots(pairs_ref, lower_ref, upper_ref)
    turn = turn_ref[0]

    def send(i):
        at = pl.ds(2 * i, 2)
        return pltpu.make_async_copy(out_ref.at[at], out_hbm.at[at], sems.at[i])

    steps = channels // 2
    for i in range(steps):
        sides = []
        for c in range(2 * i, 2 * i + 2):
            first, second = (
                returned_ref[:, sample, :, (c // 2) * 16 : (c // 2) * 16 + 16]
                .astype(jnp.float32)[:, :, (c % 2) * SLOTS : (c % 2 + 1) * SLOTS]
                .reshape(HALF, LANES)
                for sample in range(2)
            )
            group = lax.broadcasted_iota(jnp.int32, first.shape, 1) >> 5
            keep = ((group - turn) & 3) < 2
            sides.append(
                (
                    jnp.where(keep, first, pltpu.roll(second, 64, 1)),
                    jnp.where(keep, pltpu.roll(first, 64, 1), second),
                )
            )
        for o, one_hot_ref in enumerate((lower_ref, upper_ref)):
            by_slot = jnp.concatenate([side[o] for side in sides], axis=1)
            field = dot_tn(by_slot.astype(jnp.bfloat16), one_hot_ref[...]).astype(jnp.bfloat16)
            for c in range(2):
                for z in range(4):
                    at = c * LANES + z * 32
                    out_ref[2 * i + c, (z - turn) & 3, :, o * HALF : (o + 1) * HALF] = field[at : at + 32]
        send(i).start()
    for i in range(steps):
        send(i).wait()


def unpack(turn, pairs, returned, channels):
    whole = pl.BlockSpec(memory_space=pltpu.VMEM)
    return pl.pallas_call(
        functools.partial(unpack_kernel, channels),
        in_specs=[pl.BlockSpec(memory_space=pltpu.SMEM), whole, whole],
        out_specs=pl.BlockSpec(memory_space=pltpu.HBM),
        out_shape=pltpu.HBM((channels, 4, 32, DEGREES), jnp.bfloat16),
        scratch_shapes=[
            pltpu.VMEM((channels, 4, 32, DEGREES), jnp.bfloat16),
            pltpu.VMEM((HALF, HALF), jnp.bfloat16),
            pltpu.VMEM((HALF, HALF), jnp.bfloat16),
            pltpu.SemaphoreType.DMA((channels // 2,)),
        ],
        compiler_params=pltpu.CompilerParams(vmem_limit_bytes=KERNEL_LIMIT),
        cost_estimate=pl.CostEstimate(
            flops=DEGREES * DEGREES * LANES * channels,
            bytes_accessed=4 * LANES * DEGREES * channels,
            transcendentals=0,
        ),
        name="unpack",
    )(turn, pairs, in_vmem(returned))


def exchange(values, axes):
    return lax.all_to_all(values, axes, split_axis=0, concat_axis=0, tiled=True)


def per_device(pred_four, target_four, legendre, pair_order):
    channels = pred_four.shape[0]
    devices = DEGREES // SLOTS
    rows = 4 * channels
    core = lax.axis_index("core")
    device = lax.axis_index(DEVICES)
    turn = ((2 * lax.axis_index("zx") + core) & 3).reshape(1)
    pair_row = pair_order.reshape(1, HALF)
    other_legendre = lax.ppermute(legendre, "core", [(0, 1), (1, 0)])
    own_order = lax.dynamic_slice_in_dim(pair_order, device * PAIRS, PAIRS)
    other_order = lax.dynamic_slice_in_dim(pair_order, (device ^ 4) * PAIRS, PAIRS)
    scalars = jnp.concatenate([own_order, other_order, core.astype(jnp.int32).reshape(1)])

    by_group = (channels, 4, 32, DEGREES)
    packed = pack(turn, pair_row, pred_four.reshape(by_group), target_four.reshape(by_group))
    arrived = exchange(packed.reshape(devices, rows * 4, LANES), DEVICES)
    edges = jnp.concatenate([legendre[:, DEGREES], other_legendre[:, DEGREES]]).astype(jnp.float32)
    coeffs, last, moments = analysis(
        scalars, arrived, edges, turned(legendre), turned(other_legendre), rows
    )
    spectra = exchange(moments.reshape(devices // 2, 2 * SLOTS, LANES), SAME_CORE)
    factors = exchange(factors_of(spectra, rows), SAME_CORE)
    going = synthesis(scalars, coeffs, last, factors, legendre, other_legendre, rows)
    returned = exchange(going.reshape(devices, rows * 2, LANES), DEVICES)
    returned = returned.reshape(16, 2, 4, rows * 2, LANES)
    return unpack(turn, pair_row, returned, channels).reshape(pred_four.shape)


def solution(mesh):
    by_core = Mesh(mesh.devices.reshape(16, 2, 4), DEVICES)
    field = P("col", None, None, ("zx", "core"), None)
    return jax.shard_map(
        per_device,
        mesh=by_core,
        in_specs=(field, field, P(DEVICES, None, None), P()),
        out_specs=field,
        check_vma=False,
    )
```

```python
import functools

import jax
import jax.numpy as jnp
from jax import lax
from jax.experimental import pallas as pl
from jax.experimental.pallas import tpu as pltpu
from jax.sharding import Mesh
from jax.sharding import PartitionSpec as P

DEGREES = 1024
HALF = DEGREES // 2
POWER_FLOOR = 0.5
LANES = 128
SLOTS = 8
PAIRS = 4
DEVICES = ("zx", "core", "col")
SAME_CORE = ("zx", "col")
KERNEL_LIMIT = 36 * 1024 * 1024
SMALL_LIMIT = 16 * 1024 * 1024
TINY_LIMIT = 4 * 1024 * 1024


def dot_nt(left, right):
    return lax.dot_general(left, right, (((1,), (1,)), ((), ())), preferred_element_type=jnp.float32)


def dot_nn(left, right):
    return lax.dot_general(left, right, (((1,), (0,)), ((), ())), preferred_element_type=jnp.float32)


def dot_tn(left, right):
    return lax.dot_general(left, right, (((0,), (0,)), ((), ())), preferred_element_type=jnp.float32)


def by_position(blocks, shift):
    group = lax.broadcasted_iota(jnp.int32, blocks[0].shape, 1) >> 5
    result = blocks[-shift % 4]
    for z in range(1, 4):
        result = jnp.where(group == z, blocks[(z - shift) % 4], result)
    return result


def trade_halves(first, second):
    top = lax.broadcasted_iota(jnp.int32, first.shape, 1) < 4
    return (
        jnp.where(top, first, pltpu.roll(second, 4, 1)),
        jnp.where(top, pltpu.roll(first, 4, 1), second),
    )


def one_hots(pairs_ref, lower_ref, upper_ref):
    order = jnp.broadcast_to(pairs_ref[...].astype(jnp.float32), (LANES, HALF)).T
    by_core = order.reshape(16, 2, 2, 8, LANES)
    first, second = by_core[:, 0].reshape(32, 8, LANES), by_core[:, 1].reshape(32, 8, LANES)
    order = jnp.stack(trade_halves(first, second), axis=1).reshape(HALF, LANES)
    order = jnp.concatenate([order] * (HALF // LANES), axis=1).astype(jnp.int32)
    lane = lax.broadcasted_iota(jnp.int32, (HALF, HALF), 1)
    lower_ref[...] = jnp.where(lane == order, 1.0, 0.0).astype(jnp.bfloat16)
    upper_ref[...] = jnp.where(lane == HALF - 1 - order, 1.0, 0.0).astype(jnp.bfloat16)


def pack_kernel(
    channels, turn_ref, pairs_hbm, pred_hbm, target_hbm, out_hbm,
    pairs_ref, field_ref, out_ref, lower_ref, upper_ref, pair_sem, in_sems, out_sems,
):
    steps = channels // 2
    ahead = 2

    def fetch(i, f):
        source = (pred_hbm, target_hbm)[f].at[pl.ds(2 * i, 2)]
        return pltpu.make_async_copy(source, field_ref.at[f, pl.ds(2 * i, 2)], in_sems.at[f, i])

    def send(i):
        return pltpu.make_async_copy(
            out_ref.at[i], out_hbm.at[:, :, :, pl.ds(2 * i, 2)], out_sems.at[i]
        )

    pair_copy = pltpu.make_async_copy(pairs_hbm, pairs_ref, pair_sem)
    pair_copy.start()
    for i in range(ahead):
        for f in range(2):
            fetch(i, f).start()
    pair_copy.wait()
    one_hots(pairs_ref, lower_ref, upper_ref)

    turn = turn_ref[0]

    def step(i, carry):
        @pl.when(i + ahead < steps)
        def _():
            for f in range(2):
                fetch(i + ahead, f).start()

        for f in range(2):
            fetch(i, f).wait()
        for c in range(2):
            pieces = []
            for sample in range(2):
                for z in range(4):
                    group = (z - turn) & 3
                    pieces.append(field_ref[group >> 1, 2 * i + c, 2 * sample + (group & 1)])
            field = jnp.concatenate(pieces, axis=0)
            low = dot_nt(lower_ref[...], field[:, :HALF]).reshape(HALF // 8, 8, 2 * LANES)
            high = dot_nt(upper_ref[...], field[:, HALF:]).reshape(HALF // 8, 8, 2 * LANES)
            both = jnp.concatenate([low, high], axis=1).astype(jnp.bfloat16)
            for sample in range(2):
                block = both[:, :, sample * LANES : (sample + 1) * LANES]
                out_ref[i, :, sample, :, c] = block.reshape(16, 4, 16, LANES)
        send(i).start()
        return carry

    lax.fori_loop(0, steps, step, 0, unroll=True)
    for i in range(steps):
        send(i).wait()


def pack(turn, pairs, pred, target):
    channels = pred.shape[0]
    steps = channels // 2
    far = pl.BlockSpec(memory_space=pltpu.HBM)
    return pl.pallas_call(
        functools.partial(pack_kernel, channels),
        in_specs=[pl.BlockSpec(memory_space=pltpu.SMEM), far, far, far],
        out_specs=far,
        out_shape=pltpu.HBM((16, 2, 4, channels, 16, LANES), jnp.bfloat16),
        scratch_shapes=[
            pltpu.VMEM((1, HALF), jnp.int32),
            pltpu.VMEM((2, channels, 4, 32, DEGREES), jnp.bfloat16),
            pltpu.VMEM((steps, 16, 2, 4, 2, 16, LANES), jnp.bfloat16),
            pltpu.VMEM((HALF, HALF), jnp.bfloat16),
            pltpu.VMEM((HALF, HALF), jnp.bfloat16),
            pltpu.SemaphoreType.DMA,
            pltpu.SemaphoreType.DMA((2, steps)),
            pltpu.SemaphoreType.DMA((steps,)),
        ],
        compiler_params=pltpu.CompilerParams(vmem_limit_bytes=KERNEL_LIMIT),
        cost_estimate=pl.CostEstimate(
            flops=DEGREES * DEGREES * 2 * LANES * channels,
            bytes_accessed=8 * LANES * DEGREES * channels,
            transcendentals=0,
        ),
        name="pack",
    )(turn, in_hbm(pairs), in_hbm(pred), in_hbm(target))


def moments_of(values, rows):
    shaped = values.reshape(2, 2, rows, values.shape[-1])
    pieces = []
    for left, right in ((0, 0), (1, 1), (0, 1)):
        real = shaped[left, 0] * shaped[right, 0]
        imag = shaped[left, 1] * shaped[right, 1]
        pieces.append(real + imag)
    return jnp.concatenate(pieces, axis=0)


def leg_stream(own_hbm, other_hbm, leg_ref, sems):
    def start(p):
        for hbm, here in ((own_hbm, p < PAIRS), (other_hbm, p >= PAIRS)):

            @pl.when(here)
            def _(hbm=hbm):
                at = p & 3
                pltpu.make_async_copy(hbm.at[at], leg_ref.at[at], sems.at[at]).start()

    def wait(p):
        at = p & 3
        pltpu.make_async_copy(own_hbm.at[at], leg_ref.at[at], sems.at[at]).wait()

    return start, wait


def analysis_kernel(
    rows, scalar_ref, arrived_ref, edge_ref, own_hbm, other_hbm, coef_ref, last_ref, moment_ref,
    narrow_ref, leg_ref, sort_ref, turned_edge_ref, field_ref, lower_ref, upper_ref, tail_ref, sems, leg_sems,
):
    size = 3 * rows
    span = arrived_ref.shape[2]
    slots = 2 * SLOTS

    def chunk(k):
        at = pl.ds(4 * k, 4)
        return pltpu.make_async_copy(arrived_ref.at[at], narrow_ref.at[at], sems.at[k])

    start_leg, wait_leg = leg_stream(own_hbm, other_hbm, leg_ref, leg_sems)
    for k in range(8):
        chunk(k).start()
    lower_ref[...] = jnp.zeros_like(lower_ref)
    upper_ref[...] = jnp.zeros_like(upper_ref)
    tail_ref[...] = jnp.zeros_like(tail_ref)
    edges = jnp.concatenate([edge_ref[...], jnp.zeros((LANES - SLOTS, DEGREES), jnp.float32)], axis=0)
    turned_edge_ref[...] = edges.T.astype(jnp.bfloat16)
    row = lax.broadcasted_iota(jnp.int32, (LANES, LANES), 0)
    column = lax.broadcasted_iota(jnp.int32, (LANES, LANES), 1)
    takes = column == (row & (SLOTS - 1)) * slots + (row >> 3)
    sort_ref[...] = jnp.where(takes, 1.0, 0.0).astype(jnp.bfloat16)

    def build(k, carry):
        chunk(k).wait()

        @pl.when((k == 1) | (k == 3) | (k == 5))
        def _():
            start_leg(k >> 1)

        at = pl.multiple_of(k * LANES, LANES)
        for f in range(2):
            tiles = []
            for col in range(4):
                both = []
                for q in range(2):
                    g = 2 * f + q
                    block = by_position([narrow_ref[4 * k + i, col] for i in range(4)], g)
                    if g > 0:
                        block = pltpu.roll(block, LANES - 32 * g, 1)
                    both.append(block)
                both = jnp.concatenate(both, axis=1)
                tiles += [both[c * slots : (c + 1) * slots] for c in range(span // slots)]
            sorted_rows = []
            for u in range(rows // SLOTS):
                group = jnp.concatenate(tiles[u * SLOTS : (u + 1) * SLOTS], axis=0)
                sorted_rows.append(dot_nn(sort_ref[...], group))
            for slot in range(slots):
                parts = [
                    block[slot * SLOTS : (slot + 1) * SLOTS, q * LANES : (q + 1) * LANES]
                    for q in range(2)
                    for block in sorted_rows
                ]
                low = 4 * rows * (slot // SLOTS) + 2 * f * rows
                field_ref[slot % SLOTS, low : low + 2 * rows, pl.ds(at, LANES)] = jnp.concatenate(
                    parts, axis=0
                ).astype(jnp.bfloat16)
        return carry

    lax.fori_loop(0, 8, build, 0)
    core = scalar_ref[2 * PAIRS]

    def one_pair(p, carry):
        @pl.when(p + 3 < 2 * PAIRS)
        def _():
            start_leg(p + 3)

        wait_leg(p)
        ring = p & 3
        slot = p ^ (core * PAIRS)
        lower_order = scalar_ref[p]
        boundary = DEGREES - lower_order
        width = 256
        lower_weight = jnp.where(lower_order == 0, 1.0, 2.0)
        tiles_up = lower_order >> 7
        lanes_up = lower_order & (LANES - 1)
        lane = lax.broadcasted_iota(jnp.int32, (size, LANES), 1)
        late = (lower_order <= width).astype(jnp.int32)
        at = pl.multiple_of(HALF + width * late, width)
        low = pl.multiple_of(4 * rows * (1 - late), 4 * rows)
        extra = dot_nn(field_ref[slot, pl.ds(low, 4 * rows)], leg_ref[ring, :, pl.ds(at, width)])
        before = jnp.zeros((size, LANES), jnp.float32)
        for tile in range(DEGREES // width):
            start = tile * width
            low = 4 * rows * (tile // 3)
            values = dot_nn(field_ref[slot, low : low + 4 * rows], leg_ref[ring, :, start : start + width])
            if start >= HALF:
                row = lax.broadcasted_iota(jnp.int32, values.shape, 1) + start
                first, second = (values, extra) if tile == 2 else (extra, values)
                values = jnp.where(row < boundary, first, second)
            coef_ref[p, :, start : start + width] = values
            for sub in range(width // LANES):
                moments = moments_of(values[:, sub * LANES : (sub + 1) * LANES], rows)
                now = start + sub * LANES
                if start >= HALF:
                    upper_ref[:, now - HALF : now - HALF + LANES] += jnp.where(
                        lane + now < boundary, 0.0, moments
                    )
                turned = pltpu.roll(moments, lanes_up, 1)
                at = pl.multiple_of(now + tiles_up * LANES, LANES)
                lower_ref[:, pl.ds(at, LANES)] += lower_weight * jnp.where(
                    lane < lanes_up, before, turned
                )
                before = turned
        last = dot_nn(field_ref[slot, 4 * rows :], turned_edge_ref[...])
        last_ref[p] = last
        tail_ref[...] += jnp.where(lane == p, moments_of(last, rows), 0.0)
        return carry

    lax.fori_loop(0, 2 * PAIRS, one_pair, 0)

    lane = lax.broadcasted_iota(jnp.int32, (size, LANES), 1)
    after = jnp.broadcast_to(jnp.sum(tail_ref[...], axis=1, keepdims=True), (size, LANES))
    for tile in reversed(range(8)):
        total = lower_ref[:, tile * LANES : (tile + 1) * LANES]
        if tile >= 4:
            turned = pltpu.roll(upper_ref[:, (tile - 4) * LANES : (tile - 3) * LANES], LANES - 1, 1)
            total = total + 2.0 * jnp.where(lane == LANES - 1, after, turned)
            after = turned
        total = jnp.concatenate([total, jnp.zeros((LANES - size, LANES), jnp.float32)], axis=0)
        moment_ref[tile * LANES : (tile + 1) * LANES, :] = total.T


def in_vmem(value):
    return pltpu.with_memory_space_constraint(value, pltpu.VMEM)


def in_hbm(value):
    return pltpu.with_memory_space_constraint(value, pltpu.HBM)


def turn_kernel(leg_ref, out_ref):
    out_ref[0] = leg_ref[0].T


def turned(legendre):
    pairs, _, size = legendre.shape
    width = 256
    return pl.pallas_call(
        turn_kernel,
        grid=(pairs, DEGREES // width),
        in_specs=[pl.BlockSpec((1, width, size), lambda p, i: (p, i, 0))],
        out_specs=pl.BlockSpec((1, size, width), lambda p, i: (p, 0, i)),
        out_shape=pltpu.HBM((pairs, size, DEGREES), legendre.dtype),
        compiler_params=pltpu.CompilerParams(vmem_limit_bytes=SMALL_LIMIT),
        cost_estimate=pl.CostEstimate(flops=0, bytes_accessed=4 * legendre.size, transcendentals=0),
        name="turned",
    )(in_hbm(legendre))


def analysis(scalars, arrived, edges, own, other, rows):
    span = rows * 4
    arrived = arrived.reshape(32, 4, span, LANES)
    whole = pl.BlockSpec(memory_space=pltpu.VMEM)
    far = pl.BlockSpec(memory_space=pltpu.HBM)
    return pl.pallas_call(
        functools.partial(analysis_kernel, rows),
        in_specs=[pl.BlockSpec(memory_space=pltpu.SMEM), far, whole, far, far],
        out_specs=[whole, whole, whole],
        out_shape=[
            pltpu.VMEM((2 * PAIRS, 4 * rows, DEGREES), jnp.float32),
            pltpu.VMEM((2 * PAIRS, 4 * rows, LANES), jnp.float32),
            pltpu.VMEM((DEGREES, LANES), jnp.float32),
        ],
        scratch_shapes=[
            pltpu.VMEM((32, 4, span, LANES), jnp.bfloat16),
            pltpu.VMEM((4, DEGREES, DEGREES), jnp.bfloat16),
            pltpu.VMEM((LANES, LANES), jnp.bfloat16),
            pltpu.VMEM((DEGREES, LANES), jnp.bfloat16),
            pltpu.VMEM((SLOTS, 8 * rows, DEGREES), jnp.bfloat16),
            pltpu.VMEM((3 * rows, DEGREES + HALF), jnp.float32),
            pltpu.VMEM((3 * rows, HALF), jnp.float32),
            pltpu.VMEM((3 * rows, LANES), jnp.float32),
            pltpu.SemaphoreType.DMA((8,)),
            pltpu.SemaphoreType.DMA((4,)),
        ],
        compiler_params=pltpu.CompilerParams(vmem_limit_bytes=KERNEL_LIMIT),
        cost_estimate=pl.CostEstimate(
            flops=20 * rows * PAIRS * DEGREES * DEGREES,
            bytes_accessed=4 * own.size + 16 * rows * PAIRS * DEGREES + 2 * arrived.size,
            transcendentals=0,
        ),
        name="analysis",
    )(scalars, in_hbm(arrived), edges, in_hbm(own), in_hbm(other))


def factor_kernel(span, parts_ref, out_ref):
    total = jnp.sum(parts_ref[...], axis=0)
    size = total.shape[1]
    power_pred = total
    power_true = pltpu.roll(total, size - span, 1)
    cross = pltpu.roll(total, size - 2 * span, 1)
    pred = jnp.maximum(power_pred, POWER_FLOOR)
    true = jnp.maximum(power_true, POWER_FLOOR)
    root_pred = jnp.sqrt(pred)
    root_true = jnp.sqrt(true)
    both = pred + true
    upper_mean = (pred * pred + true * true) / both
    inverse = 1.0 / (root_pred * root_true)
    coherence = cross * inverse
    mean_slope = (2.0 * pred - upper_mean) / both
    slope = (
        (root_pred - root_true) / root_pred
        + 2.0 * mean_slope * (1.0 - coherence)
        + upper_mean * coherence / pred
    )
    binds = jnp.where(power_pred > POWER_FLOOR, 1.0, jnp.where(power_pred == POWER_FLOOR, 0.5, 0.0))
    dpower = 2.0 * slope * binds
    dcross = -2.0 * upper_mean * inverse
    lane = lax.broadcasted_iota(jnp.int32, total.shape, 1)
    factors = jnp.where(lane < span, dpower, pltpu.roll(dcross, span, 1))
    out_ref[...] = jnp.broadcast_to(factors[None], out_ref.shape)


def factors_of(parts, rows):
    whole = pl.BlockSpec(memory_space=pltpu.VMEM)
    return pl.pallas_call(
        functools.partial(factor_kernel, rows),
        in_specs=[whole],
        out_specs=whole,
        out_shape=pltpu.VMEM(parts.shape, jnp.float32),
        compiler_params=pltpu.CompilerParams(vmem_limit_bytes=TINY_LIMIT),
        cost_estimate=pl.CostEstimate(flops=parts.size, bytes_accessed=8 * parts.size, transcendentals=0),
        name="factors",
    )(in_vmem(parts))


def synthesis_kernel(
    rows, scalar_ref, coef_ref, last_ref, factor_ref, own_ref, other_ref, out_ref,
    spread_ref, upspread_ref, early_ref, late_ref, wide_ref,
):
    size = 2 * rows
    lane = lax.broadcasted_iota(jnp.int32, (size, LANES), 1)
    before = None
    for tile in range(8):
        turned = factor_ref[tile * LANES : (tile + 1) * LANES, :].T[:size]
        spread_ref[:, tile * LANES : (tile + 1) * LANES] = turned
        shifted = pltpu.roll(turned, 1, 1)
        if tile >= 4:
            upspread_ref[:, (tile - 4) * LANES : (tile - 3) * LANES] = 2.0 * jnp.where(
                lane == 0, before, shifted
            )
        before = shifted
    core = scalar_ref[2 * PAIRS]

    def one_pair(leg_ref, first, ring, carry):
        p = first + ring
        slot = p ^ (core * PAIRS)
        lower_order = scalar_ref[p]
        boundary = DEGREES - lower_order
        lower_weight = jnp.where(lower_order == 0, 1.0, 2.0)
        tiles_up = lower_order >> 7
        lanes_up = lower_order & (LANES - 1)
        back = (LANES - lanes_up) & (LANES - 1)

        def turned_tile(tile):
            at = pl.multiple_of((tile + tiles_up) * LANES, LANES)
            return pltpu.roll(spread_ref[:, pl.ds(at, LANES)], back, 1)

        def graded(factors, observe):
            grads = []
            for q in range(2):
                predicted = observe(q * rows)
                observed = observe((2 + q) * rows)
                grads.append(factors[:rows] * predicted + factors[rows:] * observed)
            return jnp.concatenate(grads, axis=0)

        now = turned_tile(0)
        for tile in range(8):
            start = tile * LANES
            then = turned_tile(tile + 1)
            factors = lower_weight * jnp.where(lane < LANES - lanes_up, now, then)
            now = then
            row = lane + start
            if tile >= 4:
                factors = jnp.where(
                    row < boundary, factors, upspread_ref[:, start - HALF : start - HALF + LANES]
                )
            grad = graded(factors, lambda at: coef_ref[p, at : at + rows, start : start + LANES])
            if tile >= 4:
                at = start - HALF
                late_ref[:size, at : at + LANES] = jnp.where(row < boundary, grad, 0.0).astype(
                    jnp.bfloat16
                )
                late_ref[size:, at : at + LANES] = jnp.where(row < boundary, 0.0, grad).astype(
                    jnp.bfloat16
                )
            else:
                early_ref[:, start : start + LANES] = grad.astype(jnp.bfloat16)
        last_factors = jnp.broadcast_to(2.0 * spread_ref[:, DEGREES - 1 : DEGREES], (size, LANES))
        edge_lane = lax.broadcasted_iota(jnp.int32, (4 * rows, LANES), 1)
        last = jnp.sum(jnp.where(edge_lane == p, last_ref[p], 0.0), axis=1, keepdims=True)
        last = jnp.broadcast_to(last, (4 * rows, LANES))
        last_grad = graded(last_factors, lambda at: last[at : at + rows])
        last_grad = last_grad.astype(jnp.bfloat16).astype(jnp.float32)
        last_leg = leg_ref[ring, DEGREES : DEGREES + 1, :].astype(jnp.float32)

        width = 256
        for tile in range(DEGREES // width):
            start = tile * width
            early = dot_nn(early_ref[...], leg_ref[ring, :HALF, start : start + width])
            late = dot_nn(late_ref[...], leg_ref[ring, HALF:DEGREES, start : start + width])
            lower, upper = early + late[:size], late[size:]
            for sub in range(width // LANES):
                at = start + sub * LANES
                inside = slice(sub * LANES, (sub + 1) * LANES)
                top = lower[:, inside]
                bottom = upper[:, inside] + last_grad * last_leg[:, at : at + LANES]
                blocks = [top[:rows], top[rows:], bottom[:rows], bottom[rows:]]
                blocks = [
                    block if g == 0 else pltpu.roll(block, 32 * g, 1) for g, block in enumerate(blocks)
                ]
                for i in range(4):
                    wide_ref[at // 32 + i, pl.ds(slot, rows, stride=SLOTS), :] = by_position(blocks, i)
        return carry

    lax.fori_loop(0, PAIRS, functools.partial(one_pair, own_ref, 0), 0, unroll=4)
    lax.fori_loop(0, PAIRS, functools.partial(one_pair, other_ref, PAIRS), 0, unroll=4)

    def narrow(j, carry):
        out_ref[j] = wide_ref[j].astype(jnp.bfloat16)
        return carry

    lax.fori_loop(0, 32, narrow, 0, unroll=8)


def synthesis(scalars, coeffs, last, factors, own, other, rows):
    whole = pl.BlockSpec(memory_space=pltpu.VMEM)
    return pl.pallas_call(
        functools.partial(synthesis_kernel, rows),
        in_specs=[pl.BlockSpec(memory_space=pltpu.SMEM)] + [whole] * 5,
        out_specs=whole,
        out_shape=pltpu.VMEM((32, rows * SLOTS, LANES), jnp.bfloat16),
        scratch_shapes=[
            pltpu.VMEM((2 * rows, DEGREES + HALF), jnp.float32),
            pltpu.VMEM((2 * rows, HALF), jnp.float32),
            pltpu.VMEM((2 * rows, HALF), jnp.bfloat16),
            pltpu.VMEM((4 * rows, HALF), jnp.bfloat16),
            pltpu.VMEM((32, rows * SLOTS, LANES), jnp.float32),
        ],
        compiler_params=pltpu.CompilerParams(vmem_limit_bytes=SMALL_LIMIT),
        cost_estimate=pl.CostEstimate(
            flops=12 * rows * PAIRS * DEGREES * DEGREES,
            bytes_accessed=4 * own.size + 16 * rows * PAIRS * DEGREES + 64 * rows * SLOTS * LANES,
            transcendentals=0,
        ),
        name="synthesis",
    )(scalars, *(in_vmem(value) for value in (coeffs, last, factors, own, other)))


def unpack_kernel(
    channels, turn_ref, lower_ref, upper_ref, returned_ref, out_hbm, out_ref, sems
):
    turn = turn_ref[0]

    def send(i):
        at = pl.ds(2 * i, 2)
        return pltpu.make_async_copy(out_ref.at[at], out_hbm.at[at], sems.at[i])

    steps = channels // 2
    for i in range(steps):
        sides = []
        for c in range(2 * i, 2 * i + 2):
            first, second = (
                returned_ref[:, sample, :, (c // 2) * 16 : (c // 2) * 16 + 16]
                .astype(jnp.float32)[:, :, (c % 2) * SLOTS : (c % 2 + 1) * SLOTS]
                .reshape(HALF, LANES)
                for sample in range(2)
            )
            group = lax.broadcasted_iota(jnp.int32, first.shape, 1) >> 5
            keep = ((group - turn) & 3) < 2
            sides.append(
                (
                    jnp.where(keep, first, pltpu.roll(second, 64, 1)),
                    jnp.where(keep, pltpu.roll(first, 64, 1), second),
                )
            )
        for o, one_hot_ref in enumerate((lower_ref, upper_ref)):
            by_slot = jnp.concatenate([side[o] for side in sides], axis=1)
            field = dot_tn(by_slot.astype(jnp.bfloat16), one_hot_ref[...]).astype(jnp.bfloat16)
            for c in range(2):
                for z in range(4):
                    at = c * LANES + z * 32
                    out_ref[2 * i + c, (z - turn) & 3, :, o * HALF : (o + 1) * HALF] = field[at : at + 32]
        send(i).start()
    for i in range(steps):
        send(i).wait()


def both_one_hots(pairs):
    return pl.pallas_call(
        one_hots,
        out_shape=[pltpu.HBM((HALF, HALF), jnp.bfloat16)] * 2,
        compiler_params=pltpu.CompilerParams(vmem_limit_bytes=SMALL_LIMIT),
        cost_estimate=pl.CostEstimate(flops=0, bytes_accessed=4 * HALF * HALF, transcendentals=0),
        name="one_hots",
    )(pairs)


def unpack(turn, lower, upper, returned, channels):
    whole = pl.BlockSpec(memory_space=pltpu.VMEM)
    return pl.pallas_call(
        functools.partial(unpack_kernel, channels),
        in_specs=[pl.BlockSpec(memory_space=pltpu.SMEM), whole, whole, whole],
        out_specs=pl.BlockSpec(memory_space=pltpu.HBM),
        out_shape=pltpu.HBM((channels, 4, 32, DEGREES), jnp.bfloat16),
        scratch_shapes=[
            pltpu.VMEM((channels, 4, 32, DEGREES), jnp.bfloat16),
            pltpu.SemaphoreType.DMA((channels // 2,)),
        ],
        compiler_params=pltpu.CompilerParams(vmem_limit_bytes=KERNEL_LIMIT),
        cost_estimate=pl.CostEstimate(
            flops=DEGREES * DEGREES * LANES * channels,
            bytes_accessed=4 * LANES * DEGREES * channels,
            transcendentals=0,
        ),
        name="unpack",
    )(turn, in_vmem(lower), in_vmem(upper), in_vmem(returned))


def exchange(values, axes):
    return lax.all_to_all(values, axes, split_axis=0, concat_axis=0, tiled=True)


def per_device(pred_four, target_four, legendre, pair_order):
    channels = pred_four.shape[0]
    devices = DEGREES // SLOTS
    rows = 4 * channels
    core = lax.axis_index("core")
    device = lax.axis_index(DEVICES)
    turn = ((2 * lax.axis_index("zx") + core) & 3).reshape(1)
    pair_row = pair_order.reshape(1, HALF)
    other_legendre = lax.ppermute(legendre, "core", [(0, 1), (1, 0)])
    own_order = lax.dynamic_slice_in_dim(pair_order, device * PAIRS, PAIRS)
    other_order = lax.dynamic_slice_in_dim(pair_order, (device ^ 4) * PAIRS, PAIRS)
    scalars = jnp.concatenate([own_order, other_order, core.astype(jnp.int32).reshape(1)])

    by_group = (channels, 4, 32, DEGREES)
    packed = pack(turn, pair_row, pred_four.reshape(by_group), target_four.reshape(by_group))
    arrived = exchange(packed.reshape(devices, rows * 4, LANES), DEVICES)
    edges = jnp.concatenate([legendre[:, DEGREES], other_legendre[:, DEGREES]]).astype(jnp.float32)
    own_turned = turned(legendre)
    late_row, own_turned = lax.optimization_barrier((pair_row, own_turned))
    lower_hot, upper_hot = both_one_hots(late_row)
    coeffs, last, moments = analysis(
        scalars, arrived, edges, own_turned, turned(other_legendre), rows
    )
    spectra = exchange(moments.reshape(devices // 2, 2 * SLOTS, LANES), SAME_CORE)
    factors = exchange(factors_of(spectra, rows), SAME_CORE).reshape(DEGREES, LANES)
    going = synthesis(scalars, coeffs, last, factors, legendre, other_legendre, rows)
    returned = exchange(going.reshape(devices, rows * 2, LANES), DEVICES)
    returned = returned.reshape(16, 2, 4, rows * 2, LANES)
    return unpack(turn, lower_hot, upper_hot, returned, channels).reshape(pred_four.shape)


def solution(mesh):
    by_core = Mesh(mesh.devices.reshape(16, 2, 4), DEVICES)
    field = P("col", None, None, ("zx", "core"), None)
    return jax.shard_map(
        per_device,
        mesh=by_core,
        in_specs=(field, field, P(DEVICES, None, None), P()),
        out_specs=field,
        check_vma=False,
    )
```
